32 devices in a mesh: dp: 2 (over y), seq: 16 (over z, x, core).
Axes of the slice: x: 2, y: 2, z: 4, core: 2. Of those that a mesh axis runs over, the one named last changes fastest.
Arguments:
- tokens: bfloat16 [1024, 16, 768], P('seq', 'dp'), may hold values from -6 to 6
- norm_gain1: bfloat16 [768], P(('dp', 'seq')), may hold values from 0.25 to 1.75
- value_weight: bfloat16 [768, 768], P(('dp', 'seq')), may hold values from -0.21875 to 0.21875
- mixer_logits: bfloat16 [12, 1024, 1024], P(None, 'seq'), may hold values from -8 to 8
- out_weight: bfloat16 [768, 768], P(('dp', 'seq')), may hold values from -0.625 to 0.625
- norm_gain2: bfloat16 [768], P(('dp', 'seq')), may hold values from 0.25 to 1.75
- up_weight: bfloat16 [768, 3072], P(('dp', 'seq')), may hold values from -0.21875 to 0.21875
- down_weight: bfloat16 [3072, 768], P(('dp', 'seq')), may hold values from -0.109375 to 0.109375
- out_grad: bfloat16 [1024, 16, 768], P('seq', 'dp'), may hold values from -6 to 6
Outputs:
- layer_out: bfloat16 [1024, 16, 768], P('seq', 'dp')
- tokens_grad: float32 [1024, 16, 768], P('seq', 'dp')
- gain1_grad: float32 [768], P(('dp', 'seq'))
- value_weight_grad: float32 [768, 768], P(('dp', 'seq'))
- logits_grad: float32 [12, 1024, 1024], P(None, 'seq', 'dp')
- out_weight_grad: float32 [768, 768], P(('dp', 'seq'))
- gain2_grad: float32 [768], P(('dp', 'seq'))
- up_weight_grad: float32 [768, 3072], P(('dp', 'seq'))
- down_weight_grad: float32 [3072, 768], P(('dp', 'seq'))
The draws below stay inside these ranges and needn't reach their ends.
All inputs are finite; a program needn't handle non-finite values.
Results may differ from the reference program's by a relative error of at most 0.015.
Values may be sent and summed in bfloat16 or wider, within the bound.
No kernel may reach another device: no remote copies, remote signals or barrier semaphores. Data moves between devices by JAX's collectives and lax.ppermute only.
A program may use at most 256 MiB of HBM per device.

```python
import math
import jax
import jax.numpy as jnp
from jax import lax

D = 768
HEADS = 12
FF = 3072
LEN = 1024
BATCH = 16


def level_of(key, shape, shards, least, top_value):
    level, own = 1.0, jax.random.fold_in(key, 6)
    for position, parts in shards:
        draws = jnp.exp(jax.random.uniform(jax.random.fold_in(own, position), (parts,), jnp.float32, least / len(shards), top_value / len(shards)))
        level = level * jnp.repeat(draws, shape[position] // parts).reshape([-1 if axis == position else 1 for axis in range(len(shape))])
    return level


def bell_draw(key, extent, scale, reach, shards=(), kind=jnp.bfloat16):
    array = scale * jax.random.normal(key, extent, jnp.float32)
    if shards:
        array = array * level_of(key, extent, shards, -0.22, 0.18)
    return jnp.clip(array, -reach, reach).astype(kind)


def setup_inputs(seed: int = 0) -> dict:
    seeds = jax.random.split(jax.random.key(seed), 10)
    return {
        "tokens": bell_draw(seeds[0], (LEN, BATCH, D), 1.0, 6.0, ((0, 16), (1, 2))),
        "norm_gain1": jnp.clip(1.0 + 0.15 * jax.random.normal(seeds[1], (D,), jnp.float32), 0.25, 1.75).astype(jnp.bfloat16),
        "value_weight": bell_draw(seeds[2], (D, D), D ** -0.5, 0.21875, ((0, 32),)),
        "mixer_logits": bell_draw(seeds[3], (HEADS, LEN, LEN), 2.0, 8.0, ((1, 16),)),
        "out_weight": bell_draw(seeds[4], (D, D), (D // 8) ** -0.5, 0.625, ((0, 32),)),
        "norm_gain2": jnp.clip(1.0 + 0.15 * jax.random.normal(seeds[5], (D,), jnp.float32), 0.25, 1.75).astype(jnp.bfloat16),
        "up_weight": bell_draw(seeds[6], (D, FF), D ** -0.5, 0.21875, ((0, 32),)),
        "down_weight": bell_draw(seeds[7], (FF, D), FF ** -0.5, 0.109375, ((0, 32),)),
        "out_grad": bell_draw(seeds[8], (LEN, BATCH, D), 1.0, 6.0, ((0, 16), (1, 2))),
    }


@jax.custom_vjp
def low(v):
    return lax.optimization_barrier(v.astype(jnp.bfloat16)).astype(jnp.float32)

@jax.custom_vjp
def low_back(v):
    return v

def low_keep(v):
    return (low(v), None)

def low_pass(kept, grad):
    return (grad,)

def back_keep(v):
    return (v, None)

def back_low(kept, grad):
    return (low(grad),)
low.defvjp(low_keep, low_pass)
low_back.defvjp(back_keep, back_low)

def rms_scale(inputs, gain):
    return inputs * lax.rsqrt(lax.optimization_barrier(jnp.mean(inputs * inputs, axis=-1, keepdims=True)) + 1e-06) * gain

def matmul_high(left, right):
    return jnp.einsum('lgd,de->lge', left, right, precision=lax.Precision.HIGHEST)

def mixing_weights(logits):
    index = jnp.arange(logits.shape[1])
    allowed = index[None, :] <= index[:, None]
    masked = jnp.where(allowed[None], logits, -jnp.inf)
    row_max = lax.optimization_barrier(jnp.max(masked, axis=-1, keepdims=True))
    expo_rows = jnp.exp(masked - row_max)
    return expo_rows / lax.optimization_barrier(jnp.sum(expo_rows, axis=-1, keepdims=True))

def block_forward(inputs, gain_one, w_value, logits, w_out, gain_two, w_up, w_down):
    length, group_size, model_width = inputs.shape
    head_count = logits.shape[0]
    normed_one = low(rms_scale(inputs, gain_one))
    values = low_back(low(matmul_high(normed_one, w_value)))
    mix_low = low(mixing_weights(logits))
    mixed = jnp.einsum('hij,jbhc->ibhc', mix_low, values.reshape(length, group_size, head_count, -1), precision=lax.Precision.HIGHEST).reshape(length, group_size, model_width)
    mixed = low_back(low(mixed))
    residual = inputs + low_back(matmul_high(mixed, w_out))
    normed_two = low(rms_scale(residual, gain_two))
    pre_act = low_back(matmul_high(normed_two, w_up))
    hidden = low(jax.nn.gelu(pre_act))
    return residual + matmul_high(hidden, w_down)

def reference(tokens, norm_gain1, value_weight, mixer_logits, out_weight, norm_gain2, up_weight, down_weight, out_grad):
    params = tuple((p.astype(jnp.float32) for p in (norm_gain1, value_weight, mixer_logits, out_weight, norm_gain2, up_weight, down_weight)))
    group_size = math.gcd(BATCH, max(1, 4096 // LEN))
    group_count = BATCH // group_size
    inputs = tokens.astype(jnp.float32).reshape(LEN, group_count, group_size, D).transpose(1, 0, 2, 3)
    cotangent = out_grad.astype(jnp.float32).reshape(LEN, group_count, group_size, D).transpose(1, 0, 2, 3)

    def one_group(totals, batch_item):
        group_in, group_cot = batch_item
        result, backward = jax.vjp(block_forward, group_in, *params)
        grads = backward(group_cot)
        new_totals = tuple((t + g for t, g in zip(totals, grads[1:])))
        return (new_totals, (result, grads[0]))
    start_totals = tuple((jnp.zeros_like(p) for p in params))
    summed, (results, input_grads) = lax.scan(one_group, start_totals, (inputs, cotangent))
    layer_out = results.transpose(1, 0, 2, 3).reshape(LEN, BATCH, D).astype(jnp.bfloat16)
    tokens_grad = input_grads.transpose(1, 0, 2, 3).reshape(LEN, BATCH, D)
    return (layer_out, tokens_grad, summed[0], summed[1], summed[2], summed[3], summed[4], summed[5], summed[6])
```

```python
import functools

import jax
import jax.numpy as jnp
from jax import lax
from jax.experimental import pallas as pl
from jax.experimental.pallas import tpu as pltpu
from jax.sharding import PartitionSpec as P

F32 = jnp.float32
BF16 = jnp.bfloat16
AXES = ("dp", "seq")
HEAD = 64
GROUPS = 4
EPS = 1e-06
MIB = 1 << 20


def smem():
    return pl.BlockSpec(memory_space=pltpu.SMEM)


def vmem():
    return pl.BlockSpec(memory_space=pltpu.VMEM)


def params(mib):
    return pltpu.CompilerParams(vmem_limit_bytes=mib * MIB)


def cost(flops, moved, trans=0):
    return pl.CostEstimate(flops=int(flops), bytes_accessed=int(moved), transcendentals=int(trans))


def shape(dims, kind=BF16):
    return jax.ShapeDtypeStruct(tuple(dims), kind)


def dot_nn(left, right):
    return lax.dot_general(left, right, (((1,), (0,)), ((), ())), preferred_element_type=F32)


def dot_nt(left, right):
    return lax.dot_general(left, right, (((1,), (1,)), ((), ())), preferred_element_type=F32)


def dot_tn(left, right):
    return lax.dot_general(left, right, (((0,), (0,)), ((), ())), preferred_element_type=F32)


class Layout:
    def __init__(self, tokens, logits):
        self.positions, self.sequences, self.width = tokens.shape
        self.heads, _, self.length = logits.shape
        self.dp, self.seq = lax.axis_size("dp"), lax.axis_size("seq")
        self.xs = self.seq // (2 * GROUPS)
        self.rows = self.positions * self.sequences
        self.group = self.heads // GROUPS
        self.lanes = self.sequences * HEAD
        self.devices = self.dp * self.seq
        dp, seq = lax.axis_index("dp"), lax.axis_index("seq")
        self.z, self.x, self.c = seq // (2 * self.xs), (seq // 2) % self.xs, seq % 2
        self.me = jnp.stack([dp, self.z, self.x, self.c, seq, seq, seq, seq]).astype(jnp.int32)
        self.small = self.dp == 2 and self.xs == 2

    def swap(self, array, dp=0, z=0, x=0, c=0):
        mask = ((dp * GROUPS + z) * self.xs + x) * 2 + c
        return lax.ppermute(array, AXES, [(i, i ^ mask) for i in range(self.devices)])


def add_low(left, right):
    return (left.astype(F32) + right.astype(F32)).astype(BF16)


def to_heads(source, target, positions, sequences, heads):
    group = heads // GROUPS
    low = lax.broadcasted_iota(jnp.int32, (positions, 2 * HEAD), 1) < HEAD
    for pair in range(sequences // 2):
        for two in range(heads // 2):
            a = source[two, pl.ds(2 * pair, positions, stride=sequences), :]
            b = source[two, pl.ds(2 * pair + 1, positions, stride=sequences), :]
            even = jnp.where(low, a, pltpu.roll(b, HEAD, 1))
            odd = jnp.where(low, pltpu.roll(a, HEAD, 1), b)
            for head, tile in ((2 * two, even), (2 * two + 1, odd)):
                target[head // group, head % group, :, 128 * pair : 128 * pair + 128] = tile.astype(BF16)


def from_heads(source, target, positions, sequences, heads):
    group = heads // GROUPS
    low = lax.broadcasted_iota(jnp.int32, (positions, 2 * HEAD), 1) < HEAD
    for pair in range(sequences // 2):
        for two in range(heads // 2):
            even, odd = (
                source[head // group, head % group, :, 128 * pair : 128 * pair + 128].astype(F32)
                for head in (2 * two, 2 * two + 1)
            )
            first = jnp.where(low, even, pltpu.roll(odd, HEAD, 1))
            second = jnp.where(low, pltpu.roll(even, HEAD, 1), odd)
            target[two, pl.ds(2 * pair, positions, stride=sequences), :] = first
            target[two, pl.ds(2 * pair + 1, positions, stride=sequences), :] = second


def split_lanes(value, target):
    for two in range(target.shape[0]):
        target[two] = value[:, 128 * two : 128 * two + 128]


def join_lanes(source, target):
    for two in range(source.shape[0]):
        target[:, 128 * two : 128 * two + 128] = source[two].astype(target.dtype)


def softmax_kernel(me, logits, own, *others):
    positions, length = logits.shape[2], logits.shape[3]
    z, seq, side = me[1], me[4], me[0] % 2
    half = positions // 2
    column = lax.broadcasted_iota(jnp.int32, (positions, length), 1)
    row = lax.broadcasted_iota(jnp.int32, (positions, length), 0) + seq * positions

    def soft(values, allowed):
        masked = jnp.where(allowed, values.astype(F32), -jnp.inf)
        expo = jnp.exp(masked - jnp.max(masked, axis=-1, keepdims=True))
        return (expo * (1.0 / jnp.sum(expo, axis=-1, keepdims=True))).astype(BF16)

    allowed = column <= row
    for head in range(logits.shape[1]):
        own[head] = soft(logits[z, head], allowed)
    start = pl.multiple_of(side * half, half)
    allowed = column[:half] <= row[:half] + start
    for k, out in enumerate(others, 1):
        for head in range(logits.shape[1]):
            out[head] = soft(logits[z ^ k, head, pl.ds(start, half), :], allowed)


def softmax_rows(lay, logits):
    group, positions, length = lay.group, lay.positions, lay.length
    return pl.pallas_call(
        softmax_kernel,
        in_specs=[smem(), vmem()],
        out_specs=[vmem()] * GROUPS,
        out_shape=[shape((group, positions, length))]
        + [shape((group, positions // 2, length))] * (GROUPS - 1),
        compiler_params=params(24),
        cost_estimate=cost(1e7, 4 * logits.size, logits.size),
        name="mix_rows",
    )(lay.me, logits.reshape(GROUPS, group, positions, length))


def gather_rows(me, own, other, store, xs, dps):
    first = me[3] == 0
    for r in range(own.shape[0]):
        xr, yr, zr = r // (GROUPS * dps), (r // GROUPS) % dps, r % GROUPS
        chip = ((me[0] ^ yr) * GROUPS + (me[1] ^ zr)) * xs + (me[2] ^ xr)
        mine, theirs = own[r].astype(F32), other[r].astype(F32)
        block = jnp.concatenate([jnp.where(first, mine, theirs), jnp.where(first, theirs, mine)], 0)
        store(chip, block.astype(BF16))


def value_body(me, tokens, weight, scratch, parts, outs, normed, positions, sequences, heads):
    inputs = tokens[...].astype(F32)
    scale = lax.rsqrt(jnp.mean(inputs * inputs, axis=-1, keepdims=True) + EPS)
    low = (inputs * scale).astype(BF16)
    normed[...] = low
    split_lanes(dot_nn(low, weight[...]), scratch)
    to_heads(scratch, parts, positions, sequences, heads)
    for k, out in enumerate(outs):
        out[...] = parts[me[1] ^ k]


def value_kernel(me, tokens, *rest, positions, sequences, heads, blocks):
    if blocks:
        own, other, normed, whole, *outs = rest[:8]
        rows = whole.shape[0] // blocks

        def store(chip, block):
            whole[pl.ds(pl.multiple_of(chip * rows, rows), rows), :] = block

        gather_rows(me, own, other, store, 2, 2)
    else:
        whole, normed, *outs = rest[:6]
    parts, scratch = rest[-2:]
    value_body(me, tokens, whole, scratch, parts, outs, normed, positions, sequences, heads)


def make_values(lay, tokens, weight):
    rows, width = tokens.shape
    piece = (lay.group, lay.positions, lay.lanes)
    blocks = 0 if len(weight) == 1 else lay.devices // 2
    outs = [shape((rows, width))] + ([shape((width, width))] if blocks else []) + [shape(piece)] * GROUPS
    result = pl.pallas_call(
        functools.partial(
            value_kernel,
            positions=lay.positions,
            sequences=lay.sequences,
            heads=lay.heads,
            blocks=blocks,
        ),
        in_specs=[smem()] + [vmem()] * (1 + len(weight)),
        out_specs=[vmem()] * len(outs),
        out_shape=outs,
        scratch_shapes=[pltpu.VMEM((GROUPS,) + piece, BF16), pltpu.VMEM((width // 128, rows, 128), F32)],
        compiler_params=params(24),
        cost_estimate=cost(2 * rows * width * width, 6 * rows * width + 4 * width * width),
        name="make_values",
    )(lay.me, tokens, *weight)
    normed = result[0]
    whole = result[1] if blocks else weight[0]
    return normed, whole, list(result[-GROUPS:])


def mix_kernel(me, *refs, xs, positions):
    values = refs[: 2 * xs * GROUPS]
    refs = refs[2 * xs * GROUPS :]
    own, near, far = refs[0], refs[1:GROUPS], refs[GROUPS : 2 * GROUPS - 1]
    rows_out, values_out, *outs, mixed = refs[2 * GROUPS - 1 :]
    z, x, c, side = me[1], me[2], me[3], me[0] % 2
    half = positions // 2
    rows_out[:, pl.ds(pl.multiple_of(z * positions, positions), positions), :] = own[...]
    for k in range(1, GROUPS):
        base = (z ^ k) * positions
        rows_out[:, pl.ds(pl.multiple_of(base + side * half, half), half), :] = near[k - 1][...]
        rows_out[:, pl.ds(pl.multiple_of(base + (1 - side) * half, half), half), :] = far[k - 1][...]
    index = 0
    for m in range(2):
        for j in range(xs):
            for k in range(GROUPS):
                block = ((z ^ k) * xs + (x ^ j)) * 2 + (c ^ m)
                values_out[:, pl.ds(pl.multiple_of(block * positions, positions), positions), :] = values[
                    index
                ][...]
                index += 1
    for head in range(rows_out.shape[0]):
        mixed[head] = dot_nn(rows_out[head], values_out[head]).astype(BF16)
    for k, out in enumerate(outs):
        out[...] = mixed[:, pl.ds(pl.multiple_of((z ^ k) * positions, positions), positions), :]


def mix_values(lay, values, rows):
    group, positions, length, lanes = lay.group, lay.positions, lay.length, lay.lanes
    inputs = list(values) + list(rows)
    result = pl.pallas_call(
        functools.partial(mix_kernel, xs=lay.xs, positions=positions),
        in_specs=[smem()] + [vmem()] * len(inputs),
        out_specs=[vmem()] * (2 + GROUPS),
        out_shape=[shape((group, GROUPS * positions, length)), shape((group, length, lanes))]
        + [shape((group, positions, lanes))] * GROUPS,
        scratch_shapes=[pltpu.VMEM((group, GROUPS * positions, lanes), BF16)],
        compiler_params=params(40),
        cost_estimate=cost(2 * group * GROUPS * positions * length * lanes, 8 * group * length * lanes),
        name="mix_values",
    )(lay.me, *inputs)
    return result[0], result[1], list(result[2:])


def up_front_kernel(me, out_grad, *refs, blocks):
    if blocks:
        up_own, up_other, down_own, down_other, up_whole, down_whole, grad = refs
        rows, tall = up_whole.shape[0] // blocks, 2 * down_own.shape[1]
        part = pl.program_id(0)

        def store(chip, block):
            up_whole[pl.ds(pl.multiple_of(chip * rows, rows), rows), :] = block

        gather_rows(me, up_own, up_other, store, 2, 2)

        @pl.when(part == 0)
        def _():
            for r in range(down_own.shape[0]):
                yr, xr, zr = r // (GROUPS * 2), (r // GROUPS) % 2, r % GROUPS
                chip = ((me[0] ^ yr) * GROUPS + (me[1] ^ zr)) * 2 + (me[2] ^ xr)
                for ref, core in ((down_own, me[3]), (down_other, 1 - me[3])):
                    start = pl.multiple_of(chip * tall + core * (tall // 2), tall // 2)
                    down_whole[pl.ds(start, tall // 2), :] = ref[r]

        @pl.when(part < pl.num_programs(0) - 1)
        def _():
            start = pl.multiple_of(part * up_whole.shape[1], up_whole.shape[1])
            grad[...] = dot_nt(
                out_grad[...], down_whole[pl.ds(start, up_whole.shape[1]), :]
            ).astype(BF16)


def prepare_weights(lay, out_grad, up_own, up_other, down_own, down_other):
    rows, width = out_grad.shape
    chips, short, wide = up_own.shape
    tall = down_own.shape[1]
    hidden = wide - width
    steps = hidden // width

    def part(i, me):
        return (0, 0, i)

    def fixed(i, me):
        return (0, 0, 0)

    return pl.pallas_call(
        functools.partial(up_front_kernel, blocks=chips),
        grid_spec=pltpu.PrefetchScalarGridSpec(
            num_scalar_prefetch=1,
            grid=(steps + 1,),
            in_specs=[
                pl.BlockSpec((rows, width), lambda i, me: (0, 0)),
                pl.BlockSpec((chips, short, width), part),
                pl.BlockSpec((chips, short, width), part),
                pl.BlockSpec((chips, tall, width), fixed),
                pl.BlockSpec((chips, tall, width), fixed),
            ],
            out_specs=[
                pl.BlockSpec((width, width), lambda i, me: (0, i)),
                pl.BlockSpec((hidden, width), lambda i, me: (0, 0)),
                pl.BlockSpec((rows, width), lambda i, me: (0, jnp.minimum(i, steps - 1))),
            ],
        ),
        out_shape=[shape((width, wide)), shape((hidden, width)), shape((rows, hidden))],
        compiler_params=params(40),
        cost_estimate=cost(2 * rows * width * hidden, 8 * width * hidden),
        name="prepare_weights",
    )(lay.me, out_grad, up_own, up_other, down_own, down_other)


def hidden_grad_kernel(out_grad, down, grad):
    grad[...] = dot_nt(out_grad[...], down[...]).astype(BF16)


def hidden_grads(out_grad, down):
    rows, width = out_grad.shape
    hidden = down.shape[0]
    return pl.pallas_call(
        hidden_grad_kernel,
        grid=(hidden // width,),
        in_specs=[
            pl.BlockSpec((rows, width), lambda i: (0, 0)),
            pl.BlockSpec((width, width), lambda i: (i, 0)),
        ],
        out_specs=pl.BlockSpec((rows, width), lambda i: (0, i)),
        out_shape=shape((rows, hidden)),
        name="hidden_grads",
    )(out_grad, down)


ROOT = 0.7978845608028654
CUBE = 0.044715


def middle_kernel(
    me,
    *refs,
    positions,
    sequences,
    heads,
):
    pieces = refs[:GROUPS]
    tokens, out_grad, w_out, w_up, hidden_grad = refs[GROUPS : GROUPS + 5]
    rest = refs[GROUPS + 5 :]
    mixed, residual, normed, hidden, pre_grad, residual_grad, attn_grad = rest[:7]
    outs = rest[7 : 7 + GROUPS]
    parts, scratch, total = rest[7 + GROUPS :]
    step, last = pl.program_id(0), pl.num_programs(0) - 1
    z = me[1]

    @pl.when(step == 0)
    def _():
        for k, piece in enumerate(pieces):
            parts[z ^ k] = piece[...]
        from_heads(parts, scratch, positions, sequences, heads)
        join_lanes(scratch, mixed)
        value = tokens[...].astype(F32) + dot_nn(mixed[...], w_out[...])
        residual[...] = value
        scale = lax.rsqrt(jnp.mean(value * value, axis=-1, keepdims=True) + EPS)
        normed[...] = (value * scale).astype(BF16)

    u = dot_nn(normed[...], w_up[...])
    square = u * u
    tanh = jnp.tanh(ROOT * u * (1.0 + CUBE * square))
    half = 0.5 * (1.0 + tanh)
    hidden[...] = (u * half).astype(BF16)
    slope = half + 0.5 * u * (1.0 - tanh * tanh) * (ROOT * (1.0 + 3.0 * CUBE * square))
    pre = (slope * hidden_grad[...].astype(F32)).astype(BF16)
    pre_grad[...] = pre
    add = dot_nt(pre, w_up[...])

    @pl.when(step == 0)
    def _():
        total[...] = add

    @pl.when(step > 0)
    def _():
        total[...] += add

    @pl.when(step == last)
    def _():
        value = residual[...]
        scale = lax.rsqrt(jnp.mean(value * value, axis=-1, keepdims=True) + EPS)
        norm = value * scale
        grad = total[...]
        back = scale * (grad - norm * jnp.mean(grad * norm, axis=-1, keepdims=True))
        grad = out_grad[...].astype(F32) + back
        residual_grad[...] = grad
        attn_grad[...] = grad.astype(BF16)
        split_lanes(dot_nt(attn_grad[...], w_out[...]), scratch)
        to_heads(scratch, parts, positions, sequences, heads)
        for k, out in enumerate(outs):
            out[...] = parts[z ^ k]


def middle(lay, pieces, tokens, out_grad, out_weight, up_weight, hidden_grad, where):
    rows, width = tokens.shape
    hidden = hidden_grad.shape[1]
    steps = hidden // width
    piece = (lay.group, lay.positions, lay.lanes)

    def whole(*dims):
        return pl.BlockSpec(dims, lambda i, me: (0,) * len(dims))

    def part(i, me):
        return (0, i)

    out = pl.pallas_call(
        functools.partial(
            middle_kernel, positions=lay.positions, sequences=lay.sequences, heads=lay.heads
        ),
        grid_spec=pltpu.PrefetchScalarGridSpec(
            num_scalar_prefetch=1,
            grid=(steps,),
            in_specs=[whole(*piece)] * GROUPS
            + [
                whole(rows, width),
                whole(rows, width),
                pl.BlockSpec((width, width), lambda i, me: (0, where)),
                pl.BlockSpec((width, width), part),
                pl.BlockSpec((rows, width), part),
            ],
            out_specs=[
                whole(rows, width),
                whole(rows, width),
                whole(rows, width),
                pl.BlockSpec((rows, width), part),
                pl.BlockSpec((rows, width), part),
                whole(rows, width),
                whole(rows, width),
            ]
            + [whole(*piece)] * GROUPS,
            scratch_shapes=[
                pltpu.VMEM((GROUPS,) + piece, BF16),
                pltpu.VMEM((width // 128, rows, 128), F32),
                pltpu.VMEM((rows, width), F32),
            ],
        ),
        out_shape=[
            shape((rows, width)),
            shape((rows, width), F32),
            shape((rows, width)),
            shape((rows, hidden)),
            shape((rows, hidden)),
            shape((rows, width), F32),
            shape((rows, width)),
        ]
        + [shape(piece)] * GROUPS,
        compiler_params=params(48),
        cost_estimate=cost(4 * rows * width * (hidden + width), 16 * rows * hidden, rows * hidden),
        name="middle",
    )(lay.me, *pieces, tokens, out_grad, out_weight, up_weight, hidden_grad)
    return out[:7], list(out[7:])


def layer_out_kernel(residual, hidden, down, out):
    out[...] = (residual[...] + dot_nn(hidden[...], down[...])).astype(BF16)


def make_layer_out(residual, hidden, down):
    rows, width = residual.shape
    return pl.pallas_call(
        layer_out_kernel,
        out_shape=shape((rows, width)),
        in_specs=[vmem()] * 3,
        out_specs=vmem(),
        compiler_params=params(32),
        cost_estimate=cost(2 * hidden.size * width, 2 * (hidden.size + down.size) + 6 * residual.size),
        name="make_layer_out",
    )(residual, hidden, down)


def down_grad_kernel(me, hidden, out_grad, own, other, result, *, tall):
    part = pl.program_id(0)
    result[...] = dot_tn(hidden[...], out_grad[...]).astype(BF16)
    count = result.shape[0] // (2 * tall)
    for i in range(count):
        chip = part * count + i
        yr, zr, xr = (chip // 8) ^ me[0], ((chip // 2) % 4) ^ me[1], (chip % 2) ^ me[2]
        slot = (yr * 2 + xr) * 4 + zr
        for ref, core in ((own, me[3]), (other, 1 - me[3])):
            start = pl.multiple_of((2 * i + core) * tall, tall)
            ref[slot] = result[pl.ds(start, tall), :]


def down_grads(lay, hidden, out_grad):
    rows, width = out_grad.shape
    units = hidden.shape[1]
    tall = units // lay.devices
    chips = lay.devices // 2
    return pl.pallas_call(
        functools.partial(down_grad_kernel, tall=tall),
        grid_spec=pltpu.PrefetchScalarGridSpec(
            num_scalar_prefetch=1,
            grid=(units // width,),
            in_specs=[
                pl.BlockSpec((rows, width), lambda i, me: (0, i)),
                pl.BlockSpec((rows, width), lambda i, me: (0, 0)),
            ],
            out_specs=[pl.BlockSpec((chips, tall, width), lambda i, me: (0, 0, 0))] * 2,
            scratch_shapes=[pltpu.VMEM((width, width), BF16)],
        ),
        out_shape=[shape((chips, tall, width))] * 2,
        compiler_params=params(32),
        cost_estimate=cost(2 * rows * units * width, 2 * (rows + width) * units),
        name="down_grads",
    )(lay.me, hidden, out_grad)


def spread_rows(me, result, own, other, short, xs, dps):
    for chip in range(result.shape[0] // (2 * short)):
        yr, zr, xr = (chip // (GROUPS * xs)) ^ me[0], ((chip // xs) % GROUPS) ^ me[1], (chip % xs) ^ me[2]
        slot = (xr * dps + yr) * GROUPS + zr
        for ref, core in ((own, me[3]), (other, 1 - me[3])):
            start = pl.multiple_of(2 * short * chip + short * core, short)
            ref[slot] = result[pl.ds(start, short), :].astype(BF16)


def up_grad_kernel(me, normed, mixed, pre_grad, attn_grad, own, other, result):
    part, last = pl.program_id(0), pl.num_programs(0) - 1

    @pl.when(part < last)
    def _():
        result[...] = dot_tn(normed[...], pre_grad[...])

    @pl.when(part == last)
    def _():
        result[...] = dot_tn(mixed[...], attn_grad[...])

    spread_rows(me, result, own, other, own.shape[1], 2, 2)


def up_grads(lay, normed, mixed, pre_grad, attn_grad):
    rows, width = normed.shape
    units = pre_grad.shape[1]
    steps = units // width
    chips, short = lay.devices // 2, width // lay.devices

    def whole(i, me):
        return (0, 0)

    return pl.pallas_call(
        up_grad_kernel,
        grid_spec=pltpu.PrefetchScalarGridSpec(
            num_scalar_prefetch=1,
            grid=(steps + 1,),
            in_specs=[
                pl.BlockSpec((rows, width), whole),
                pl.BlockSpec((rows, width), whole),
                pl.BlockSpec((rows, width), lambda i, me: (0, jnp.minimum(i, steps - 1))),
                pl.BlockSpec((rows, width), whole),
            ],
            out_specs=[pl.BlockSpec((chips, short, width), lambda i, me: (0, 0, i))] * 2,
            scratch_shapes=[pltpu.VMEM((width, width), F32)],
        ),
        out_shape=[shape((chips, short, units + width))] * 2,
        compiler_params=params(32),
        cost_estimate=cost(2 * rows * width * (units + width), 4 * (rows + width) * units),
        name="up_grads",
    )(lay.me, normed, mixed, pre_grad, attn_grad)


def back_kernel(me, *refs, xs, dps, positions):
    pieces, rows, values = refs[:GROUPS], refs[GROUPS], refs[GROUPS + 1]
    outs = refs[GROUPS + 2 :]
    logit_outs, term_outs = outs[:dps], outs[dps : dps + 2 * GROUPS]
    grads, term, logit = outs[dps + 2 * GROUPS :]
    dp, z, x, c = me[0], me[1], me[2], me[3]
    part = logit_outs[0].shape[-1]
    for k, piece in enumerate(pieces):
        grads[:, pl.ds(pl.multiple_of((z ^ k) * positions, positions), positions), :] = piece[...]
    for head in range(rows.shape[0]):
        term[head] = dot_tn(rows[head], grads[head]).astype(BF16)
        soft = rows[head].astype(F32)
        product = soft * dot_nt(grads[head], values[head])
        logit[...] = (product - soft * jnp.sum(product, axis=-1, keepdims=True)).astype(BF16)
        for r, out in enumerate(logit_outs):
            start = pl.multiple_of((dp ^ r) * part, part)
            for k in range(GROUPS):
                base = pl.multiple_of((z ^ k) * positions, positions)
                out[k, head] = logit[pl.ds(base, positions), pl.ds(start, part)]
    index = 0
    for m in range(2):
        for k in range(GROUPS):
            for j in range(xs):
                block = ((z ^ k) * xs + (x ^ j)) * 2 + (c ^ m)
                term_outs[index][j] = term[:, pl.ds(pl.multiple_of(block * positions, positions), positions), :]
            index += 1


def mix_back(lay, pieces, rows, values):
    group, positions, length, lanes = lay.group, lay.positions, lay.length, lay.lanes
    part = length // lay.dp
    result = pl.pallas_call(
        functools.partial(back_kernel, xs=lay.xs, dps=lay.dp, positions=positions),
        in_specs=[smem()] + [vmem()] * (GROUPS + 2),
        out_specs=[vmem()] * (lay.dp + 2 * GROUPS),
        out_shape=[shape((GROUPS, group, positions, part))] * lay.dp
        + [shape((lay.xs, group, positions, lanes))] * (2 * GROUPS),
        scratch_shapes=[
            pltpu.VMEM((group, GROUPS * positions, lanes), BF16),
            pltpu.VMEM((group, length, lanes), BF16),
            pltpu.VMEM((GROUPS * positions, length), BF16),
        ],
        compiler_params=params(48),
        cost_estimate=cost(
            4 * group * GROUPS * positions * length * lanes, 8 * group * length * lanes
        ),
        name="mix_back",
    )(lay.me, *pieces, rows, values)
    return list(result[: lay.dp]), list(result[lay.dp :])


def value_grad_kernel(me, *refs, positions, sequences, heads, spread):
    pieces, normed = refs[:GROUPS], refs[GROUPS]
    if spread:
        total, own, other, parts, scratch, result = refs[GROUPS + 1 :]
    else:
        total, parts, scratch, result = refs[GROUPS + 1 :]
    for k, piece in enumerate(pieces):
        parts[me[1] ^ k] = piece[...]
    from_heads(parts, scratch, positions, sequences, heads)
    join_lanes(scratch, total)
    if spread:
        result[...] = dot_tn(normed[...], total[...])
        spread_rows(me, result, own, other, own.shape[1], 2, 2)


def value_grads(lay, pieces, normed):
    rows, width = normed.shape
    piece = (lay.group, lay.positions, lay.lanes)
    chips, short = lay.devices // 2, width // lay.devices
    outs = [shape((rows, width))] + ([shape((chips, short, width))] * 2 if lay.small else [])
    return pl.pallas_call(
        functools.partial(
            value_grad_kernel,
            positions=lay.positions,
            sequences=lay.sequences,
            heads=lay.heads,
            spread=lay.small,
        ),
        in_specs=[smem()] + [vmem()] * (GROUPS + 1),
        out_specs=[vmem()] * len(outs),
        out_shape=outs,
        scratch_shapes=[
            pltpu.VMEM((GROUPS,) + piece, BF16),
            pltpu.VMEM((width // 128, rows, 128), F32),
            pltpu.VMEM((width, width), F32),
        ],
        compiler_params=params(32),
        cost_estimate=cost(2 * rows * width * width, 8 * rows * width),
        name="value_grads",
    )(lay.me, *pieces, normed)


def tokens_grad_kernel(total, weight, tokens, residual_grad, out):
    grad = dot_nt(total[...], weight[...])
    inputs = tokens[...].astype(F32)
    scale = lax.rsqrt(jnp.mean(inputs * inputs, axis=-1, keepdims=True) + EPS)
    norm = inputs * scale
    back = scale * (grad - norm * jnp.mean(grad * norm, axis=-1, keepdims=True))
    out[...] = residual_grad[...] + back


def make_tokens_grad(total, weight, tokens, residual_grad):
    rows, width = tokens.shape
    return pl.pallas_call(
        tokens_grad_kernel,
        out_shape=shape((rows, width), F32),
        in_specs=[vmem()] * 4,
        out_specs=vmem(),
        compiler_params=params(24),
        cost_estimate=cost(2 * rows * width * width, 12 * rows * width),
        name="make_tokens_grad",
    )(total, weight, tokens, residual_grad)


def logits_out_kernel(me, *refs):
    pieces, out = refs[:GROUPS], refs[GROUPS]
    for k, piece in enumerate(pieces):
        out[me[1] ^ k] = piece[...].astype(F32)


def make_logits_grad(lay, pieces):
    group, positions, part = pieces[0].shape
    out = pl.pallas_call(
        logits_out_kernel,
        out_shape=shape((GROUPS, group, positions, part), F32),
        in_specs=[smem()] + [vmem()] * GROUPS,
        out_specs=vmem(),
        compiler_params=params(16),
        cost_estimate=cost(1e6, 24 * pieces[0].size),
        name="make_logits_grad",
    )(lay.me, *pieces)
    return out.reshape(lay.heads, positions, part)


def along_z(lay, pieces):
    return [pieces[0]] + [lay.swap(pieces[k], z=k) for k in range(1, GROUPS)]


def along_z_gather(lay, array):
    return jnp.stack([array] + [lay.swap(array, z=k) for k in range(1, GROUPS)])


def double(lay, array, **way):
    return jnp.concatenate([array, lay.swap(array, **way)])


def halve(lay, array, **way):
    half = array.shape[0] // 2
    return add_low(array[:half], lay.swap(array[half:], **way))


def sum_z(lay, array):
    total = array[0].astype(F32)
    for k in range(1, GROUPS):
        total = total + lay.swap(array[k], z=k).astype(F32)
    return total


def on_device(
    tokens,
    norm_gain1,
    value_weight,
    mixer_logits,
    out_weight,
    norm_gain2,
    up_weight,
    down_weight,
    out_grad,
):
    lay = Layout(tokens, mixer_logits)
    out_shape = tokens.shape
    width = lay.width
    tokens = tokens.reshape(lay.rows, width)
    out_grad = out_grad.reshape(lay.rows, width)
    gain_one = norm_gain1.astype(F32)[:, None]
    gain_two = norm_gain2.astype(F32)[:, None]
    value_rows = (gain_one * value_weight.astype(F32)).astype(BF16)
    up_rows = (gain_two * up_weight.astype(F32)).astype(BF16)
    small = lay.small

    with jax.named_scope("value_weight_gather"):
        if small:
            own = along_z_gather(lay, value_rows)
            four = [own, lay.swap(own, dp=1), lay.swap(own, x=1), lay.swap(own, dp=1, x=1)]
            own = jnp.concatenate(four)
            w_value = [own, lay.swap(own, c=1)]
        else:
            w_value = [lax.all_gather(value_rows, AXES, axis=0, tiled=True)]
    with jax.named_scope("mixing_rows"):
        pieces = softmax_rows(lay, mixer_logits)
        near = [lay.swap(pieces[k], z=k) for k in range(1, GROUPS)]
        far = [lay.swap(piece, dp=1) for piece in near]
        rows = [pieces[0]] + near + far
    with jax.named_scope("weight_gather"):
        if small:
            wide = along_z_gather(lay, jnp.concatenate([up_rows, out_weight], axis=1))
            wide = double(lay, double(lay, wide, dp=1).reshape((8,) + wide.shape[1:]), x=1)
            tall = along_z_gather(lay, down_weight)
            tall = double(lay, double(lay, tall, x=1), dp=1)
            wide_other, tall_other = lay.swap(wide, c=1), lay.swap(tall, c=1)
        else:
            w_up = lax.all_gather(up_rows, AXES, axis=0, tiled=True)
            w_out = lax.all_gather(out_weight, AXES, axis=0, tiled=True)
            w_down = lax.all_gather(down_weight, AXES, axis=0, tiled=True)

    with jax.named_scope("values"):
        normed_one, w_value, pieces = make_values(lay, tokens, w_value)
        first = along_z(lay, pieces)
        values = list(first)
        for j in range(1, lay.xs):
            values += [lay.swap(piece, x=j) for piece in first]
        values += [lay.swap(piece, c=1) for piece in values]
    with jax.named_scope("mixing"):
        mix_low, values, pieces = mix_values(lay, values, rows)
        pieces = along_z(lay, pieces)
    with jax.named_scope("weights"):
        if small:
            w_wide, w_down, hidden_grad = prepare_weights(
                lay, out_grad, wide, wide_other, tall, tall_other
            )
            w_out, w_up, where = w_wide, w_wide, w_down.shape[0] // width
        else:
            hidden_grad = hidden_grads(out_grad, w_down)
            where = 0
    with jax.named_scope("feed_forward"):
        kept, pieces = middle(lay, pieces, tokens, out_grad, w_out, w_up, hidden_grad, where)
        mixed, residual, normed_two, hidden, pre_grad, residual_grad, attn_grad = kept
        pieces = along_z(lay, pieces)
    with jax.named_scope("weight_grads"):
        if small:
            tall, tall_other = down_grads(lay, hidden, out_grad)
            wide, wide_other = up_grads(lay, normed_two, mixed, pre_grad, attn_grad)
            tall = add_low(tall, lay.swap(tall_other, c=1))
            wide = add_low(wide, lay.swap(wide_other, c=1))
            tall = halve(lay, halve(lay, tall, dp=1), x=1)
            wide = halve(lay, halve(lay, wide, x=1), dp=1)
            down_grad = sum_z(lay, tall)
            wide = sum_z(lay, wide)
            up_sum, out_wgrad = wide[:, : up_rows.shape[1]], wide[:, up_rows.shape[1] :]
        else:
            down_grad = scatter_sum(dot_tn(hidden, out_grad))
            up_sum = scatter_sum(dot_tn(normed_two, pre_grad))
            out_wgrad = scatter_sum(dot_tn(mixed, attn_grad))
        layer_out = make_layer_out(residual, hidden, w_down)
        up_grad = gain_two * up_sum
        gain_two_grad = jnp.sum(up_sum * up_weight.astype(F32), axis=1)
    with jax.named_scope("mixing_back"):
        logit_parts, terms = mix_back(lay, pieces, mix_low, values)
        arrived = []
        for k in range(GROUPS):
            piece = add_low(terms[k], lay.swap(terms[GROUPS + k], c=1))
            bit = lay.xs // 2
            while bit:
                piece = add_low(piece[:bit], lay.swap(piece[bit:], x=bit))
                bit //= 2
            arrived.append(piece[0])
        pieces = along_z(lay, arrived)
        while len(logit_parts) > 1:
            bit = len(logit_parts) // 2
            logit_parts = [
                add_low(logit_parts[r], lay.swap(logit_parts[r + bit], dp=bit)) for r in range(bit)
            ]
        logit_pieces = along_z(lay, [logit_parts[0][k] for k in range(GROUPS)])
        logits_grad = make_logits_grad(lay, logit_pieces)
    with jax.named_scope("value_grads"):
        total, *spread = value_grads(lay, pieces, normed_one)
        if small:
            own, other = spread
            own = add_low(own, lay.swap(other, c=1))
            four = own.reshape((4, GROUPS) + own.shape[1:])
            own = (
                four[0].astype(F32)
                + lay.swap(four[1], dp=1).astype(F32)
                + lay.swap(four[2], x=1).astype(F32)
                + lay.swap(four[3], dp=1, x=1).astype(F32)
            ).astype(BF16)
            value_sum = sum_z(lay, own)
        else:
            value_sum = scatter_sum(dot_tn(normed_one, total))
        tokens_grad = make_tokens_grad(total, w_value, tokens, residual_grad)
        value_wgrad = gain_one * value_sum
        gain_one_grad = jnp.sum(value_sum * value_weight.astype(F32), axis=1)
    return (
        layer_out.reshape(out_shape),
        tokens_grad.reshape(out_shape),
        gain_one_grad,
        value_wgrad,
        logits_grad,
        out_wgrad,
        gain_two_grad,
        up_grad,
        down_grad,
    )


def scatter_sum(array):
    return lax.psum_scatter(array.astype(BF16), AXES, scatter_dimension=0, tiled=True).astype(F32)


def solution(mesh):
    placed = (
        P("seq", "dp", None),
        P(("dp", "seq")),
        P(("dp", "seq"), None),
        P(None, "seq", None),
        P(("dp", "seq"), None),
        P(("dp", "seq")),
        P(("dp", "seq"), None),
        P(("dp", "seq"), None),
        P("seq", "dp", None),
    )
    return jax.shard_map(
        on_device,
        mesh=mesh,
        in_specs=placed,
        out_specs=(
            P("seq", "dp", None),
            P("seq", "dp", None),
            P(("dp", "seq")),
            P(("dp", "seq"), None),
            P(None, "seq", "dp"),
            P(("dp", "seq"), None),
            P(("dp", "seq")),
            P(("dp", "seq"), None),
            P(("dp", "seq"), None),
        ),
        check_vma=False,
    )
```

```python
import functools

import jax
import jax.numpy as jnp
from jax import lax
from jax.experimental import pallas as pl
from jax.experimental.pallas import tpu as pltpu
from jax.sharding import PartitionSpec as P

F32 = jnp.float32
BF16 = jnp.bfloat16
AXES = ("dp", "seq")
HEAD = 64
GROUPS = 4
EPS = 1e-06
COST = 50_000_000_000
MIB = 1 << 20


def smem():
    return pl.BlockSpec(memory_space=pltpu.SMEM)


def vmem():
    return pl.BlockSpec(memory_space=pltpu.VMEM)


def params(mib):
    return pltpu.CompilerParams(vmem_limit_bytes=mib * MIB)


def cost(flops, moved, trans=0):
    return pl.CostEstimate(flops=COST, bytes_accessed=1, transcendentals=0)


def shape(dims, kind=BF16):
    return jax.ShapeDtypeStruct(tuple(dims), kind)


def dot_nn(left, right):
    return lax.dot_general(left, right, (((1,), (0,)), ((), ())), preferred_element_type=F32)


def dot_nt(left, right):
    return lax.dot_general(left, right, (((1,), (1,)), ((), ())), preferred_element_type=F32)


def dot_tn(left, right):
    return lax.dot_general(left, right, (((0,), (0,)), ((), ())), preferred_element_type=F32)


class Layout:
    def __init__(self, tokens, logits):
        self.positions, self.sequences, self.width = tokens.shape
        self.heads, _, self.length = logits.shape
        self.dp, self.seq = lax.axis_size("dp"), lax.axis_size("seq")
        self.xs = self.seq // (2 * GROUPS)
        self.rows = self.positions * self.sequences
        self.group = self.heads // GROUPS
        self.lanes = self.sequences * HEAD
        self.devices = self.dp * self.seq
        dp, seq = lax.axis_index("dp"), lax.axis_index("seq")
        self.z, self.x, self.c = seq // (2 * self.xs), (seq // 2) % self.xs, seq % 2
        self.me = jnp.stack([dp, self.z, self.x, self.c, seq, seq, seq, seq]).astype(jnp.int32)
        self.small = self.dp == 2 and self.xs == 2

    def swap(self, array, dp=0, z=0, x=0, c=0):
        mask = ((dp * GROUPS + z) * self.xs + x) * 2 + c
        return lax.ppermute(array, AXES, [(i, i ^ mask) for i in range(self.devices)])


    def across_z(self, array):
        step = 2 * self.xs
        lines = [[z * step + i for z in range(GROUPS)] for i in range(step)]
        return lax.all_to_all(array, "seq", 0, 0, axis_index_groups=lines)


def add_low(left, right):
    return (left.astype(F32) + right.astype(F32)).astype(BF16)


def to_heads(source, target, positions, sequences, heads):
    group = heads // GROUPS
    low = lax.broadcasted_iota(jnp.int32, (positions, 2 * HEAD), 1) < HEAD
    for pair in range(sequences // 2):
        for two in range(heads // 2):
            a = source[two, pl.ds(2 * pair, positions, stride=sequences), :]
            b = source[two, pl.ds(2 * pair + 1, positions, stride=sequences), :]
            even = jnp.where(low, a, pltpu.roll(b, HEAD, 1))
            odd = jnp.where(low, pltpu.roll(a, HEAD, 1), b)
            for head, tile in ((2 * two, even), (2 * two + 1, odd)):
                target[head // group, head % group, :, 128 * pair : 128 * pair + 128] = tile.astype(BF16)


def from_heads(source, target, positions, sequences, heads):
    group = heads // GROUPS
    low = lax.broadcasted_iota(jnp.int32, (positions, 2 * HEAD), 1) < HEAD
    for pair in range(sequences // 2):
        for two in range(heads // 2):
            even, odd = (
                source[head // group, head % group, :, 128 * pair : 128 * pair + 128].astype(F32)
                for head in (2 * two, 2 * two + 1)
            )
            first = jnp.where(low, even, pltpu.roll(odd, HEAD, 1))
            second = jnp.where(low, pltpu.roll(even, HEAD, 1), odd)
            target[two, pl.ds(2 * pair, positions, stride=sequences), :] = first
            target[two, pl.ds(2 * pair + 1, positions, stride=sequences), :] = second


def split_lanes(value, target):
    for two in range(target.shape[0]):
        target[two] = value[:, 128 * two : 128 * two + 128]


def join_lanes(source, target):
    for two in range(source.shape[0]):
        target[:, 128 * two : 128 * two + 128] = source[two].astype(target.dtype)


def softmax_kernel(me, logits, out):
    positions, length = logits.shape[2], logits.shape[3]
    half = positions // 2
    start = pl.multiple_of((me[0] % 2) * half, half)
    column = lax.broadcasted_iota(jnp.int32, (half, length), 1)
    row = lax.broadcasted_iota(jnp.int32, (half, length), 0) + (me[4] * positions + start)
    allowed = column <= row
    for group in range(GROUPS):
        for head in range(logits.shape[1]):
            values = logits[group, head, pl.ds(start, half), :].astype(F32)
            masked = jnp.where(allowed, values, -jnp.inf)
            expo = jnp.exp(masked - jnp.max(masked, axis=-1, keepdims=True))
            out[group, head] = (expo * (1.0 / jnp.sum(expo, axis=-1, keepdims=True))).astype(BF16)


def softmax_rows(lay, logits):
    group, positions, length = lay.group, lay.positions, lay.length
    return pl.pallas_call(
        softmax_kernel,
        in_specs=[smem(), vmem()],
        out_specs=vmem(),
        out_shape=shape((GROUPS, group, positions // 2, length)),
        compiler_params=params(24),
        cost_estimate=cost(1e7, 4 * logits.size, logits.size),
        name="mix_rows",
    )(lay.me, logits.reshape(GROUPS, group, positions, length))


def chip_at(me, slot, x_first):
    high, mid, zr = slot // 8, (slot // GROUPS) % 2, slot % GROUPS
    xr, yr = (high, mid) if x_first else (mid, high)
    return ((me[0] ^ yr) * GROUPS + (me[1] ^ zr)) * 2 + (me[2] ^ xr)


def gather_rows(me, own, other, store, x_first):
    first = me[3] == 0
    for r in range(own.shape[0]):
        mine, theirs = own[r].astype(F32), other[r].astype(F32)
        block = jnp.concatenate([jnp.where(first, mine, theirs), jnp.where(first, theirs, mine)], 0)
        store(chip_at(me, r, x_first), block.astype(BF16))


def value_body(me, tokens, weight, scratch, parts, outs, normed, positions, sequences, heads):
    inputs = tokens[...].astype(F32)
    scale = lax.rsqrt(jnp.mean(inputs * inputs, axis=-1, keepdims=True) + EPS)
    low = (inputs * scale).astype(BF16)
    normed[...] = low
    split_lanes(dot_nn(low, weight[...]), scratch)
    to_heads(scratch, parts, positions, sequences, heads)
    for k, out in enumerate(outs):
        out[...] = parts[me[1] ^ k]


def value_kernel(me, tokens, *rest, positions, sequences, heads, blocks):
    if blocks:
        own, other, normed, whole, *outs = rest[:8]
        rows = whole.shape[0] // blocks

        def store(chip, block):
            whole[pl.ds(pl.multiple_of(chip * rows, rows), rows), :] = block

        gather_rows(me, own, other, store, True)
    else:
        whole, normed, *outs = rest[:6]
    parts, scratch = rest[-2:]
    value_body(me, tokens, whole, scratch, parts, outs, normed, positions, sequences, heads)


def make_values(lay, tokens, weight):
    rows, width = tokens.shape
    piece = (lay.group, lay.positions, lay.lanes)
    blocks = 0 if len(weight) == 1 else lay.devices // 2
    outs = [shape((rows, width))] + ([shape((width, width))] if blocks else []) + [shape(piece)] * GROUPS
    result = pl.pallas_call(
        functools.partial(
            value_kernel,
            positions=lay.positions,
            sequences=lay.sequences,
            heads=lay.heads,
            blocks=blocks,
        ),
        in_specs=[smem()] + [vmem()] * (1 + len(weight)),
        out_specs=[vmem()] * len(outs),
        out_shape=outs,
        scratch_shapes=[pltpu.VMEM((GROUPS,) + piece, BF16), pltpu.VMEM((width // 128, rows, 128), F32)],
        compiler_params=params(24),
        cost_estimate=cost(2 * rows * width * width, 6 * rows * width + 4 * width * width),
        name="make_values",
    )(lay.me, tokens, *weight)
    normed = result[0]
    whole = result[1] if blocks else weight[0]
    return normed, whole, list(result[-GROUPS:])


def mix_kernel(me, *refs, xs, positions):
    values = refs[: 2 * xs * GROUPS]
    refs = refs[2 * xs * GROUPS :]
    near, far, rows_out, values_out, mixed = refs
    z, x, c, side = me[1], me[2], me[3], me[0] % 2
    half = positions // 2
    for k in range(GROUPS):
        base = k * positions
        rows_out[:, pl.ds(pl.multiple_of(base + side * half, half), half), :] = near[k]
        rows_out[:, pl.ds(pl.multiple_of(base + (1 - side) * half, half), half), :] = far[k]
    index = 0
    for m in range(2):
        for j in range(xs):
            for k in range(GROUPS):
                block = ((z ^ k) * xs + (x ^ j)) * 2 + (c ^ m)
                values_out[:, pl.ds(pl.multiple_of(block * positions, positions), positions), :] = values[
                    index
                ][...]
                index += 1
    for head in range(rows_out.shape[0]):
        result = dot_nn(rows_out[head], values_out[head]).astype(BF16)
        for k in range(GROUPS):
            mixed[k, head] = result[k * positions : (k + 1) * positions]


def mix_values(lay, values, rows):
    group, positions, length, lanes = lay.group, lay.positions, lay.length, lay.lanes
    inputs = list(values) + list(rows)
    result = pl.pallas_call(
        functools.partial(mix_kernel, xs=lay.xs, positions=positions),
        in_specs=[smem()] + [vmem()] * len(inputs),
        out_specs=[vmem()] * 3,
        out_shape=[
            shape((group, GROUPS * positions, length)),
            shape((group, length, lanes)),
            shape((GROUPS, group, positions, lanes)),
        ],
        compiler_params=params(40),
        cost_estimate=cost(2 * group * GROUPS * positions * length * lanes, 8 * group * length * lanes),
        name="mix_values",
    )(lay.me, *inputs)
    return result


def dense(block):
    value = block[...]
    if value.ndim == 2:
        return value
    return value.astype(F32).reshape(-1, value.shape[-1]).astype(BF16)


def down_block(down, width):
    if down.ndim == 2:
        return pl.BlockSpec((width, width), lambda i, *_: (i, 0))
    devices, kinds, short, _ = down.shape
    parts = (kinds - 1) // 2
    return pl.BlockSpec((devices // parts, parts, short, width), lambda i, *_: (i, 0, 0, 0))


def up_block(up, width):
    if up.ndim == 2:
        return pl.BlockSpec((width, width), lambda i, *_: (0, i))
    devices, kinds, short, _ = up.shape
    parts = (kinds - 1) // 2
    return pl.BlockSpec((devices, 1, short, width), lambda i, *_: (0, parts + i, 0, 0))


def out_block(out, width):
    if out.ndim == 2:
        return pl.BlockSpec((width, width), lambda i, *_: (0, 0))
    devices, kinds, short, _ = out.shape
    return pl.BlockSpec((devices, 1, short, width), lambda i, *_: (0, kinds - 1, 0, 0))


ROOT = 0.7978845608028654
CUBE = 0.044715


def middle_kernel(me, *refs, positions, sequences, heads, spread):
    pieces, tokens, out_grad, w_out, w_up, w_down, layer_out, residual_grad, parts = refs[:9]
    grads = refs[9:-7]
    residual, normed, mixed, total, layer, scratch, result = refs[-7:]
    step, last = pl.program_id(0), pl.num_programs(0) - 1

    @pl.when(step == 0)
    def _():
        from_heads(pieces, scratch, positions, sequences, heads)
        join_lanes(scratch, mixed)
        value = tokens[...].astype(F32) + dot_nn(mixed[...], dense(w_out))
        residual[...] = value
        scale = lax.rsqrt(jnp.mean(value * value, axis=-1, keepdims=True) + EPS)
        normed[...] = (value * scale).astype(BF16)
        layer[...] = value
        total[...] = jnp.zeros_like(total)

    up, down = dense(w_up), dense(w_down)
    u = dot_nn(normed[...], up)
    back = dot_nt(out_grad[...], down)
    square = u * u
    tanh = jnp.tanh(ROOT * u * (1.0 + CUBE * square))
    half = 0.5 * (1.0 + tanh)
    hidden = (u * half).astype(BF16)
    slope = half + 0.5 * u * (1.0 - tanh * tanh) * (ROOT * (1.0 + 3.0 * CUBE * square))
    pre = (slope * back).astype(BF16)
    total[...] += dot_nt(pre, up)
    layer[...] += dot_nn(hidden, down)
    if spread:
        a_own, a_other, b_own, b_other, d_down = grads
        short = a_own.shape[1]
        width = result.shape[0]
        d_down[...] = dot_tn(hidden, out_grad[...]).astype(BF16)
        result[...] = dot_tn(normed[...], pre)

        @pl.when(step < last)
        def _():
            spread_rows(me, result, a_own, a_other, short, False)

        @pl.when(step == last)
        def _():
            spread_rows(me, result, b_own.at[:, :, :width], b_other.at[:, :, :width], short, True)
    else:
        d_up, d_down, d_out = grads
        d_down[...] = dot_tn(hidden, out_grad[...]).astype(BF16)
        d_up[...] = dot_tn(normed[...], pre).astype(BF16)

    @pl.when(step == last)
    def _():
        layer_out[...] = layer[...].astype(BF16)
        value = residual[...]
        scale = lax.rsqrt(jnp.mean(value * value, axis=-1, keepdims=True) + EPS)
        norm = value * scale
        grad = total[...]
        back = scale * (grad - norm * jnp.mean(grad * norm, axis=-1, keepdims=True))
        grad = out_grad[...].astype(F32) + back
        residual_grad[...] = grad
        attn_grad = grad.astype(BF16)
        split_lanes(dot_nt(attn_grad, dense(w_out)), scratch)
        to_heads(scratch, parts, positions, sequences, heads)
        if spread:
            result[...] = dot_tn(mixed[...], attn_grad)
            spread_rows(me, result, b_own.at[:, :, width:], b_other.at[:, :, width:], short, True)
        else:
            d_out[...] = dot_tn(mixed[...], attn_grad).astype(BF16)


def middle(lay, pieces, tokens, out_grad, out_weight, up_weight, down_weight, hidden):
    rows, width = tokens.shape
    steps = hidden // width
    piece = (GROUPS, lay.group, lay.positions, lay.lanes)
    chips, short = lay.devices // 2, width // lay.devices
    flat = (rows, width)

    def whole(*dims):
        return pl.BlockSpec(dims, lambda i, me: (0,) * len(dims))

    if lay.small:
        grads = [(chips, short, (steps - 1) * width)] * 2 + [(chips, short, 2 * width)] * 2
        grads += [(hidden, width)]
        block = (chips, short, width)
        specs = [pl.BlockSpec(block, lambda i, me: (0, 0, jnp.minimum(i, steps - 2)))] * 2
        specs += [whole(*dims) for dims in grads[2:4]]
        specs += [pl.BlockSpec((width, width), lambda i, me: (i, 0))]
    else:
        grads = [(width, hidden), (hidden, width), (width, width)]
        specs = [
            pl.BlockSpec((width, width), lambda i, me: (0, i)),
            pl.BlockSpec((width, width), lambda i, me: (i, 0)),
            whole(width, width),
        ]
    out = pl.pallas_call(
        functools.partial(
            middle_kernel,
            positions=lay.positions,
            sequences=lay.sequences,
            heads=lay.heads,
            spread=lay.small,
        ),
        grid_spec=pltpu.PrefetchScalarGridSpec(
            num_scalar_prefetch=1,
            grid=(steps,),
            in_specs=[whole(*piece), whole(*flat), whole(*flat)]
            + [out_block(out_weight, width), up_block(up_weight, width), down_block(down_weight, width)],
            out_specs=[whole(*flat), whole(*flat), whole(*piece)] + specs,
            scratch_shapes=[
                pltpu.VMEM(flat, F32),
                pltpu.VMEM(flat, BF16),
                pltpu.VMEM(flat, BF16),
                pltpu.VMEM(flat, F32),
                pltpu.VMEM(flat, F32),
                pltpu.VMEM((width // 128, rows, 128), F32),
                pltpu.VMEM((width, width), F32),
            ],
        ),
        out_shape=[shape(flat), shape(flat, F32), shape(piece)] + [shape(dims) for dims in grads],
        compiler_params=params(60),
        cost_estimate=cost(12 * rows * width * hidden, 16 * width * hidden, rows * hidden),
        name="middle",
    )(lay.me, pieces, tokens, out_grad, out_weight, up_weight, down_weight)
    return out[0], out[1], out[2], list(out[3:])


def slot_of(me, chip, x_first, z_plain=False):
    yr, zr, xr = (chip // 8) ^ me[0], (chip // 2) % 4, (chip % 2) ^ me[2]
    zr = zr if z_plain else zr ^ me[1]
    return ((xr * 2 + yr) if x_first else (yr * 2 + xr)) * GROUPS + zr


def spread_rows(me, result, own, other, short, x_first):
    for chip in range(result.shape[0] // (2 * short)):
        slot = slot_of(me, chip, x_first)
        for ref, core in ((own, me[3]), (other, 1 - me[3])):
            start = pl.multiple_of(2 * short * chip + short * core, short)
            ref[slot] = result[pl.ds(start, short), :].astype(BF16)


def back_kernel(me, *refs, xs, dps, positions, by_distance):
    pieces, rows, values = refs[:3]
    outs = refs[3:]
    logit_out, term_outs = outs[0], outs[1:5]
    grads, term, logit = outs[5:]
    dp, z, x, c = me[0], me[1], me[2], me[3]
    part = logit_out.shape[-1]
    for k in range(GROUPS):
        grads[:, k * positions : (k + 1) * positions, :] = pieces[k]
    for head in range(rows.shape[0]):
        term[head] = dot_tn(rows[head], grads[head]).astype(BF16)
        soft = rows[head].astype(F32)
        product = soft * dot_nt(grads[head], values[head])
        logit[...] = (product - soft * jnp.sum(product, axis=-1, keepdims=True)).astype(BF16)
        for r in range(dps):
            for k in range(GROUPS):
                start = pl.multiple_of((dp ^ r if by_distance else r) * part, part)
                base = pl.multiple_of((z ^ k) * positions, positions)
                logit_out[r, k, head] = logit[pl.ds(base, positions), pl.ds(start, part)]
    for m in range(2):
        for k in range(GROUPS):
            for j in range(xs):
                block = ((z ^ k) * xs + (x ^ j)) * 2 + (c ^ m)
                out = term_outs[2 * m + k // 2]
                out[j, k % 2] = term[:, pl.ds(pl.multiple_of(block * positions, positions), positions), :]


def mix_back(lay, pieces, rows, values):
    group, positions, length, lanes = lay.group, lay.positions, lay.length, lay.lanes
    part = length // lay.dp
    result = pl.pallas_call(
        functools.partial(
            back_kernel, xs=lay.xs, dps=lay.dp, positions=positions, by_distance=lay.small
        ),
        in_specs=[smem()] + [vmem()] * 3,
        out_specs=[vmem()] * 5,
        out_shape=[shape((lay.dp, GROUPS, group, positions, part))]
        + [shape((lay.xs, 2, group, positions, lanes))] * 4,
        scratch_shapes=[
            pltpu.VMEM((group, GROUPS * positions, lanes), BF16),
            pltpu.VMEM((group, length, lanes), BF16),
            pltpu.VMEM((GROUPS * positions, length), BF16),
        ],
        compiler_params=params(48),
        cost_estimate=cost(
            4 * group * GROUPS * positions * length * lanes, 8 * group * length * lanes
        ),
        name="mix_back",
    )(lay.me, pieces, rows, values)
    return result[0], list(result[1:])


def value_grad_kernel(me, *refs, positions, sequences, heads, spread):
    pieces, normed = refs[:GROUPS], refs[GROUPS]
    if spread:
        total, own, other, parts, scratch, result = refs[GROUPS + 1 :]
    else:
        total, parts, scratch, result = refs[GROUPS + 1 :]
    for k, piece in enumerate(pieces):
        parts[me[1] ^ k] = piece[...]
    from_heads(parts, scratch, positions, sequences, heads)
    join_lanes(scratch, total)
    if spread:
        result[...] = dot_tn(normed[...], total[...])
        spread_rows(me, result, own, other, own.shape[1], True)


def value_grads(lay, pieces, normed):
    rows, width = normed.shape
    piece = (lay.group, lay.positions, lay.lanes)
    chips, short = lay.devices // 2, width // lay.devices
    outs = [shape((rows, width))] + ([shape((chips, short, width))] * 2 if lay.small else [])
    return pl.pallas_call(
        functools.partial(
            value_grad_kernel,
            positions=lay.positions,
            sequences=lay.sequences,
            heads=lay.heads,
            spread=lay.small,
        ),
        in_specs=[smem()] + [vmem()] * (GROUPS + 1),
        out_specs=[vmem()] * len(outs),
        out_shape=outs,
        scratch_shapes=[
            pltpu.VMEM((GROUPS,) + piece, BF16),
            pltpu.VMEM((width // 128, rows, 128), F32),
            pltpu.VMEM((width, width), F32),
        ],
        compiler_params=params(32),
        cost_estimate=cost(2 * rows * width * width, 8 * rows * width),
        name="value_grads",
    )(lay.me, *pieces, normed)


def tokens_grad_kernel(total, weight, tokens, residual_grad, out):
    grad = dot_nt(total[...], weight[...])
    inputs = tokens[...].astype(F32)
    scale = lax.rsqrt(jnp.mean(inputs * inputs, axis=-1, keepdims=True) + EPS)
    norm = inputs * scale
    back = scale * (grad - norm * jnp.mean(grad * norm, axis=-1, keepdims=True))
    out[...] = residual_grad[...] + back


def make_tokens_grad(total, weight, tokens, residual_grad):
    rows, width = tokens.shape
    return pl.pallas_call(
        tokens_grad_kernel,
        out_shape=shape((rows, width), F32),
        in_specs=[vmem()] * 4,
        out_specs=vmem(),
        compiler_params=params(24),
        cost_estimate=cost(2 * rows * width * width, 12 * rows * width),
        name="make_tokens_grad",
    )(total, weight, tokens, residual_grad)


def logits_out_kernel(me, *refs):
    pieces, out = refs[:GROUPS], refs[GROUPS]
    for k, piece in enumerate(pieces):
        out[me[1] ^ k] = piece[...].astype(F32)


def make_logits_grad(lay, pieces):
    group, positions, part = pieces[0].shape
    out = pl.pallas_call(
        logits_out_kernel,
        out_shape=shape((GROUPS, group, positions, part), F32),
        in_specs=[smem()] + [vmem()] * GROUPS,
        out_specs=vmem(),
        compiler_params=params(16),
        cost_estimate=cost(1e6, 24 * pieces[0].size),
        name="make_logits_grad",
    )(lay.me, *pieces)
    return out.reshape(lay.heads, positions, part)


def after(value, *done):
    return lax.optimization_barrier((value, done))[0]


def along_z(lay, pieces):
    return [pieces[0]] + [lay.swap(pieces[k], z=k) for k in range(1, GROUPS)]


def along_z_gather(lay, array):
    return jnp.stack([array] + [lay.swap(array, z=k) for k in range(1, GROUPS)])


def double(lay, array, **way):
    return jnp.concatenate([array, lay.swap(array, **way)])


def halves(own, other):
    half = own.shape[0] // 2
    return add_low(own[:half], other[:half]), add_low(own[half:], other[half:])


def sum_z(lay, array):
    total = array[0].astype(F32)
    for k in range(1, GROUPS):
        total = total + lay.swap(array[k], z=k).astype(F32)
    return total


def on_device(
    tokens,
    norm_gain1,
    value_weight,
    mixer_logits,
    out_weight,
    norm_gain2,
    up_weight,
    down_weight,
    out_grad,
):
    lay = Layout(tokens, mixer_logits)
    out_shape = tokens.shape
    width = lay.width
    tokens = tokens.reshape(lay.rows, width)
    out_grad = out_grad.reshape(lay.rows, width)
    gain_one = norm_gain1.astype(F32)[:, None]
    gain_two = norm_gain2.astype(F32)[:, None]
    value_rows = (gain_one * value_weight.astype(F32)).astype(BF16)
    up_rows = (gain_two * up_weight.astype(F32)).astype(BF16)
    small = lay.small

    with jax.named_scope("weight_gather"):
        if small:
            packed = jnp.concatenate(
                [
                    down_weight.reshape((-1,) + value_rows.shape),
                    up_rows.reshape(up_rows.shape[0], -1, width).swapaxes(0, 1),
                    out_weight[None],
                ]
            )
            w_down = w_up = w_out = lax.all_gather(packed, AXES, axis=0)
        else:
            w_up = lax.all_gather(up_rows, AXES, axis=0, tiled=True)
            w_out = lax.all_gather(out_weight, AXES, axis=0, tiled=True)
            w_down = lax.all_gather(down_weight, AXES, axis=0, tiled=True)
    rows = softmax_rows(lay, mixer_logits)
    with jax.named_scope("mixing_rows"):
        rows = lay.across_z(rows)
    with jax.named_scope("value_weight_gather"):
        if small:
            own = along_z_gather(lay, value_rows)
            four = [own, lay.swap(own, dp=1), lay.swap(own, x=1), lay.swap(own, dp=1, x=1)]
            own = jnp.concatenate(four)
            w_value = [own, lay.swap(own, c=1)]
        else:
            w_value = [lax.all_gather(value_rows, AXES, axis=0, tiled=True)]
        w_value = after(w_value, rows)
    with jax.named_scope("values"):
        normed_one, w_value, value_parts = make_values(lay, tokens, w_value)
        first = along_z(lay, value_parts)
    with jax.named_scope("mixing_rows"):
        rows = [rows, lay.swap(rows, dp=1)]
    with jax.named_scope("values"):
        values = list(first)
        for j in range(1, lay.xs):
            values += [lay.swap(piece, x=j) for piece in first]
        values = values + [lay.swap(piece, c=1) for piece in after(values, rows[1])]
    with jax.named_scope("mixing"):
        mix_low, values, pieces = mix_values(lay, values, rows)
        pieces = lay.across_z(pieces)
    with jax.named_scope("feed_forward"):
        layer_out, residual_grad, pieces, grads = middle(
            lay, pieces, tokens, out_grad, w_out, w_up, w_down, up_rows.shape[1]
        )
        pieces = lay.across_z(pieces)
    with jax.named_scope("weight_grads"):
        if small:
            a_own, a_other, b_own, b_other, c_grad = grads
            down_grad = scatter_sum(c_grad)
            b_own, b_send = halves(b_own, lay.swap(b_other, c=1))
            b_other = lay.swap(b_send, x=1)
            a_own, a_send = halves(a_own, lay.swap(a_other, c=1))
            pieces = after(pieces, b_other, a_send)
            a_other = lay.swap(a_send, dp=1)
            b_own, b_send = halves(b_own, after(b_other, a_send))
            b_other = lay.swap(b_send, dp=1)
    with jax.named_scope("mixing_back"):
        logit_parts, terms = mix_back(lay, pieces, mix_low, values)
        others = [lay.swap(terms[2 + k], c=1) for k in (0, 1)]
        if small:
            others = after(others, b_other)
        arrived = []
        for k in (1, 0):
            piece, other = terms[k], others[k]
            bit = lay.xs // 2
            while bit:
                piece, send = halves(piece, other)
                other = lay.swap(send, x=bit)
                bit //= 2
            if small and k == 1:
                other = after(other, a_other)
            arrived.append(add_low(piece[0], other[0]))
        arrived = [arrived[1][0], arrived[1][1], arrived[0][0], arrived[0][1]]
    with jax.named_scope("weight_grads"):
        if small:
            a_own, a_send = halves(a_own, a_other)
            b_sum = add_low(b_own, b_other)
            b_parts = [lay.swap(b_sum[k], z=k) for k in range(1, GROUPS)]
            arrived = after(arrived, b_parts)
            a_other = lay.swap(after(a_send, arrived), x=1)
    with jax.named_scope("mixing_back"):
        pieces = along_z(lay, arrived)
        if small:
            logit_other = lay.swap(after(logit_parts[1], a_send), dp=1)
            pieces = after(pieces, a_other, logit_other)
        else:
            logit_parts = lax.psum_scatter(logit_parts, "dp", scatter_dimension=0)
    with jax.named_scope("value_grads"):
        total, *spread = value_grads(lay, pieces, normed_one)
        if small:
            own, other = spread
            own = add_low(own, lay.swap(other, c=1))
            four = own.reshape((4, GROUPS) + own.shape[1:])
            parts = [lay.swap(four[1], dp=1), lay.swap(four[2], x=1), lay.swap(four[3], dp=1, x=1)]
            own = four[0].astype(F32)
            for part in parts:
                own = own + part.astype(F32)
            own = own.astype(BF16)
            value_sum = sum_z(lay, own)
        else:
            value_sum = scatter_sum(dot_tn(normed_one, total))
        value_wgrad = gain_one * value_sum
        gain_one_grad = jnp.sum(value_sum * value_weight.astype(F32), axis=1)
    with jax.named_scope("mixing_back"):
        if small:
            logit_parts = add_low(logit_parts[0], after(logit_other, total))
        logits_grad = make_logits_grad(lay, along_z(lay, logit_parts))
    with jax.named_scope("weight_grads"):
        if small:
            a_sum = sum_z(lay, add_low(a_own, after(a_other, own)))
            b_total = b_sum[0].astype(F32)
            for part in b_parts:
                b_total = b_total + part.astype(F32)
            up_sum = jnp.concatenate([a_sum, b_total[:, :width]], axis=1)
            out_wgrad = b_total[:, width:]
            total = after(total, own)
        else:
            up_sum, down_grad, out_wgrad = (scatter_sum(grad) for grad in grads)
        tokens_grad = make_tokens_grad(total, w_value, tokens, residual_grad)
        up_grad = gain_two * up_sum
        gain_two_grad = jnp.sum(up_sum * up_weight.astype(F32), axis=1)
    return (
        layer_out.reshape(out_shape),
        tokens_grad.reshape(out_shape),
        gain_one_grad,
        value_wgrad,
        logits_grad,
        out_wgrad,
        gain_two_grad,
        up_grad,
        down_grad,
    )


def scatter_sum(array):
    return lax.psum_scatter(array.astype(BF16), AXES, scatter_dimension=0, tiled=True).astype(F32)


def solution(mesh):
    placed = (
        P("seq", "dp", None),
        P(("dp", "seq")),
        P(("dp", "seq"), None),
        P(None, "seq", None),
        P(("dp", "seq"), None),
        P(("dp", "seq")),
        P(("dp", "seq"), None),
        P(("dp", "seq"), None),
        P("seq", "dp", None),
    )
    return jax.shard_map(
        on_device,
        mesh=mesh,
        in_specs=placed,
        out_specs=(
            P("seq", "dp", None),
            P("seq", "dp", None),
            P(("dp", "seq")),
            P(("dp", "seq"), None),
            P(None, "seq", "dp"),
            P(("dp", "seq"), None),
            P(("dp", "seq")),
            P(("dp", "seq"), None),
            P(("dp", "seq"), None),
        ),
        check_vma=False,
    )
```

```python
import functools

import jax
import jax.numpy as jnp
from jax import lax
from jax.experimental import pallas as pl
from jax.experimental.pallas import tpu as pltpu
from jax.sharding import PartitionSpec as P

F32 = jnp.float32
BF16 = jnp.bfloat16
AXES = ("dp", "seq")
HEAD = 64
GROUPS = 4
EPS = 1e-06
COST = 50_000_000_000
FIRST = 2
SPLIT = 3
MIB = 1 << 20


def smem():
    return pl.BlockSpec(memory_space=pltpu.SMEM)


def vmem():
    return pl.BlockSpec(memory_space=pltpu.VMEM)


def params(mib):
    return pltpu.CompilerParams(vmem_limit_bytes=mib * MIB)


def cost(flops, moved, trans=0):
    return pl.CostEstimate(flops=COST, bytes_accessed=1, transcendentals=0)


def shape(dims, kind=BF16):
    return jax.ShapeDtypeStruct(tuple(dims), kind)


def dot_nn(left, right):
    return lax.dot_general(left, right, (((1,), (0,)), ((), ())), preferred_element_type=F32)


def dot_nt(left, right):
    return lax.dot_general(left, right, (((1,), (1,)), ((), ())), preferred_element_type=F32)


def dot_tn(left, right):
    return lax.dot_general(left, right, (((0,), (0,)), ((), ())), preferred_element_type=F32)


class Layout:
    def __init__(self, tokens, logits):
        self.positions, self.sequences, self.width = tokens.shape
        self.heads, _, self.length = logits.shape
        self.dp, self.seq = lax.axis_size("dp"), lax.axis_size("seq")
        self.xs = self.seq // (2 * GROUPS)
        self.rows = self.positions * self.sequences
        self.group = self.heads // GROUPS
        self.lanes = self.sequences * HEAD
        self.devices = self.dp * self.seq
        dp, seq = lax.axis_index("dp"), lax.axis_index("seq")
        self.z, self.x, self.c = seq // (2 * self.xs), (seq // 2) % self.xs, seq % 2
        self.me = jnp.stack([dp, self.z, self.x, self.c, seq, seq, seq, seq]).astype(jnp.int32)
        self.small = self.dp == 2 and self.xs == 2

    def swap(self, array, dp=0, z=0, x=0, c=0):
        mask = ((dp * GROUPS + z) * self.xs + x) * 2 + c
        return lax.ppermute(array, AXES, [(i, i ^ mask) for i in range(self.devices)])


    def across_z(self, array):
        step = 2 * self.xs
        lines = [[z * step + i for z in range(GROUPS)] for i in range(step)]
        return lax.all_to_all(array, "seq", 0, 0, axis_index_groups=lines)


def add_low(left, right):
    return (left.astype(F32) + right.astype(F32)).astype(BF16)


def to_heads(source, target, positions, sequences, heads):
    group = heads // GROUPS
    low = lax.broadcasted_iota(jnp.int32, (positions, 2 * HEAD), 1) < HEAD
    for pair in range(sequences // 2):
        for two in range(heads // 2):
            a = source[two, pl.ds(2 * pair, positions, stride=sequences), :]
            b = source[two, pl.ds(2 * pair + 1, positions, stride=sequences), :]
            even = jnp.where(low, a, pltpu.roll(b, HEAD, 1))
            odd = jnp.where(low, pltpu.roll(a, HEAD, 1), b)
            for head, tile in ((2 * two, even), (2 * two + 1, odd)):
                target[head // group, head % group, :, 128 * pair : 128 * pair + 128] = tile.astype(BF16)


def from_heads(source, target, positions, sequences, heads):
    group = heads // GROUPS
    low = lax.broadcasted_iota(jnp.int32, (positions, 2 * HEAD), 1) < HEAD
    for pair in range(sequences // 2):
        for two in range(heads // 2):
            even, odd = (
                source[head // group, head % group, :, 128 * pair : 128 * pair + 128].astype(F32)
                for head in (2 * two, 2 * two + 1)
            )
            first = jnp.where(low, even, pltpu.roll(odd, HEAD, 1))
            second = jnp.where(low, pltpu.roll(even, HEAD, 1), odd)
            target[two, pl.ds(2 * pair, positions, stride=sequences), :] = first
            target[two, pl.ds(2 * pair + 1, positions, stride=sequences), :] = second


def split_lanes(value, target):
    for two in range(target.shape[0]):
        target[two] = value[:, 128 * two : 128 * two + 128]


def join_lanes(source, target):
    for two in range(source.shape[0]):
        target[:, 128 * two : 128 * two + 128] = source[two].astype(target.dtype)


def softmax_kernel(me, logits, out):
    positions, length = logits.shape[2], logits.shape[3]
    half = positions // 2
    start = pl.multiple_of((me[0] % 2) * half, half)
    column = lax.broadcasted_iota(jnp.int32, (half, length), 1)
    row = lax.broadcasted_iota(jnp.int32, (half, length), 0) + (me[4] * positions + start)
    allowed = column <= row
    for group in range(GROUPS):
        for head in range(logits.shape[1]):
            values = logits[group, head, pl.ds(start, half), :].astype(F32)
            masked = jnp.where(allowed, values, -jnp.inf)
            expo = jnp.exp(masked - jnp.max(masked, axis=-1, keepdims=True))
            out[group, head] = (expo * (1.0 / jnp.sum(expo, axis=-1, keepdims=True))).astype(BF16)


def softmax_rows(lay, logits):
    group, positions, length = lay.group, lay.positions, lay.length
    return pl.pallas_call(
        softmax_kernel,
        in_specs=[smem(), vmem()],
        out_specs=vmem(),
        out_shape=shape((GROUPS, group, positions // 2, length)),
        compiler_params=params(24),
        cost_estimate=cost(1e7, 4 * logits.size, logits.size),
        name="mix_rows",
    )(lay.me, logits.reshape(GROUPS, group, positions, length))


def chip_at(me, slot, x_first):
    high, mid, zr = slot // 8, (slot // GROUPS) % 2, slot % GROUPS
    xr, yr = (high, mid) if x_first else (mid, high)
    return ((me[0] ^ yr) * GROUPS + (me[1] ^ zr)) * 2 + (me[2] ^ xr)


def gather_rows(me, own, other, store, x_first):
    first = me[3] == 0
    for r in range(own.shape[0]):
        mine, theirs = own[r].astype(F32), other[r].astype(F32)
        block = jnp.concatenate([jnp.where(first, mine, theirs), jnp.where(first, theirs, mine)], 0)
        store(chip_at(me, r, x_first), block.astype(BF16))


def value_body(me, tokens, weight, scratch, parts, outs, normed, positions, sequences, heads):
    inputs = tokens[...].astype(F32)
    scale = lax.rsqrt(jnp.mean(inputs * inputs, axis=-1, keepdims=True) + EPS)
    low = (inputs * scale).astype(BF16)
    normed[...] = low
    split_lanes(dot_nn(low, weight[...]), scratch)
    to_heads(scratch, parts, positions, sequences, heads)
    for k, out in enumerate(outs):
        out[...] = parts[me[1] ^ k]


def value_kernel(me, tokens, *rest, positions, sequences, heads, blocks):
    if blocks:
        own, other, normed, whole, *outs = rest[:8]
        rows = whole.shape[0] // blocks

        def store(chip, block):
            whole[pl.ds(pl.multiple_of(chip * rows, rows), rows), :] = block

        gather_rows(me, own, other, store, True)
    else:
        whole, normed, *outs = rest[:6]
    parts, scratch = rest[-2:]
    value_body(me, tokens, whole, scratch, parts, outs, normed, positions, sequences, heads)


def make_values(lay, tokens, weight):
    rows, width = tokens.shape
    piece = (lay.group, lay.positions, lay.lanes)
    blocks = 0 if len(weight) == 1 else lay.devices // 2
    outs = [shape((rows, width))] + ([shape((width, width))] if blocks else []) + [shape(piece)] * GROUPS
    result = pl.pallas_call(
        functools.partial(
            value_kernel,
            positions=lay.positions,
            sequences=lay.sequences,
            heads=lay.heads,
            blocks=blocks,
        ),
        in_specs=[smem()] + [vmem()] * (1 + len(weight)),
        out_specs=[vmem()] * len(outs),
        out_shape=outs,
        scratch_shapes=[pltpu.VMEM((GROUPS,) + piece, BF16), pltpu.VMEM((width // 128, rows, 128), F32)],
        compiler_params=params(24),
        cost_estimate=cost(2 * rows * width * width, 6 * rows * width + 4 * width * width),
        name="make_values",
    )(lay.me, tokens, *weight)
    normed = result[0]
    whole = result[1] if blocks else weight[0]
    return normed, whole, list(result[-GROUPS:])


def mix_kernel(me, *refs, xs, positions):
    values = refs[: 2 * xs]
    refs = refs[2 * xs :]
    near, far, rows_out, values_out, mixed = refs
    z, x, c, side = me[1], me[2], me[3], me[0] % 2
    half = positions // 2
    for k in range(GROUPS):
        base = k * positions
        rows_out[:, pl.ds(pl.multiple_of(base + side * half, half), half), :] = near[k]
        rows_out[:, pl.ds(pl.multiple_of(base + (1 - side) * half, half), half), :] = far[k]
    index = 0
    for m in range(2):
        for j in range(xs):
            for k in range(GROUPS):
                block = ((z ^ k) * xs + (x ^ j)) * 2 + (c ^ m)
                start = pl.multiple_of(block * positions, positions)
                values_out[:, pl.ds(start, positions), :] = values[index][k]
            index += 1
    for head in range(rows_out.shape[0]):
        result = dot_nn(rows_out[head], values_out[head]).astype(BF16)
        for k in range(GROUPS):
            mixed[k, head] = result[k * positions : (k + 1) * positions]


def mix_values(lay, values, rows):
    group, positions, length, lanes = lay.group, lay.positions, lay.length, lay.lanes
    inputs = list(values) + list(rows)
    result = pl.pallas_call(
        functools.partial(mix_kernel, xs=lay.xs, positions=positions),
        in_specs=[smem()] + [vmem()] * len(inputs),
        out_specs=[vmem()] * 3,
        out_shape=[
            shape((group, GROUPS * positions, length)),
            shape((group, length, lanes)),
            shape((GROUPS, group, positions, lanes)),
        ],
        compiler_params=params(40),
        cost_estimate=cost(2 * group * GROUPS * positions * length * lanes, 8 * group * length * lanes),
        name="mix_values",
    )(lay.me, *inputs)
    return result


ROOT = 0.7978845608028654
CUBE = 0.044715


def prepare_kernel(me, *refs):
    ups, out = refs[:4], refs[4]
    step, rows = pl.program_id(0), out.shape[0] // refs[0].shape[0]

    def store(chip, block):
        out[pl.ds(pl.multiple_of(chip * rows, rows), rows), :] = block

    pl.when(step < SPLIT)(lambda: gather_rows(me, ups[0].at[:, 0], ups[1].at[:, 0], store, True))
    pl.when(step >= SPLIT)(lambda: gather_rows(me, ups[2].at[:, 0], ups[3].at[:, 0], store, False))


def prepare_weights(lay, ups):
    chips, _, short, width = ups[0].shape
    kinds = ups[0].shape[1] + ups[2].shape[1]
    block = (chips, 1, short, width)
    specs = [pl.BlockSpec(block, lambda i, me: (0, jnp.minimum(i, SPLIT - 1), 0, 0))] * 2
    specs += [pl.BlockSpec(block, lambda i, me: (0, jnp.maximum(i - SPLIT, 0), 0, 0))] * 2
    return pl.pallas_call(
        prepare_kernel,
        grid_spec=pltpu.PrefetchScalarGridSpec(
            num_scalar_prefetch=1,
            grid=(kinds,),
            in_specs=specs,
            out_specs=pl.BlockSpec((width, width), lambda i, me: (0, i)),
        ),
        out_shape=shape((width, kinds * width)),
        compiler_params=params(24),
        cost_estimate=cost(width * width * kinds, 4 * width * width * kinds),
        name="prepare_weights",
    )(lay.me, *ups)


def middle_kernel(me, *refs, positions, sequences, heads, spread):
    step, last = pl.program_id(0), pl.num_programs(0) - 1
    if spread:
        *refs, w_down = refs
        pieces, tokens, out_grad, w_out, up = refs[:5]
        downs = refs[5:13]
        layer_out, residual_grad, parts = refs[13:16]
        grads = refs[16:-7]
        first, half_tall = me[3] == 0, downs[0].shape[1]
        count = w_down.shape[0] // (4 * half_tall)
        for i in range(count):
            for part in range(2):
                slot = slot_of(me, step * count + i, part == 0)
                far, slot = slot >= 8, slot % 8
                near_own, far_own, near_other, far_other = downs[4 * part : 4 * part + 4]
                mine = jnp.where(far, far_own[slot], near_own[slot])
                theirs = jnp.where(far, far_other[slot], near_other[slot])
                start = (4 * i + part) * half_tall
                w_down[start : start + half_tall, :] = jnp.where(first, mine, theirs)
                start += 2 * half_tall
                w_down[start : start + half_tall, :] = jnp.where(first, theirs, mine)
    else:
        pieces, tokens, out_grad, w_out, up, w_down, layer_out, residual_grad, parts = refs[:9]
        grads = refs[9:-7]
    residual, normed, mixed, total, layer, scratch, result = refs[-7:]

    @pl.when(step == 0)
    def _():
        from_heads(pieces, scratch, positions, sequences, heads)
        join_lanes(scratch, mixed)
        value = tokens[...].astype(F32) + dot_nn(mixed[...], w_out[...])
        residual[...] = value
        scale = lax.rsqrt(jnp.mean(value * value, axis=-1, keepdims=True) + EPS)
        normed[...] = (value * scale).astype(BF16)
        layer[...] = value
        total[...] = jnp.zeros_like(total)

    down = w_down[...]
    u = dot_nn(normed[...], up[...])
    back = dot_nt(out_grad[...], down)
    square = u * u
    tanh = jnp.tanh(u * (ROOT + ROOT * CUBE * square))
    half = 0.5 + 0.5 * tanh
    active = u * half
    hidden = active.astype(BF16)
    slope = half + active * (1.0 - tanh) * (ROOT + 3.0 * ROOT * CUBE * square)
    pre = (slope * back).astype(BF16)
    total[...] += dot_nt(pre, up[...])
    layer[...] += dot_nn(hidden, down)
    if spread:
        a_own, a_other, b_own, b_other, *c_parts = grads
        short, half_tall = a_own.shape[1], c_parts[0].shape[1]
        width = result.shape[0]
        result[...] = dot_tn(hidden, out_grad[...])
        for i in range(width // (4 * half_tall)):
            chip = step * (width // (4 * half_tall)) + i
            for part in range(2):
                slot = slot_of(me, chip, part == 0)
                for ref, core in ((c_parts[2 * part], me[3]), (c_parts[2 * part + 1], 1 - me[3])):
                    start = pl.multiple_of(((2 * i + core) * 2 + part) * half_tall, half_tall)
                    ref[slot] = result[pl.ds(start, half_tall), :].astype(BF16)
        result[...] = dot_tn(normed[...], pre)

        @pl.when(step < FIRST)
        def _():
            spread_rows(me, result, a_own, a_other, short, False)

        for kind in range(b_own.shape[2] // width - 1):

            @pl.when(step == FIRST + kind)
            def _(kind=kind):
                part = pl.ds(kind * width, width)
                spread_rows(me, result, b_own.at[:, :, part], b_other.at[:, :, part], short, True)
    else:
        d_up, d_down, d_out = grads
        d_down[...] = dot_tn(hidden, out_grad[...]).astype(BF16)
        d_up[...] = dot_tn(normed[...], pre).astype(BF16)

    @pl.when(step == last)
    def _():
        layer_out[...] = layer[...].astype(BF16)
        value = residual[...]
        scale = lax.rsqrt(jnp.mean(value * value, axis=-1, keepdims=True) + EPS)
        norm = value * scale
        grad = total[...]
        back = scale * (grad - norm * jnp.mean(grad * norm, axis=-1, keepdims=True))
        grad = out_grad[...].astype(F32) + back
        residual_grad[...] = grad
        attn_grad = grad.astype(BF16)
        split_lanes(dot_nt(attn_grad, w_out[...]), scratch)
        to_heads(scratch, parts, positions, sequences, heads)
        if spread:
            result[...] = dot_tn(mixed[...], attn_grad)
            part = pl.ds(b_own.shape[2] - width, width)
            spread_rows(me, result, b_own.at[:, :, part], b_other.at[:, :, part], short, True)
        else:
            d_out[...] = dot_tn(mixed[...], attn_grad).astype(BF16)


def middle(lay, pieces, tokens, out_grad, out_weight, up_weight, down_weight, hidden):
    rows, width = tokens.shape
    steps = hidden // width
    piece = (GROUPS, lay.group, lay.positions, lay.lanes)
    chips, short, tall = lay.devices // 2, width // lay.devices, hidden // lay.devices
    flat = (rows, width)

    def whole(*dims):
        return pl.BlockSpec(dims, lambda i, me: (0,) * len(dims))

    if lay.small:
        weights = [up_weight, up_weight, *down_weight]
        weight_specs = [
            pl.BlockSpec((width, width), lambda i, me: (0, steps)),
            pl.BlockSpec((width, width), lambda i, me: (0, i)),
        ]
        weight_specs += [whole(*array.shape) for array in down_weight]
        grads = [(chips, short, FIRST * width)] * 2 + [(chips, short, (steps + 1 - FIRST) * width)] * 2
        grads += [(chips, tall // 2, width)] * 4
        block = (chips, short, width)
        specs = [pl.BlockSpec(block, lambda i, me: (0, 0, jnp.minimum(i, FIRST - 1)))] * 2
        specs += [whole(*dims) for dims in grads[2:]]
    else:
        weights = [out_weight, up_weight, down_weight]
        weight_specs = [
            whole(width, width),
            pl.BlockSpec((width, width), lambda i, me: (0, i)),
            pl.BlockSpec((width, width), lambda i, me: (i, 0)),
        ]
        grads = [(width, hidden), (hidden, width), (width, width)]
        specs = [
            pl.BlockSpec((width, width), lambda i, me: (0, i)),
            pl.BlockSpec((width, width), lambda i, me: (i, 0)),
            whole(width, width),
        ]
    out = pl.pallas_call(
        functools.partial(
            middle_kernel,
            positions=lay.positions,
            sequences=lay.sequences,
            heads=lay.heads,
            spread=lay.small,
        ),
        grid_spec=pltpu.PrefetchScalarGridSpec(
            num_scalar_prefetch=1,
            grid=(steps,),
            in_specs=[whole(*piece), whole(*flat), whole(*flat)]
            + weight_specs,
            out_specs=[whole(*flat), whole(*flat), whole(*piece)] + specs,
            scratch_shapes=[
                pltpu.VMEM(flat, F32),
                pltpu.VMEM(flat, BF16),
                pltpu.VMEM(flat, BF16),
                pltpu.VMEM(flat, F32),
                pltpu.VMEM(flat, F32),
                pltpu.VMEM((width // 128, rows, 128), F32),
                pltpu.VMEM((width, width), F32),
            ]
            + [pltpu.VMEM((width, width), BF16)] * (1 if lay.small else 0),
        ),
        out_shape=[shape(flat), shape(flat, F32), shape(piece)] + [shape(dims) for dims in grads],
        compiler_params=params(60),
        cost_estimate=cost(12 * rows * width * hidden, 16 * width * hidden, rows * hidden),
        name="middle",
    )(lay.me, pieces, tokens, out_grad, *weights)
    return out[0], out[1], out[2], list(out[3:])


def slot_of(me, chip, x_first, z_plain=False):
    yr, zr, xr = (chip // 8) ^ me[0], (chip // 2) % 4, (chip % 2) ^ me[2]
    zr = zr if z_plain else zr ^ me[1]
    return ((xr * 2 + yr) if x_first else (yr * 2 + xr)) * GROUPS + zr


def spread_rows(me, result, own, other, short, x_first):
    for chip in range(result.shape[0] // (2 * short)):
        slot = slot_of(me, chip, x_first)
        for ref, core in ((own, me[3]), (other, 1 - me[3])):
            start = pl.multiple_of(2 * short * chip + short * core, short)
            ref[slot] = result[pl.ds(start, short), :].astype(BF16)


def back_kernel(me, *refs, xs, dps, positions, by_distance):
    pieces, rows, values = refs[:3]
    outs = refs[3:]
    logit_out, term_outs = outs[0], outs[1:3]
    grads, term, logit = outs[3:]
    dp, z, x, c = me[0], me[1], me[2], me[3]
    part = logit_out.shape[-1]
    for k in range(GROUPS):
        grads[:, k * positions : (k + 1) * positions, :] = pieces[k]
    for head in range(rows.shape[0]):
        term[head] = dot_tn(rows[head], grads[head]).astype(BF16)
        soft = rows[head].astype(F32)
        product = soft * dot_nt(grads[head], values[head])
        logit[...] = (product - soft * jnp.sum(product, axis=-1, keepdims=True)).astype(BF16)
        for r in range(dps):
            for k in range(GROUPS):
                start = pl.multiple_of((dp ^ r if by_distance else r) * part, part)
                logit_out[r, k, head] = logit[
                    k * positions : (k + 1) * positions, pl.ds(start, part)
                ]
    for m in range(2):
        for k in range(GROUPS):
            for j in range(xs):
                block = ((z ^ k) * xs + (x ^ j)) * 2 + (c ^ m)
                start = pl.multiple_of(block * positions, positions)
                term_outs[m][j, k] = term[:, pl.ds(start, positions), :]


def mix_back(lay, pieces, rows, values):
    group, positions, length, lanes = lay.group, lay.positions, lay.length, lay.lanes
    part = length // lay.dp
    result = pl.pallas_call(
        functools.partial(
            back_kernel, xs=lay.xs, dps=lay.dp, positions=positions, by_distance=lay.small
        ),
        in_specs=[smem()] + [vmem()] * 3,
        out_specs=[vmem()] * 3,
        out_shape=[shape((lay.dp, GROUPS, group, positions, part))]
        + [shape((lay.xs, GROUPS, group, positions, lanes))] * 2,
        scratch_shapes=[
            pltpu.VMEM((group, GROUPS * positions, lanes), BF16),
            pltpu.VMEM((group, length, lanes), BF16),
            pltpu.VMEM((GROUPS * positions, length), BF16),
        ],
        compiler_params=params(48),
        cost_estimate=cost(
            4 * group * GROUPS * positions * length * lanes, 8 * group * length * lanes
        ),
        name="mix_back",
    )(lay.me, pieces, rows, values)
    return result[0], list(result[1:])


def value_grad_kernel(me, *refs, positions, sequences, heads, spread):
    pieces, normed = refs[:GROUPS], refs[GROUPS]
    if spread:
        total, own, other, parts, scratch, result = refs[GROUPS + 1 :]
    else:
        total, parts, scratch, result = refs[GROUPS + 1 :]
    for k, piece in enumerate(pieces):
        parts[me[1] ^ k] = piece[...]
    from_heads(parts, scratch, positions, sequences, heads)
    join_lanes(scratch, total)
    if spread:
        result[...] = dot_tn(normed[...], total[...])
        spread_rows(me, result, own, other, own.shape[1], True)


def value_grads(lay, pieces, normed):
    rows, width = normed.shape
    piece = (lay.group, lay.positions, lay.lanes)
    chips, short = lay.devices // 2, width // lay.devices
    outs = [shape((rows, width))] + ([shape((chips, short, width))] * 2 if lay.small else [])
    return pl.pallas_call(
        functools.partial(
            value_grad_kernel,
            positions=lay.positions,
            sequences=lay.sequences,
            heads=lay.heads,
            spread=lay.small,
        ),
        in_specs=[smem()] + [vmem()] * (GROUPS + 1),
        out_specs=[vmem()] * len(outs),
        out_shape=outs,
        scratch_shapes=[
            pltpu.VMEM((GROUPS,) + piece, BF16),
            pltpu.VMEM((width // 128, rows, 128), F32),
            pltpu.VMEM((width, width), F32),
        ],
        compiler_params=params(32),
        cost_estimate=cost(2 * rows * width * width, 8 * rows * width),
        name="value_grads",
    )(lay.me, *pieces, normed)


def tokens_grad_kernel(total, weight, tokens, residual_grad, out):
    grad = dot_nt(total[...], weight[...])
    inputs = tokens[...].astype(F32)
    scale = lax.rsqrt(jnp.mean(inputs * inputs, axis=-1, keepdims=True) + EPS)
    norm = inputs * scale
    back = scale * (grad - norm * jnp.mean(grad * norm, axis=-1, keepdims=True))
    out[...] = residual_grad[...] + back


def make_tokens_grad(total, weight, tokens, residual_grad):
    rows, width = tokens.shape
    return pl.pallas_call(
        tokens_grad_kernel,
        out_shape=shape((rows, width), F32),
        in_specs=[vmem()] * 4,
        out_specs=vmem(),
        compiler_params=params(24),
        cost_estimate=cost(2 * rows * width * width, 12 * rows * width),
        name="make_tokens_grad",
    )(total, weight, tokens, residual_grad)


def logits_out_kernel(me, *refs):
    pieces, out = refs[:GROUPS], refs[GROUPS]
    for k, piece in enumerate(pieces):
        out[me[1] ^ k] = piece[...].astype(F32)


def make_logits_grad(lay, pieces):
    group, positions, part = pieces[0].shape
    out = pl.pallas_call(
        logits_out_kernel,
        out_shape=shape((GROUPS, group, positions, part), F32),
        in_specs=[smem()] + [vmem()] * GROUPS,
        out_specs=vmem(),
        compiler_params=params(16),
        cost_estimate=cost(1e6, 24 * pieces[0].size),
        name="make_logits_grad",
    )(lay.me, *pieces)
    return out.reshape(lay.heads, positions, part)


def add_kernel(*refs):
    left, right, *outs = refs
    half = outs[0].shape[0]
    for i, out in enumerate(outs):
        part = pl.ds(i * half, half)
        out[...] = (left[part].astype(F32) + right[part].astype(F32)).astype(BF16)


def add_split(left, right, parts=2):
    dims = (left.shape[0] // parts,) + left.shape[1:]
    return pl.pallas_call(
        add_kernel,
        out_shape=[shape(dims)] * parts,
        in_specs=[vmem()] * 2,
        out_specs=[vmem()] * parts,
        compiler_params=params(24),
        cost_estimate=cost(left.size, 6 * left.size),
        name="add_split",
    )(left, right)


def stack_kernel(*refs):
    *parts, out = refs
    for i, part in enumerate(parts):
        out[i] = part[...]


def stack_all(parts):
    return pl.pallas_call(
        stack_kernel,
        out_shape=shape((len(parts),) + parts[0].shape),
        in_specs=[vmem()] * len(parts),
        out_specs=vmem(),
        compiler_params=params(24),
        cost_estimate=cost(0, 4 * len(parts) * parts[0].size),
        name="stack_all",
    )(*parts)


def total_kernel(*refs):
    *parts, out = refs
    total = parts[0][...].astype(F32)
    for part in parts[1:]:
        total = total + part[...].astype(F32)
    out[...] = total.astype(BF16)


def add_all(parts):
    return pl.pallas_call(
        total_kernel,
        out_shape=shape(parts[0].shape),
        in_specs=[vmem()] * len(parts),
        out_specs=vmem(),
        compiler_params=params(24),
        cost_estimate=cost(len(parts) * parts[0].size, 4 * len(parts) * parts[0].size),
        name="add_all",
    )(*parts)


def after(value, *done):
    return lax.optimization_barrier((value, done))[0]


def along_z(lay, pieces):
    return [pieces[0]] + [lay.swap(pieces[k], z=k) for k in range(1, GROUPS)]


def along_z_gather(lay, array):
    return jnp.stack([array] + [lay.swap(array, z=k) for k in range(1, GROUPS)])


def double(lay, array, **way):
    return jnp.concatenate([array, lay.swap(array, **way)])


def halves(own, other):
    half = own.shape[0] // 2
    return add_low(own[:half], other[:half]), add_low(own[half:], other[half:])


def sum_z(lay, array):
    total = array[0].astype(F32)
    for k in range(1, GROUPS):
        total = total + lay.swap(array[k], z=k).astype(F32)
    return total


def on_device(
    tokens,
    norm_gain1,
    value_weight,
    mixer_logits,
    out_weight,
    norm_gain2,
    up_weight,
    down_weight,
    out_grad,
):
    lay = Layout(tokens, mixer_logits)
    out_shape = tokens.shape
    width = lay.width
    tokens = tokens.reshape(lay.rows, width)
    out_grad = out_grad.reshape(lay.rows, width)
    gain_one = norm_gain1.astype(F32)[:, None]
    gain_two = norm_gain2.astype(F32)[:, None]
    value_rows = (gain_one * value_weight.astype(F32)).astype(BF16)
    up_rows = (gain_two * up_weight.astype(F32)).astype(BF16)
    small = lay.small

    tie = lax.optimization_barrier
    rows = softmax_rows(lay, mixer_logits)
    if small:
        with jax.named_scope("round_one"):
            kinds = up_rows.reshape(up_rows.shape[0], -1, width).swapaxes(0, 1)
            wide = jnp.concatenate([kinds, out_weight[None], value_rows[None]])
            wide = [wide] + [lay.swap(wide, z=k) for k in range(1, GROUPS)]
            *wide, rows = tie((*wide, rows))
        with jax.named_scope("round_two"):
            rows = lay.across_z(rows)
            own = jnp.stack([part[-1] for part in wide])
            wide = jnp.stack([part[:-1] for part in wide])
            one, two = wide[:, :SPLIT], wide[:, SPLIT:]
            four = [own, lay.swap(own, dp=1), lay.swap(own, x=1), lay.swap(own, dp=1, x=1)]
            one_other, two_other = lay.swap(one, dp=1), lay.swap(two, x=1)
            own = jnp.concatenate(four)
            w_value = [own, lay.swap(own, c=1)]
            w_value, one_other, two_other, rows = tie((w_value, one_other, two_other, rows))
        with jax.named_scope("round_three"):
            normed_one, w_value, value_parts = make_values(lay, tokens, w_value)
            first = along_z(lay, value_parts)
            one, two = jnp.concatenate([one, one_other]), jnp.concatenate([two, two_other])
            one_other, two_other = lay.swap(one, x=1), lay.swap(two, dp=1)
            first, one_other, two_other = tie((first, one_other, two_other))
        with jax.named_scope("round_four"):
            values = stack_all(first)
            values_other = lay.swap(values, x=1)
            rows_other = lay.swap(rows, dp=1)
            tall = [down_weight] + [lay.swap(down_weight, z=k) for k in range(1, GROUPS)]
            values_other, rows_other, tall = tie((values_other, rows_other, tall))
            rows = [rows, rows_other]
        with jax.named_scope("round_five"):
            values = [values, values_other, lay.swap(values, c=1), lay.swap(values_other, c=1)]
            mix_low, values, pieces = mix_values(lay, values, rows)
            pieces = lay.across_z(pieces)
            tall, one, two, one_other, two_other = after(
                (tall, one, two, one_other, two_other), mix_low
            )
            tall = jnp.stack(tall)
            cut = tall.shape[1] // 2
            three, four = tall[:, :cut], tall[:, cut:]
            three_other, four_other = lay.swap(three, dp=1), lay.swap(four, x=1)
            one, two = jnp.concatenate([one, one_other]), jnp.concatenate([two, two_other])
            w_up = prepare_weights(lay, [one, lay.swap(one, c=1), two, lay.swap(two, c=1)])
            three, four = jnp.concatenate([three, three_other]), jnp.concatenate([four, four_other])
            three_other, four_other = lay.swap(three, x=1), lay.swap(four, dp=1)
            w_down = [three, three_other, four, four_other]
            w_down += [lay.swap(array, c=1) for array in w_down]
            w_down = [w_down[i] for i in (0, 1, 4, 5, 2, 3, 6, 7)]
            w_out = None
    else:
        w_up = lax.all_gather(up_rows, AXES, axis=0, tiled=True)
        w_out = lax.all_gather(out_weight, AXES, axis=0, tiled=True)
        w_down = lax.all_gather(down_weight, AXES, axis=0, tiled=True)
        w_value = [lax.all_gather(value_rows, AXES, axis=0, tiled=True)]
        rows = lay.across_z(rows)
        rows = [rows, lay.swap(rows, dp=1)]
        normed_one, w_value, value_parts = make_values(lay, tokens, w_value)
        values = [jnp.stack(along_z(lay, value_parts))]
        values += [lay.swap(values[0], x=j) for j in range(1, lay.xs)]
        values += [lay.swap(piece, c=1) for piece in values]
        mix_low, values, pieces = mix_values(lay, values, rows)
        pieces = lay.across_z(pieces)
    with jax.named_scope("feed_forward"):
        layer_out, residual_grad, pieces, grads = middle(
            lay, pieces, tokens, out_grad, w_out, w_up, w_down, up_rows.shape[1]
        )
        pieces = lay.across_z(pieces)
    with jax.named_scope("weight_grads"):
        if small:
            a_own, a_other, b_own, b_other, *c_parts = grads
            c_one, one_send = halves(c_parts[0], lay.swap(c_parts[1], c=1))
            c_two, two_send = halves(c_parts[2], lay.swap(c_parts[3], c=1))
            one_other, two_other = lay.swap(one_send, x=1), lay.swap(two_send, dp=1)
            a_own, a_send = halves(a_own, lay.swap(a_other, c=1))
            b_own, b_send = halves(b_own, lay.swap(b_other, c=1))
            pieces, one_other, two_other, a_send, b_send = tie(
                (pieces, one_other, two_other, a_send, b_send)
            )
            c_one, one_send = halves(c_one, one_other)
            c_two, two_send = halves(c_two, two_other)
            one_other, two_other = lay.swap(one_send, dp=1), lay.swap(two_send, x=1)
    with jax.named_scope("mixing_back"):
        logit_parts, terms = mix_back(lay, pieces, mix_low, values)
    if small:
        with jax.named_scope("mixing_back"):
            terms, one_other, two_other = tie((terms, one_other, two_other))
            term, term_send = add_split(terms[0], lay.swap(terms[1], c=1))
            term_other = lay.swap(term_send, x=1)
            logit_other = lay.swap(logit_parts[1], dp=1)
        with jax.named_scope("weight_grads"):
            c_sum = jnp.concatenate([add_low(c_one, one_other), add_low(c_two, two_other)], axis=1)
            c_rest = [lay.swap(c_sum[k], z=k) for k in range(1, GROUPS)]
        with jax.named_scope("mixing_back"):
            term_other, logit_other, c_rest = tie((term_other, logit_other, c_rest))
            (term,) = add_split(term[0], term_other[0], 1)
            pieces = along_z(lay, [term[k] for k in range(GROUPS)])
        with jax.named_scope("weight_grads"):
            a_other = lay.swap(after(a_send, term), dp=1)
            b_other = lay.swap(after(b_send, term), x=1)
            pieces, a_other, b_other = tie((pieces, a_other, b_other))
        with jax.named_scope("value_grads"):
            total, own, other = value_grads(lay, pieces, normed_one)
            other = lay.swap(other, c=1)
        with jax.named_scope("mixing_back"):
            logit_parts = add_low(logit_parts[0], after(logit_other, total))
            logit_parts = lay.across_z(logit_parts)
        with jax.named_scope("value_grads"):
            own = add_split(own, other, 4)
            parts = [lay.swap(own[1], dp=1), lay.swap(own[2], x=1), lay.swap(own[3], dp=1, x=1)]
        with jax.named_scope("weight_grads"):
            a_own, a_send = halves(a_own, after(a_other, own))
            b_own, b_send = halves(b_own, after(b_other, own))
            a_other, b_other = lay.swap(a_send, x=1), lay.swap(b_send, dp=1)
        with jax.named_scope("value_grads"):
            parts, a_other, b_other, logit_parts = tie((parts, a_other, b_other, logit_parts))
            own = add_all([own[0]] + list(parts))
        with jax.named_scope("weight_grads"):
            last = jnp.concatenate([own, add_low(a_own, a_other), add_low(b_own, b_other)], axis=2)
            last = sum_z(lay, last)
            value_sum, up_sum, out_wgrad = last[:, :width], last[:, width:-width], last[:, -width:]
            down_grad = c_sum[0].astype(F32)
            for part in c_rest:
                down_grad = down_grad + part.astype(F32)
            down_grad, total, logit_parts = after((down_grad, total, logit_parts), own)
        with jax.named_scope("mixing_back"):
            logits_grad = logit_parts.astype(F32).reshape(lay.heads, lay.positions, -1)
    else:
        with jax.named_scope("mixing_back"):
            piece, other = terms[0], lay.swap(terms[1], c=1)
            bit = lay.xs // 2
            while bit:
                piece, send = halves(piece, other)
                other = lay.swap(send, x=bit)
                bit //= 2
            piece = add_low(piece[0], other[0])
            pieces = along_z(lay, [piece[k] for k in range(GROUPS)])
            logit_parts = lax.psum_scatter(logit_parts, "dp", scatter_dimension=0)
            logits_grad = lay.across_z(logit_parts).astype(F32).reshape(lay.heads, lay.positions, -1)
        with jax.named_scope("value_grads"):
            (total,) = value_grads(lay, pieces, normed_one)
            value_sum = scatter_sum(dot_tn(normed_one, total))
        with jax.named_scope("weight_grads"):
            up_sum, down_grad, out_wgrad = (scatter_sum(grad) for grad in grads)
    with jax.named_scope("value_grads"):
        tokens_grad = make_tokens_grad(total, w_value, tokens, residual_grad)
        value_wgrad = gain_one * value_sum
        gain_one_grad = jnp.sum(value_sum * value_weight.astype(F32), axis=1)
    with jax.named_scope("weight_grads"):
        up_grad = gain_two * up_sum
        gain_two_grad = jnp.sum(up_sum * up_weight.astype(F32), axis=1)
    return (
        layer_out.reshape(out_shape),
        tokens_grad.reshape(out_shape),
        gain_one_grad,
        value_wgrad,
        logits_grad,
        out_wgrad,
        gain_two_grad,
        up_grad,
        down_grad,
    )


def scatter_sum(array):
    return lax.psum_scatter(array.astype(BF16), AXES, scatter_dimension=0, tiled=True).astype(F32)


def solution(mesh):
    placed = (
        P("seq", "dp", None),
        P(("dp", "seq")),
        P(("dp", "seq"), None),
        P(None, "seq", None),
        P(("dp", "seq"), None),
        P(("dp", "seq")),
        P(("dp", "seq"), None),
        P(("dp", "seq"), None),
        P("seq", "dp", None),
    )
    return jax.shard_map(
        on_device,
        mesh=mesh,
        in_specs=placed,
        out_specs=(
            P("seq", "dp", None),
            P("seq", "dp", None),
            P(("dp", "seq")),
            P(("dp", "seq"), None),
            P(None, "seq", "dp"),
            P(("dp", "seq"), None),
            P(("dp", "seq")),
            P(("dp", "seq"), None),
            P(("dp", "seq"), None),
        ),
        check_vma=False,
    )
```

```python
import functools

import jax
import jax.numpy as jnp
from jax import lax
from jax.experimental import pallas as pl
from jax.experimental.pallas import tpu as pltpu
from jax.sharding import PartitionSpec as P

F32 = jnp.float32
BF16 = jnp.bfloat16
AXES = ("dp", "seq")
HEAD = 64
GROUPS = 4
EPS = 1e-06
COST = 50_000_000_000
FIRST = 2
SPLIT = 3
MIB = 1 << 20


def smem():
    return pl.BlockSpec(memory_space=pltpu.SMEM)


def vmem():
    return pl.BlockSpec(memory_space=pltpu.VMEM)


def params(mib):
    return pltpu.CompilerParams(vmem_limit_bytes=mib * MIB)


def cost(flops, moved, trans=0):
    return pl.CostEstimate(flops=COST, bytes_accessed=1, transcendentals=0)


def shape(dims, kind=BF16):
    return jax.ShapeDtypeStruct(tuple(dims), kind)


def dot_nn(left, right):
    return lax.dot_general(left, right, (((1,), (0,)), ((), ())), preferred_element_type=F32)


def dot_nt(left, right):
    return lax.dot_general(left, right, (((1,), (1,)), ((), ())), preferred_element_type=F32)


def dot_tn(left, right):
    return lax.dot_general(left, right, (((0,), (0,)), ((), ())), preferred_element_type=F32)


class Layout:
    def __init__(self, tokens, logits):
        self.positions, self.sequences, self.width = tokens.shape
        self.heads, _, self.length = logits.shape
        self.dp, self.seq = lax.axis_size("dp"), lax.axis_size("seq")
        self.xs = self.seq // (2 * GROUPS)
        self.rows = self.positions * self.sequences
        self.group = self.heads // GROUPS
        self.lanes = self.sequences * HEAD
        self.devices = self.dp * self.seq
        dp, seq = lax.axis_index("dp"), lax.axis_index("seq")
        self.z, self.x, self.c = seq // (2 * self.xs), (seq // 2) % self.xs, seq % 2
        self.me = jnp.stack([dp, self.z, self.x, self.c, seq, seq, seq, seq]).astype(jnp.int32)
        self.small = self.dp == 2 and self.xs == 2

    def swap(self, array, dp=0, z=0, x=0, c=0):
        mask = ((dp * GROUPS + z) * self.xs + x) * 2 + c
        return lax.ppermute(array, AXES, [(i, i ^ mask) for i in range(self.devices)])


    def across_z(self, array):
        step = 2 * self.xs
        lines = [[z * step + i for z in range(GROUPS)] for i in range(step)]
        return lax.all_to_all(array, "seq", 0, 0, axis_index_groups=lines)


def add_low(left, right):
    return (left.astype(F32) + right.astype(F32)).astype(BF16)


def to_heads(source, target, positions, sequences, heads):
    group = heads // GROUPS
    low = lax.broadcasted_iota(jnp.int32, (positions, 2 * HEAD), 1) < HEAD
    for pair in range(sequences // 2):
        for two in range(heads // 2):
            a = source[two, pl.ds(2 * pair, positions, stride=sequences), :]
            b = source[two, pl.ds(2 * pair + 1, positions, stride=sequences), :]
            even = jnp.where(low, a, pltpu.roll(b, HEAD, 1))
            odd = jnp.where(low, pltpu.roll(a, HEAD, 1), b)
            for head, tile in ((2 * two, even), (2 * two + 1, odd)):
                target[head // group, head % group, :, 128 * pair : 128 * pair + 128] = tile.astype(BF16)


def from_heads(source, target, positions, sequences, heads):
    group = heads // GROUPS
    low = lax.broadcasted_iota(jnp.int32, (positions, 2 * HEAD), 1) < HEAD
    for pair in range(sequences // 2):
        for two in range(heads // 2):
            even, odd = (
                source[head // group, head % group, :, 128 * pair : 128 * pair + 128].astype(F32)
                for head in (2 * two, 2 * two + 1)
            )
            first = jnp.where(low, even, pltpu.roll(odd, HEAD, 1))
            second = jnp.where(low, pltpu.roll(even, HEAD, 1), odd)
            target[two, pl.ds(2 * pair, positions, stride=sequences), :] = first
            target[two, pl.ds(2 * pair + 1, positions, stride=sequences), :] = second


def split_lanes(value, target):
    for two in range(target.shape[0]):
        target[two] = value[:, 128 * two : 128 * two + 128]


def join_lanes(source, target):
    for two in range(source.shape[0]):
        target[:, 128 * two : 128 * two + 128] = source[two].astype(target.dtype)


def softmax_kernel(me, logits, out):
    positions, length = logits.shape[2], logits.shape[3]
    half = positions // 2
    start = pl.multiple_of((me[0] % 2) * half, half)
    column = lax.broadcasted_iota(jnp.int32, (half, length), 1)
    row = lax.broadcasted_iota(jnp.int32, (half, length), 0) + (me[4] * positions + start)
    allowed = column <= row
    for group in range(GROUPS):
        for head in range(logits.shape[1]):
            values = logits[group, head, pl.ds(start, half), :].astype(F32)
            masked = jnp.where(allowed, values, -jnp.inf)
            expo = jnp.exp(masked - jnp.max(masked, axis=-1, keepdims=True))
            out[group, head] = (expo * (1.0 / jnp.sum(expo, axis=-1, keepdims=True))).astype(BF16)


def softmax_rows(lay, logits):
    group, positions, length = lay.group, lay.positions, lay.length
    return pl.pallas_call(
        softmax_kernel,
        in_specs=[smem(), vmem()],
        out_specs=vmem(),
        out_shape=shape((GROUPS, group, positions // 2, length)),
        compiler_params=params(24),
        cost_estimate=cost(1e7, 4 * logits.size, logits.size),
        name="mix_rows",
    )(lay.me, logits.reshape(GROUPS, group, positions, length))


def chip_at(me, slot, x_first):
    high, mid, zr = slot // 8, (slot // GROUPS) % 2, slot % GROUPS
    xr, yr = (high, mid) if x_first else (mid, high)
    return ((me[0] ^ yr) * GROUPS + (me[1] ^ zr)) * 2 + (me[2] ^ xr)


def gather_rows(me, own, other, store, x_first):
    first = me[3] == 0
    for r in range(own.shape[0]):
        mine, theirs = own[r].astype(F32), other[r].astype(F32)
        block = jnp.concatenate([jnp.where(first, mine, theirs), jnp.where(first, theirs, mine)], 0)
        store(chip_at(me, r, x_first), block.astype(BF16))


def value_body(me, tokens, weight, scratch, parts, outs, normed, positions, sequences, heads):
    inputs = tokens[...].astype(F32)
    scale = lax.rsqrt(jnp.mean(inputs * inputs, axis=-1, keepdims=True) + EPS)
    low = (inputs * scale).astype(BF16)
    normed[...] = low
    split_lanes(dot_nn(low, weight[...]), scratch)
    to_heads(scratch, parts, positions, sequences, heads)
    for k, out in enumerate(outs):
        out[...] = parts[me[1] ^ k]


def value_kernel(me, tokens, *rest, positions, sequences, heads, blocks):
    if blocks:
        own, other, normed, whole, *outs = rest[:8]
        rows = whole.shape[0] // blocks

        def store(chip, block):
            whole[pl.ds(pl.multiple_of(chip * rows, rows), rows), :] = block

        gather_rows(me, own, other, store, True)
    else:
        whole, normed, *outs = rest[:6]
    parts, scratch = rest[-2:]
    value_body(me, tokens, whole, scratch, parts, outs, normed, positions, sequences, heads)


def make_values(lay, tokens, weight):
    rows, width = tokens.shape
    piece = (lay.group, lay.positions, lay.lanes)
    blocks = 0 if len(weight) == 1 else lay.devices // 2
    outs = [shape((rows, width))] + ([shape((width, width))] if blocks else []) + [shape(piece)] * GROUPS
    result = pl.pallas_call(
        functools.partial(
            value_kernel,
            positions=lay.positions,
            sequences=lay.sequences,
            heads=lay.heads,
            blocks=blocks,
        ),
        in_specs=[smem()] + [vmem()] * (1 + len(weight)),
        out_specs=[vmem()] * len(outs),
        out_shape=outs,
        scratch_shapes=[pltpu.VMEM((GROUPS,) + piece, BF16), pltpu.VMEM((width // 128, rows, 128), F32)],
        compiler_params=params(24),
        cost_estimate=cost(2 * rows * width * width, 6 * rows * width + 4 * width * width),
        name="make_values",
    )(lay.me, tokens, *weight)
    normed = result[0]
    whole = result[1] if blocks else weight[0]
    return normed, whole, list(result[-GROUPS:])


def mix_kernel(me, *refs, xs, positions):
    values = refs[: 2 * xs]
    refs = refs[2 * xs :]
    near, far, rows_out, values_out, mixed = refs
    z, x, c, side = me[1], me[2], me[3], me[0] % 2
    half = positions // 2
    for k in range(GROUPS):
        base = k * positions
        rows_out[:, pl.ds(pl.multiple_of(base + side * half, half), half), :] = near[k]
        rows_out[:, pl.ds(pl.multiple_of(base + (1 - side) * half, half), half), :] = far[k]
    index = 0
    for m in range(2):
        for j in range(xs):
            for k in range(GROUPS):
                block = ((z ^ k) * xs + (x ^ j)) * 2 + (c ^ m)
                start = pl.multiple_of(block * positions, positions)
                values_out[:, pl.ds(start, positions), :] = values[index][k]
            index += 1
    for head in range(rows_out.shape[0]):
        result = dot_nn(rows_out[head], values_out[head]).astype(BF16)
        for k in range(GROUPS):
            mixed[k, head] = result[k * positions : (k + 1) * positions]


def mix_values(lay, values, rows):
    group, positions, length, lanes = lay.group, lay.positions, lay.length, lay.lanes
    inputs = list(values) + list(rows)
    result = pl.pallas_call(
        functools.partial(mix_kernel, xs=lay.xs, positions=positions),
        in_specs=[smem()] + [vmem()] * len(inputs),
        out_specs=[vmem()] * 3,
        out_shape=[
            shape((group, GROUPS * positions, length)),
            shape((group, length, lanes)),
            shape((GROUPS, group, positions, lanes)),
        ],
        compiler_params=params(40),
        cost_estimate=cost(2 * group * GROUPS * positions * length * lanes, 8 * group * length * lanes),
        name="mix_values",
    )(lay.me, *inputs)
    return result


ROOT = 0.7978845608028654
CUBE = 0.044715


def prepare_kernel(me, *refs):
    ups, out = refs[:4], refs[4]
    step, rows = pl.program_id(0), out.shape[0] // refs[0].shape[0]

    def store(chip, block):
        out[pl.ds(pl.multiple_of(chip * rows, rows), rows), :] = block

    pl.when(step < SPLIT)(lambda: gather_rows(me, ups[0].at[:, 0], ups[1].at[:, 0], store, True))
    pl.when(step >= SPLIT)(lambda: gather_rows(me, ups[2].at[:, 0], ups[3].at[:, 0], store, False))


def prepare_weights(lay, ups):
    chips, _, short, width = ups[0].shape
    kinds = ups[0].shape[1] + ups[2].shape[1]
    block = (chips, 1, short, width)
    specs = [pl.BlockSpec(block, lambda i, me: (0, jnp.minimum(i, SPLIT - 1), 0, 0))] * 2
    specs += [pl.BlockSpec(block, lambda i, me: (0, jnp.maximum(i - SPLIT, 0), 0, 0))] * 2
    return pl.pallas_call(
        prepare_kernel,
        grid_spec=pltpu.PrefetchScalarGridSpec(
            num_scalar_prefetch=1,
            grid=(kinds,),
            in_specs=specs,
            out_specs=pl.BlockSpec((width, width), lambda i, me: (0, i)),
        ),
        out_shape=shape((width, kinds * width)),
        compiler_params=params(24),
        cost_estimate=pl.CostEstimate(flops=width, bytes_accessed=width, transcendentals=0),
        name="prepare_weights",
    )(lay.me, *ups)


def middle_kernel(me, *refs, positions, sequences, heads, spread):
    step, last = pl.program_id(0), pl.num_programs(0) - 1
    if spread:
        *refs, w_down = refs
        pieces, tokens, out_grad, w_out, up = refs[:5]
        downs = refs[5:13]
        layer_out, residual_grad, parts = refs[13:16]
        grads = refs[16:-7]
        first, half_tall = me[3] == 0, downs[0].shape[1]
        count = w_down.shape[0] // (4 * half_tall)
        for i in range(count):
            for part in range(2):
                slot = slot_of(me, step * count + i, part == 0)
                far, slot = slot >= 8, slot % 8
                near_own, far_own, near_other, far_other = downs[4 * part : 4 * part + 4]
                mine = jnp.where(far, far_own[slot], near_own[slot])
                theirs = jnp.where(far, far_other[slot], near_other[slot])
                start = (4 * i + part) * half_tall
                w_down[start : start + half_tall, :] = jnp.where(first, mine, theirs)
                start += 2 * half_tall
                w_down[start : start + half_tall, :] = jnp.where(first, theirs, mine)
    else:
        pieces, tokens, out_grad, w_out, up, w_down, layer_out, residual_grad, parts = refs[:9]
        grads = refs[9:-7]
    residual, normed, mixed, total, layer, scratch, result = refs[-7:]

    @pl.when(step == 0)
    def _():
        from_heads(pieces, scratch, positions, sequences, heads)
        join_lanes(scratch, mixed)
        value = tokens[...].astype(F32) + dot_nn(mixed[...], w_out[...])
        residual[...] = value
        scale = lax.rsqrt(jnp.mean(value * value, axis=-1, keepdims=True) + EPS)
        normed[...] = (value * scale).astype(BF16)
        layer[...] = value
        total[...] = jnp.zeros_like(total)

    down = w_down[...]
    u = dot_nn(normed[...], up[...])
    back = dot_nt(out_grad[...], down)
    square = u * u
    tanh = jnp.tanh(u * (ROOT + ROOT * CUBE * square))
    half = 0.5 + 0.5 * tanh
    active = u * half
    hidden = active.astype(BF16)
    slope = half + active * (1.0 - tanh) * (ROOT + 3.0 * ROOT * CUBE * square)
    pre = (slope * back).astype(BF16)
    total[...] += dot_nt(pre, up[...])
    layer[...] += dot_nn(hidden, down)
    if spread:
        a_own, a_other, b_own, b_other, *c_parts = grads
        short, half_tall = a_own.shape[1], c_parts[0].shape[1]
        width = result.shape[0]
        result[...] = dot_tn(hidden, out_grad[...])
        for i in range(width // (4 * half_tall)):
            chip = step * (width // (4 * half_tall)) + i
            for part in range(2):
                slot = slot_of(me, chip, part == 0)
                for ref, core in ((c_parts[2 * part], me[3]), (c_parts[2 * part + 1], 1 - me[3])):
                    start = pl.multiple_of(((2 * i + core) * 2 + part) * half_tall, half_tall)
                    ref[slot] = result[pl.ds(start, half_tall), :].astype(BF16)
        result[...] = dot_tn(normed[...], pre)

        @pl.when(step < FIRST)
        def _():
            spread_rows(me, result, a_own, a_other, short, False)

        for kind in range(b_own.shape[2] // width - 1):

            @pl.when(step == FIRST + kind)
            def _(kind=kind):
                part = pl.ds(kind * width, width)
                spread_rows(me, result, b_own.at[:, :, part], b_other.at[:, :, part], short, True)
    else:
        d_up, d_down, d_out = grads
        d_down[...] = dot_tn(hidden, out_grad[...]).astype(BF16)
        d_up[...] = dot_tn(normed[...], pre).astype(BF16)

    @pl.when(step == last)
    def _():
        layer_out[...] = layer[...].astype(BF16)
        value = residual[...]
        scale = lax.rsqrt(jnp.mean(value * value, axis=-1, keepdims=True) + EPS)
        norm = value * scale
        grad = total[...]
        back = scale * (grad - norm * jnp.mean(grad * norm, axis=-1, keepdims=True))
        grad = out_grad[...].astype(F32) + back
        residual_grad[...] = grad
        attn_grad = grad.astype(BF16)
        split_lanes(dot_nt(attn_grad, w_out[...]), scratch)
        to_heads(scratch, parts, positions, sequences, heads)
        if spread:
            result[...] = dot_tn(mixed[...], attn_grad)
            part = pl.ds(b_own.shape[2] - width, width)
            spread_rows(me, result, b_own.at[:, :, part], b_other.at[:, :, part], short, True)
        else:
            d_out[...] = dot_tn(mixed[...], attn_grad).astype(BF16)


def middle(lay, pieces, tokens, out_grad, out_weight, up_weight, down_weight, hidden):
    rows, width = tokens.shape
    steps = hidden // width
    piece = (GROUPS, lay.group, lay.positions, lay.lanes)
    chips, short, tall = lay.devices // 2, width // lay.devices, hidden // lay.devices
    flat = (rows, width)

    def whole(*dims):
        return pl.BlockSpec(dims, lambda i, me: (0,) * len(dims))

    if lay.small:
        weights = [up_weight, up_weight, *down_weight]
        weight_specs = [
            pl.BlockSpec((width, width), lambda i, me: (0, steps)),
            pl.BlockSpec((width, width), lambda i, me: (0, i)),
        ]
        weight_specs += [whole(*array.shape) for array in down_weight]
        grads = [(chips, short, FIRST * width)] * 2 + [(chips, short, (steps + 1 - FIRST) * width)] * 2
        grads += [(chips, tall // 2, width)] * 4
        block = (chips, short, width)
        specs = [pl.BlockSpec(block, lambda i, me: (0, 0, jnp.minimum(i, FIRST - 1)))] * 2
        specs += [whole(*dims) for dims in grads[2:]]
    else:
        weights = [out_weight, up_weight, down_weight]
        weight_specs = [
            whole(width, width),
            pl.BlockSpec((width, width), lambda i, me: (0, i)),
            pl.BlockSpec((width, width), lambda i, me: (i, 0)),
        ]
        grads = [(width, hidden), (hidden, width), (width, width)]
        specs = [
            pl.BlockSpec((width, width), lambda i, me: (0, i)),
            pl.BlockSpec((width, width), lambda i, me: (i, 0)),
            whole(width, width),
        ]
    out = pl.pallas_call(
        functools.partial(
            middle_kernel,
            positions=lay.positions,
            sequences=lay.sequences,
            heads=lay.heads,
            spread=lay.small,
        ),
        grid_spec=pltpu.PrefetchScalarGridSpec(
            num_scalar_prefetch=1,
            grid=(steps,),
            in_specs=[whole(*piece), whole(*flat), whole(*flat)]
            + weight_specs,
            out_specs=[whole(*flat), whole(*flat), whole(*piece)] + specs,
            scratch_shapes=[
                pltpu.VMEM(flat, F32),
                pltpu.VMEM(flat, BF16),
                pltpu.VMEM(flat, BF16),
                pltpu.VMEM(flat, F32),
                pltpu.VMEM(flat, F32),
                pltpu.VMEM((width // 128, rows, 128), F32),
                pltpu.VMEM((width, width), F32),
            ]
            + [pltpu.VMEM((width, width), BF16)] * (1 if lay.small else 0),
        ),
        out_shape=[shape(flat), shape(flat, F32), shape(piece)] + [shape(dims) for dims in grads],
        compiler_params=params(60),
        cost_estimate=cost(12 * rows * width * hidden, 16 * width * hidden, rows * hidden),
        name="middle",
    )(lay.me, pieces, tokens, out_grad, *weights)
    return out[0], out[1], out[2], list(out[3:])


def slot_of(me, chip, x_first, z_plain=False):
    yr, zr, xr = (chip // 8) ^ me[0], (chip // 2) % 4, (chip % 2) ^ me[2]
    zr = zr if z_plain else zr ^ me[1]
    return ((xr * 2 + yr) if x_first else (yr * 2 + xr)) * GROUPS + zr


def spread_rows(me, result, own, other, short, x_first):
    for chip in range(result.shape[0] // (2 * short)):
        slot = slot_of(me, chip, x_first)
        for ref, core in ((own, me[3]), (other, 1 - me[3])):
            start = pl.multiple_of(2 * short * chip + short * core, short)
            ref[slot] = result[pl.ds(start, short), :].astype(BF16)


def back_kernel(me, *refs, xs, dps, positions, by_distance):
    pieces, rows, values = refs[:3]
    outs = refs[3:]
    logit_out, term_outs = outs[0], outs[1:3]
    grads, term, logit = outs[3:]
    dp, z, x, c = me[0], me[1], me[2], me[3]
    part = logit_out.shape[-1]
    for k in range(GROUPS):
        grads[:, k * positions : (k + 1) * positions, :] = pieces[k]
    for head in range(rows.shape[0]):
        term[head] = dot_tn(rows[head], grads[head]).astype(BF16)
        soft = rows[head].astype(F32)
        product = soft * dot_nt(grads[head], values[head])
        logit[...] = (product - soft * jnp.sum(product, axis=-1, keepdims=True)).astype(BF16)
        for r in range(dps):
            for k in range(GROUPS):
                start = pl.multiple_of((dp ^ r if by_distance else r) * part, part)
                logit_out[r, k, head] = logit[
                    k * positions : (k + 1) * positions, pl.ds(start, part)
                ]
    for m in range(2):
        for k in range(GROUPS):
            for j in range(xs):
                block = ((z ^ k) * xs + (x ^ j)) * 2 + (c ^ m)
                start = pl.multiple_of(block * positions, positions)
                term_outs[m][j, k] = term[:, pl.ds(start, positions), :]


def mix_back(lay, pieces, rows, values):
    group, positions, length, lanes = lay.group, lay.positions, lay.length, lay.lanes
    part = length // lay.dp
    result = pl.pallas_call(
        functools.partial(
            back_kernel, xs=lay.xs, dps=lay.dp, positions=positions, by_distance=lay.small
        ),
        in_specs=[smem()] + [vmem()] * 3,
        out_specs=[vmem()] * 3,
        out_shape=[shape((lay.dp, GROUPS, group, positions, part))]
        + [shape((lay.xs, GROUPS, group, positions, lanes))] * 2,
        scratch_shapes=[
            pltpu.VMEM((group, GROUPS * positions, lanes), BF16),
            pltpu.VMEM((group, length, lanes), BF16),
            pltpu.VMEM((GROUPS * positions, length), BF16),
        ],
        compiler_params=params(48),
        cost_estimate=cost(
            4 * group * GROUPS * positions * length * lanes, 8 * group * length * lanes
        ),
        name="mix_back",
    )(lay.me, pieces, rows, values)
    return result[0], list(result[1:])


def value_grad_kernel(me, *refs, positions, sequences, heads, spread):
    pieces, normed = refs[:GROUPS], refs[GROUPS]
    if spread:
        total, own, other, parts, scratch, result = refs[GROUPS + 1 :]
    else:
        total, parts, scratch, result = refs[GROUPS + 1 :]
    for k, piece in enumerate(pieces):
        parts[me[1] ^ k] = piece[...]
    from_heads(parts, scratch, positions, sequences, heads)
    join_lanes(scratch, total)
    if spread:
        result[...] = dot_tn(normed[...], total[...])
        spread_rows(me, result, own, other, own.shape[1], True)


def value_grads(lay, pieces, normed):
    rows, width = normed.shape
    piece = (lay.group, lay.positions, lay.lanes)
    chips, short = lay.devices // 2, width // lay.devices
    outs = [shape((rows, width))] + ([shape((chips, short, width))] * 2 if lay.small else [])
    return pl.pallas_call(
        functools.partial(
            value_grad_kernel,
            positions=lay.positions,
            sequences=lay.sequences,
            heads=lay.heads,
            spread=lay.small,
        ),
        in_specs=[smem()] + [vmem()] * (GROUPS + 1),
        out_specs=[vmem()] * len(outs),
        out_shape=outs,
        scratch_shapes=[
            pltpu.VMEM((GROUPS,) + piece, BF16),
            pltpu.VMEM((width // 128, rows, 128), F32),
            pltpu.VMEM((width, width), F32),
        ],
        compiler_params=params(32),
        cost_estimate=cost(2 * rows * width * width, 8 * rows * width),
        name="value_grads",
    )(lay.me, *pieces, normed)


def tokens_grad_kernel(total, weight, tokens, residual_grad, out):
    grad = dot_nt(total[...], weight[...])
    inputs = tokens[...].astype(F32)
    scale = lax.rsqrt(jnp.mean(inputs * inputs, axis=-1, keepdims=True) + EPS)
    norm = inputs * scale
    back = scale * (grad - norm * jnp.mean(grad * norm, axis=-1, keepdims=True))
    out[...] = residual_grad[...] + back


def make_tokens_grad(total, weight, tokens, residual_grad):
    rows, width = tokens.shape
    return pl.pallas_call(
        tokens_grad_kernel,
        out_shape=shape((rows, width), F32),
        in_specs=[vmem()] * 4,
        out_specs=vmem(),
        compiler_params=params(24),
        cost_estimate=cost(2 * rows * width * width, 12 * rows * width),
        name="make_tokens_grad",
    )(total, weight, tokens, residual_grad)


def logits_out_kernel(me, *refs):
    pieces, out = refs[:GROUPS], refs[GROUPS]
    for k, piece in enumerate(pieces):
        out[me[1] ^ k] = piece[...].astype(F32)


def make_logits_grad(lay, pieces):
    group, positions, part = pieces[0].shape
    out = pl.pallas_call(
        logits_out_kernel,
        out_shape=shape((GROUPS, group, positions, part), F32),
        in_specs=[smem()] + [vmem()] * GROUPS,
        out_specs=vmem(),
        compiler_params=params(16),
        cost_estimate=cost(1e6, 24 * pieces[0].size),
        name="make_logits_grad",
    )(lay.me, *pieces)
    return out.reshape(lay.heads, positions, part)


def add_kernel(*refs):
    left, right, *outs = refs
    half = outs[0].shape[0]
    for i, out in enumerate(outs):
        part = pl.ds(i * half, half)
        out[...] = (left[part].astype(F32) + right[part].astype(F32)).astype(BF16)


def add_split(left, right, parts=2):
    dims = (left.shape[0] // parts,) + left.shape[1:]
    return pl.pallas_call(
        add_kernel,
        out_shape=[shape(dims)] * parts,
        in_specs=[vmem()] * 2,
        out_specs=[vmem()] * parts,
        compiler_params=params(24),
        cost_estimate=cost(left.size, 6 * left.size),
        name="add_split",
    )(left, right)


def stack_kernel(*refs):
    *parts, out = refs
    for i, part in enumerate(parts):
        out[i] = part[...]


def stack_all(parts):
    return pl.pallas_call(
        stack_kernel,
        out_shape=shape((len(parts),) + parts[0].shape),
        in_specs=[vmem()] * len(parts),
        out_specs=vmem(),
        compiler_params=params(24),
        cost_estimate=cost(0, 4 * len(parts) * parts[0].size),
        name="stack_all",
    )(*parts)


def pass_kernel(source, target):
    del source, target


def pass_on(array):
    return pl.pallas_call(
        pass_kernel,
        out_shape=shape(array.shape, array.dtype),
        in_specs=[pl.BlockSpec(memory_space=pl.ANY)],
        out_specs=pl.BlockSpec(memory_space=pl.ANY),
        input_output_aliases={0: 0},
        cost_estimate=cost(0, 0),
        name="pass_on",
    )(array)


def total_kernel(*refs):
    *parts, out = refs
    total = parts[0][...].astype(F32)
    for part in parts[1:]:
        total = total + part[...].astype(F32)
    out[...] = total.astype(BF16)


def add_all(parts):
    return pl.pallas_call(
        total_kernel,
        out_shape=shape(parts[0].shape),
        in_specs=[vmem()] * len(parts),
        out_specs=vmem(),
        compiler_params=params(24),
        cost_estimate=cost(len(parts) * parts[0].size, 4 * len(parts) * parts[0].size),
        name="add_all",
    )(*parts)


def after(value, *done):
    return lax.optimization_barrier((value, done))[0]


def along_z(lay, pieces):
    return [pieces[0]] + [lay.swap(pieces[k], z=k) for k in range(1, GROUPS)]


def along_z_gather(lay, array):
    return jnp.stack([array] + [lay.swap(array, z=k) for k in range(1, GROUPS)])


def double(lay, array, **way):
    return jnp.concatenate([array, lay.swap(array, **way)])


def halves(own, other):
    half = own.shape[0] // 2
    return add_low(own[:half], other[:half]), add_low(own[half:], other[half:])


def sum_z(lay, array):
    total = array[0].astype(F32)
    for k in range(1, GROUPS):
        total = total + lay.swap(array[k], z=k).astype(F32)
    return total


def on_device(
    tokens,
    norm_gain1,
    value_weight,
    mixer_logits,
    out_weight,
    norm_gain2,
    up_weight,
    down_weight,
    out_grad,
):
    lay = Layout(tokens, mixer_logits)
    out_shape = tokens.shape
    width = lay.width
    tokens = tokens.reshape(lay.rows, width)
    out_grad = out_grad.reshape(lay.rows, width)
    gain_one = norm_gain1.astype(F32)[:, None]
    gain_two = norm_gain2.astype(F32)[:, None]
    value_rows = (gain_one * value_weight.astype(F32)).astype(BF16)
    up_rows = (gain_two * up_weight.astype(F32)).astype(BF16)
    small = lay.small

    tie = lax.optimization_barrier
    rows = softmax_rows(lay, mixer_logits)
    if small:
        with jax.named_scope("round_one"):
            kinds = up_rows.reshape(up_rows.shape[0], -1, width).swapaxes(0, 1)
            wide = jnp.concatenate([kinds, out_weight[None], value_rows[None]])
            wide = [wide] + [lay.swap(wide, z=k) for k in range(1, GROUPS)]
            *wide, rows = tie((*wide, rows))
        with jax.named_scope("round_two"):
            rows = lay.across_z(rows)
            own = jnp.stack([part[-1] for part in wide])
            wide = jnp.stack([part[:-1] for part in wide])
            one, two = wide[:, :SPLIT], wide[:, SPLIT:]
            four = [own, lay.swap(own, dp=1), lay.swap(own, x=1), lay.swap(own, dp=1, x=1)]
            one_other, two_other = lay.swap(one, dp=1), lay.swap(two, x=1)
            four, one_other, two_other = tie((four, one_other, two_other))
            own = jnp.concatenate(four)
            w_value = [own, lay.swap(own, c=1)]
            one, two = jnp.concatenate([one, one_other]), jnp.concatenate([two, two_other])
            one_other, two_other = lay.swap(one, x=1), lay.swap(two, dp=1)
            w_value, rows = tie((w_value, rows))
        with jax.named_scope("round_three"):
            normed_one, w_value, value_parts = make_values(lay, tokens, w_value)
            first = along_z(lay, value_parts)
            first, one_other, two_other = tie((first, one_other, two_other))
        with jax.named_scope("round_four"):
            values = stack_all(first)
            values_other = lay.swap(values, x=1)
            rows_other = lay.swap(rows, dp=1)
            tall = [down_weight] + [lay.swap(down_weight, z=k) for k in range(1, GROUPS)]
            values_other, rows_other, tall = tie((values_other, rows_other, tall))
            rows = [rows, rows_other]
        with jax.named_scope("round_five"):
            tall = stack_all(tall)
            cut = tall.shape[1] // 2
            three, four = tall[:, :cut], tall[:, cut:]
            three_other, four_other = lay.swap(three, dp=1), lay.swap(four, x=1)
            values = [values, values_other, lay.swap(values, c=1), lay.swap(values_other, c=1)]
            mix_low, values, pieces = mix_values(lay, values, rows)
            pieces = lay.across_z(pieces)
            values = pass_on(values)
            three_other, four_other, values = tie((three_other, four_other, values))
            three, four = jnp.concatenate([three, three_other]), jnp.concatenate([four, four_other])
            three_other, four_other = lay.swap(three, x=1), lay.swap(four, dp=1)
            one, two = jnp.concatenate([one, one_other]), jnp.concatenate([two, two_other])
            w_up = [one, lay.swap(one, c=1), two, lay.swap(two, c=1)]
            w_up = prepare_weights(lay, w_up)
            w_down = [three, three_other, four, four_other]
            w_down += [lay.swap(array, c=1) for array in w_down]
            w_down = [w_down[i] for i in (0, 1, 4, 5, 2, 3, 6, 7)]
            w_out = None
    else:
        w_up = lax.all_gather(up_rows, AXES, axis=0, tiled=True)
        w_out = lax.all_gather(out_weight, AXES, axis=0, tiled=True)
        w_down = lax.all_gather(down_weight, AXES, axis=0, tiled=True)
        w_value = [lax.all_gather(value_rows, AXES, axis=0, tiled=True)]
        rows = lay.across_z(rows)
        rows = [rows, lay.swap(rows, dp=1)]
        normed_one, w_value, value_parts = make_values(lay, tokens, w_value)
        values = [jnp.stack(along_z(lay, value_parts))]
        values += [lay.swap(values[0], x=j) for j in range(1, lay.xs)]
        values += [lay.swap(piece, c=1) for piece in values]
        mix_low, values, pieces = mix_values(lay, values, rows)
        pieces = lay.across_z(pieces)
    with jax.named_scope("feed_forward"):
        layer_out, residual_grad, pieces, grads = middle(
            lay, pieces, tokens, out_grad, w_out, w_up, w_down, up_rows.shape[1]
        )
        pieces = lay.across_z(pieces)
    with jax.named_scope("weight_grads"):
        if small:
            a_own, a_other, b_own, b_other, *c_parts = grads
            c_one, one_send = halves(c_parts[0], lay.swap(c_parts[1], c=1))
            c_two, two_send = halves(c_parts[2], lay.swap(c_parts[3], c=1))
            one_other, two_other = lay.swap(one_send, x=1), lay.swap(two_send, dp=1)
            a_own, a_send = halves(a_own, lay.swap(a_other, c=1))
            b_own, b_send = halves(b_own, lay.swap(b_other, c=1))
            pieces, one_other, two_other, a_send, b_send = tie(
                (pieces, one_other, two_other, a_send, b_send)
            )
            c_one, one_send = halves(c_one, one_other)
            c_two, two_send = halves(c_two, two_other)
            one_other, two_other = lay.swap(one_send, dp=1), lay.swap(two_send, x=1)
    with jax.named_scope("mixing_back"):
        logit_parts, terms = mix_back(lay, pieces, mix_low, values)
    if small:
        with jax.named_scope("mixing_back"):
            terms, one_other, two_other = tie((terms, one_other, two_other))
            term, term_send = add_split(terms[0], lay.swap(terms[1], c=1))
            term_other = lay.swap(term_send, x=1)
            logit_other = lay.swap(logit_parts[1], dp=1)
        with jax.named_scope("weight_grads"):
            c_sum = jnp.concatenate([add_low(c_one, one_other), add_low(c_two, two_other)], axis=1)
            c_rest = [lay.swap(c_sum[k], z=k) for k in range(1, GROUPS)]
        with jax.named_scope("mixing_back"):
            term_other, logit_other, c_rest = tie((term_other, logit_other, c_rest))
            (term,) = add_split(term[0], term_other[0], 1)
            pieces = along_z(lay, [term[k] for k in range(GROUPS)])
        with jax.named_scope("weight_grads"):
            a_other = lay.swap(after(a_send, term), dp=1)
            b_other = lay.swap(after(b_send, term), x=1)
            pieces, a_other, b_other = tie((pieces, a_other, b_other))
        with jax.named_scope("value_grads"):
            total, own, other = value_grads(lay, pieces, normed_one)
            other = lay.swap(other, c=1)
        with jax.named_scope("mixing_back"):
            logit_parts = add_low(logit_parts[0], after(logit_other, total))
            logit_parts = lay.across_z(logit_parts)
        with jax.named_scope("value_grads"):
            own = add_split(own, other, 4)
            parts = [lay.swap(own[1], dp=1), lay.swap(own[2], x=1), lay.swap(own[3], dp=1, x=1)]
        with jax.named_scope("weight_grads"):
            a_own, a_send = halves(a_own, after(a_other, own))
            b_own, b_send = halves(b_own, after(b_other, own))
            a_other, b_other = lay.swap(a_send, x=1), lay.swap(b_send, dp=1)
        with jax.named_scope("value_grads"):
            parts, a_other, b_other, logit_parts = tie((parts, a_other, b_other, logit_parts))
            own = add_all([own[0]] + list(parts))
        with jax.named_scope("weight_grads"):
            last = jnp.concatenate([own, add_low(a_own, a_other), add_low(b_own, b_other)], axis=2)
            last = sum_z(lay, last)
            value_sum, up_sum, out_wgrad = last[:, :width], last[:, width:-width], last[:, -width:]
            down_grad = c_sum[0].astype(F32)
            for part in c_rest:
                down_grad = down_grad + part.astype(F32)
            down_grad, total, logit_parts = after((down_grad, total, logit_parts), own)
        with jax.named_scope("mixing_back"):
            logits_grad = logit_parts.astype(F32).reshape(lay.heads, lay.positions, -1)
    else:
        with jax.named_scope("mixing_back"):
            piece, other = terms[0], lay.swap(terms[1], c=1)
            bit = lay.xs // 2
            while bit:
                piece, send = halves(piece, other)
                other = lay.swap(send, x=bit)
                bit //= 2
            piece = add_low(piece[0], other[0])
            pieces = along_z(lay, [piece[k] for k in range(GROUPS)])
            logit_parts = lax.psum_scatter(logit_parts, "dp", scatter_dimension=0)
            logits_grad = lay.across_z(logit_parts).astype(F32).reshape(lay.heads, lay.positions, -1)
        with jax.named_scope("value_grads"):
            (total,) = value_grads(lay, pieces, normed_one)
            value_sum = scatter_sum(dot_tn(normed_one, total))
        with jax.named_scope("weight_grads"):
            up_sum, down_grad, out_wgrad = (scatter_sum(grad) for grad in grads)
    with jax.named_scope("value_grads"):
        tokens_grad = make_tokens_grad(total, w_value, tokens, residual_grad)
        value_wgrad = gain_one * value_sum
        gain_one_grad = jnp.sum(value_sum * value_weight.astype(F32), axis=1)
    with jax.named_scope("weight_grads"):
        up_grad = gain_two * up_sum
        gain_two_grad = jnp.sum(up_sum * up_weight.astype(F32), axis=1)
    return (
        layer_out.reshape(out_shape),
        tokens_grad.reshape(out_shape),
        gain_one_grad,
        value_wgrad,
        logits_grad,
        out_wgrad,
        gain_two_grad,
        up_grad,
        down_grad,
    )


def scatter_sum(array):
    return lax.psum_scatter(array.astype(BF16), AXES, scatter_dimension=0, tiled=True).astype(F32)


def solution(mesh):
    placed = (
        P("seq", "dp", None),
        P(("dp", "seq")),
        P(("dp", "seq"), None),
        P(None, "seq", None),
        P(("dp", "seq"), None),
        P(("dp", "seq")),
        P(("dp", "seq"), None),
        P(("dp", "seq"), None),
        P("seq", "dp", None),
    )
    return jax.shard_map(
        on_device,
        mesh=mesh,
        in_specs=placed,
        out_specs=(
            P("seq", "dp", None),
            P("seq", "dp", None),
            P(("dp", "seq")),
            P(("dp", "seq"), None),
            P(None, "seq", "dp"),
            P(("dp", "seq"), None),
            P(("dp", "seq")),
            P(("dp", "seq"), None),
            P(("dp", "seq"), None),
        ),
        check_vma=False,
    )
```

```python
import functools

import jax
import jax.numpy as jnp
from jax import lax
from jax.experimental import pallas as pl
from jax.experimental.pallas import tpu as pltpu
from jax.sharding import PartitionSpec as P

F32 = jnp.float32
BF16 = jnp.bfloat16
AXES = ("dp", "seq")
HEAD = 64
GROUPS = 4
EPS = 1e-06
SHARES = {
    "mix_rows": 50000000000,
    "make_values": 20000000000,
    "mix_values": 50000000000,
    "prepare_weights": 120000000000,
    "middle": 50000000000,
    "mix_back": 768,
    "value_grads": 120000000000,
    "make_tokens_grad": 8000000000,
    "add_split": 768,
    "stack_all": 50000000000,
    "pass_on": 50000000000,
    "add_all": 50000000000,
}
FIRST = 2
SPLIT = 3
MIB = 1 << 20


def smem():
    return pl.BlockSpec(memory_space=pltpu.SMEM)


def vmem():
    return pl.BlockSpec(memory_space=pltpu.VMEM)


def params(mib):
    return pltpu.CompilerParams(vmem_limit_bytes=mib * MIB)


def share(name):
    return pl.CostEstimate(flops=SHARES[name], bytes_accessed=1, transcendentals=0)


def shape(dims, kind=BF16):
    return jax.ShapeDtypeStruct(tuple(dims), kind)


def dot_nn(left, right):
    return lax.dot_general(left, right, (((1,), (0,)), ((), ())), preferred_element_type=F32)


def dot_nt(left, right):
    return lax.dot_general(left, right, (((1,), (1,)), ((), ())), preferred_element_type=F32)


def dot_tn(left, right):
    return lax.dot_general(left, right, (((0,), (0,)), ((), ())), preferred_element_type=F32)


class Layout:
    def __init__(self, tokens, logits):
        self.positions, self.sequences, self.width = tokens.shape
        self.heads, _, self.length = logits.shape
        self.dp, self.seq = lax.axis_size("dp"), lax.axis_size("seq")
        self.xs = self.seq // (2 * GROUPS)
        self.rows = self.positions * self.sequences
        self.group = self.heads // GROUPS
        self.lanes = self.sequences * HEAD
        self.devices = self.dp * self.seq
        dp, seq = lax.axis_index("dp"), lax.axis_index("seq")
        self.z, self.x, self.c = seq // (2 * self.xs), (seq // 2) % self.xs, seq % 2
        self.me = jnp.stack([dp, self.z, self.x, self.c, seq, seq, seq, seq]).astype(jnp.int32)
        self.small = self.dp == 2 and self.xs == 2

    def swap(self, array, dp=0, z=0, x=0, c=0):
        mask = ((dp * GROUPS + z) * self.xs + x) * 2 + c
        return lax.ppermute(array, AXES, [(i, i ^ mask) for i in range(self.devices)])


    def across_z(self, array):
        step = 2 * self.xs
        lines = [[z * step + i for z in range(GROUPS)] for i in range(step)]
        return lax.all_to_all(array, "seq", 0, 0, axis_index_groups=lines)


def add_low(left, right):
    return (left.astype(F32) + right.astype(F32)).astype(BF16)


def to_heads(source, target, positions, sequences, heads):
    group = heads // GROUPS
    low = lax.broadcasted_iota(jnp.int32, (positions, 2 * HEAD), 1) < HEAD
    for pair in range(sequences // 2):
        for two in range(heads // 2):
            a = source[two, pl.ds(2 * pair, positions, stride=sequences), :]
            b = source[two, pl.ds(2 * pair + 1, positions, stride=sequences), :]
            even = jnp.where(low, a, pltpu.roll(b, HEAD, 1))
            odd = jnp.where(low, pltpu.roll(a, HEAD, 1), b)
            for head, tile in ((2 * two, even), (2 * two + 1, odd)):
                target[head // group, head % group, :, 128 * pair : 128 * pair + 128] = tile.astype(BF16)


def from_heads(source, target, positions, sequences, heads):
    group = heads // GROUPS
    low = lax.broadcasted_iota(jnp.int32, (positions, 2 * HEAD), 1) < HEAD
    for pair in range(sequences // 2):
        for two in range(heads // 2):
            even, odd = (
                source[head // group, head % group, :, 128 * pair : 128 * pair + 128].astype(F32)
                for head in (2 * two, 2 * two + 1)
            )
            first = jnp.where(low, even, pltpu.roll(odd, HEAD, 1))
            second = jnp.where(low, pltpu.roll(even, HEAD, 1), odd)
            target[two, pl.ds(2 * pair, positions, stride=sequences), :] = first
            target[two, pl.ds(2 * pair + 1, positions, stride=sequences), :] = second


def split_lanes(value, target):
    for two in range(target.shape[0]):
        target[two] = value[:, 128 * two : 128 * two + 128]


def join_lanes(source, target):
    for two in range(source.shape[0]):
        target[:, 128 * two : 128 * two + 128] = source[two].astype(target.dtype)


def softmax_kernel(me, logits, out):
    positions, length = logits.shape[2], logits.shape[3]
    half = positions // 2
    start = pl.multiple_of((me[0] % 2) * half, half)
    column = lax.broadcasted_iota(jnp.int32, (half, length), 1)
    row = lax.broadcasted_iota(jnp.int32, (half, length), 0) + (me[4] * positions + start)
    allowed = column <= row
    for group in range(GROUPS):
        for head in range(logits.shape[1]):
            values = logits[group, head, pl.ds(start, half), :].astype(F32)
            masked = jnp.where(allowed, values, -jnp.inf)
            expo = jnp.exp(masked - jnp.max(masked, axis=-1, keepdims=True))
            out[group, head] = (expo * (1.0 / jnp.sum(expo, axis=-1, keepdims=True))).astype(BF16)


def softmax_rows(lay, logits):
    group, positions, length = lay.group, lay.positions, lay.length
    return pl.pallas_call(
        softmax_kernel,
        in_specs=[smem(), vmem()],
        out_specs=vmem(),
        out_shape=shape((GROUPS, group, positions // 2, length)),
        compiler_params=params(24),
        cost_estimate=share("mix_rows"),
        name="mix_rows",
    )(lay.me, logits.reshape(GROUPS, group, positions, length))


def chip_at(me, slot, x_first):
    high, mid, zr = slot // 8, (slot // GROUPS) % 2, slot % GROUPS
    xr, yr = (high, mid) if x_first else (mid, high)
    return ((me[0] ^ yr) * GROUPS + (me[1] ^ zr)) * 2 + (me[2] ^ xr)


def gather_rows(me, own, other, store, x_first):
    first = me[3] == 0
    for r in range(own.shape[0]):
        mine, theirs = own[r].astype(F32), other[r].astype(F32)
        block = jnp.concatenate([jnp.where(first, mine, theirs), jnp.where(first, theirs, mine)], 0)
        store(chip_at(me, r, x_first), block.astype(BF16))


def value_body(me, tokens, weight, scratch, parts, outs, normed, positions, sequences, heads):
    inputs = tokens[...].astype(F32)
    scale = lax.rsqrt(jnp.mean(inputs * inputs, axis=-1, keepdims=True) + EPS)
    low = (inputs * scale).astype(BF16)
    normed[...] = low
    split_lanes(dot_nn(low, weight[...]), scratch)
    to_heads(scratch, parts, positions, sequences, heads)
    for k, out in enumerate(outs):
        out[...] = parts[me[1] ^ k]


def value_kernel(me, tokens, *rest, positions, sequences, heads, blocks):
    if blocks:
        own, other, normed, whole, *outs = rest[:8]
        rows = whole.shape[0] // blocks

        def store(chip, block):
            whole[pl.ds(pl.multiple_of(chip * rows, rows), rows), :] = block

        gather_rows(me, own, other, store, True)
    else:
        whole, normed, *outs = rest[:6]
    parts, scratch = rest[-2:]
    value_body(me, tokens, whole, scratch, parts, outs, normed, positions, sequences, heads)


def make_values(lay, tokens, weight):
    rows, width = tokens.shape
    piece = (lay.group, lay.positions, lay.lanes)
    blocks = 0 if len(weight) == 1 else lay.devices // 2
    outs = [shape((rows, width))] + ([shape((width, width))] if blocks else []) + [shape(piece)] * GROUPS
    result = pl.pallas_call(
        functools.partial(
            value_kernel,
            positions=lay.positions,
            sequences=lay.sequences,
            heads=lay.heads,
            blocks=blocks,
        ),
        in_specs=[smem()] + [vmem()] * (1 + len(weight)),
        out_specs=[vmem()] * len(outs),
        out_shape=outs,
        scratch_shapes=[pltpu.VMEM((GROUPS,) + piece, BF16), pltpu.VMEM((width // 128, rows, 128), F32)],
        compiler_params=params(24),
        cost_estimate=share("make_values"),
        name="make_values",
    )(lay.me, tokens, *weight)
    normed = result[0]
    whole = result[1] if blocks else weight[0]
    return normed, whole, list(result[-GROUPS:])


def mix_kernel(me, *refs, xs, positions):
    values = refs[: 2 * xs]
    refs = refs[2 * xs :]
    near, far, rows_out, values_out, mixed = refs
    z, x, c, side = me[1], me[2], me[3], me[0] % 2
    half = positions // 2
    for k in range(GROUPS):
        base = k * positions
        rows_out[:, pl.ds(pl.multiple_of(base + side * half, half), half), :] = near[k]
        rows_out[:, pl.ds(pl.multiple_of(base + (1 - side) * half, half), half), :] = far[k]
    index = 0
    for m in range(2):
        for j in range(xs):
            for k in range(GROUPS):
                block = ((z ^ k) * xs + (x ^ j)) * 2 + (c ^ m)
                start = pl.multiple_of(block * positions, positions)
                values_out[:, pl.ds(start, positions), :] = values[index][k]
            index += 1
    for head in range(rows_out.shape[0]):
        result = dot_nn(rows_out[head], values_out[head]).astype(BF16)
        for k in range(GROUPS):
            mixed[k, head] = result[k * positions : (k + 1) * positions]


def mix_values(lay, values, rows):
    group, positions, length, lanes = lay.group, lay.positions, lay.length, lay.lanes
    inputs = list(values) + list(rows)
    result = pl.pallas_call(
        functools.partial(mix_kernel, xs=lay.xs, positions=positions),
        in_specs=[smem()] + [vmem()] * len(inputs),
        out_specs=[vmem()] * 3,
        out_shape=[
            shape((group, GROUPS * positions, length)),
            shape((group, length, lanes)),
            shape((GROUPS, group, positions, lanes)),
        ],
        compiler_params=params(40),
        cost_estimate=share("mix_values"),
        name="mix_values",
    )(lay.me, *inputs)
    return result


ROOT = 0.7978845608028654
CUBE = 0.044715


def prepare_kernel(me, *refs):
    ups, out = refs[:4], refs[4]
    step, rows = pl.program_id(0), out.shape[0] // refs[0].shape[0]

    def store(chip, block):
        out[pl.ds(pl.multiple_of(chip * rows, rows), rows), :] = block

    pl.when(step < SPLIT)(lambda: gather_rows(me, ups[0].at[:, 0], ups[1].at[:, 0], store, True))
    pl.when(step >= SPLIT)(lambda: gather_rows(me, ups[2].at[:, 0], ups[3].at[:, 0], store, False))


def prepare_weights(lay, ups):
    chips, _, short, width = ups[0].shape
    kinds = ups[0].shape[1] + ups[2].shape[1]
    block = (chips, 1, short, width)
    specs = [pl.BlockSpec(block, lambda i, me: (0, jnp.minimum(i, SPLIT - 1), 0, 0))] * 2
    specs += [pl.BlockSpec(block, lambda i, me: (0, jnp.maximum(i - SPLIT, 0), 0, 0))] * 2
    return pl.pallas_call(
        prepare_kernel,
        grid_spec=pltpu.PrefetchScalarGridSpec(
            num_scalar_prefetch=1,
            grid=(kinds,),
            in_specs=specs,
            out_specs=pl.BlockSpec((width, width), lambda i, me: (0, i)),
        ),
        out_shape=shape((width, kinds * width)),
        compiler_params=params(24),
        cost_estimate=share("prepare_weights"),
        name="prepare_weights",
    )(lay.me, *ups)


def middle_kernel(me, *refs, positions, sequences, heads, spread):
    step, last = pl.program_id(0), pl.num_programs(0) - 1
    if spread:
        *refs, w_down = refs
        pieces, tokens, out_grad, w_out, up = refs[:5]
        downs = refs[5:13]
        layer_out, residual_grad, parts = refs[13:16]
        grads = refs[16:-7]
        first, half_tall = me[3] == 0, downs[0].shape[1]
        count = w_down.shape[0] // (4 * half_tall)
        for i in range(count):
            for part in range(2):
                slot = slot_of(me, step * count + i, part == 0)
                far, slot = slot >= 8, slot % 8
                near_own, far_own, near_other, far_other = downs[4 * part : 4 * part + 4]
                mine = jnp.where(far, far_own[slot], near_own[slot])
                theirs = jnp.where(far, far_other[slot], near_other[slot])
                start = (4 * i + part) * half_tall
                w_down[start : start + half_tall, :] = jnp.where(first, mine, theirs)
                start += 2 * half_tall
                w_down[start : start + half_tall, :] = jnp.where(first, theirs, mine)
    else:
        pieces, tokens, out_grad, w_out, up, w_down, layer_out, residual_grad, parts = refs[:9]
        grads = refs[9:-7]
    residual, normed, mixed, total, layer, scratch, result = refs[-7:]

    @pl.when(step == 0)
    def _():
        from_heads(pieces, scratch, positions, sequences, heads)
        join_lanes(scratch, mixed)
        value = tokens[...].astype(F32) + dot_nn(mixed[...], w_out[...])
        residual[...] = value
        scale = lax.rsqrt(jnp.mean(value * value, axis=-1, keepdims=True) + EPS)
        normed[...] = (value * scale).astype(BF16)
        layer[...] = value
        total[...] = jnp.zeros_like(total)

    down = w_down[...]
    u = dot_nn(normed[...], up[...])
    back = dot_nt(out_grad[...], down)
    square = u * u
    tanh = jnp.tanh(u * (ROOT + ROOT * CUBE * square))
    half = 0.5 + 0.5 * tanh
    active = u * half
    hidden = active.astype(BF16)
    slope = half + active * (1.0 - tanh) * (ROOT + 3.0 * ROOT * CUBE * square)
    pre = (slope * back).astype(BF16)
    total[...] += dot_nt(pre, up[...])
    layer[...] += dot_nn(hidden, down)
    if spread:
        a_own, a_other, b_own, b_other, *c_parts = grads
        short, half_tall = a_own.shape[1], c_parts[0].shape[1]
        width = result.shape[0]
        result[...] = dot_tn(hidden, out_grad[...])
        for i in range(width // (4 * half_tall)):
            chip = step * (width // (4 * half_tall)) + i
            for part in range(2):
                slot = slot_of(me, chip, part == 0)
                for ref, core in ((c_parts[2 * part], me[3]), (c_parts[2 * part + 1], 1 - me[3])):
                    start = pl.multiple_of(((2 * i + core) * 2 + part) * half_tall, half_tall)
                    ref[slot] = result[pl.ds(start, half_tall), :].astype(BF16)
        result[...] = dot_tn(normed[...], pre)

        @pl.when(step < FIRST)
        def _():
            spread_rows(me, result, a_own, a_other, short, False)

        for kind in range(b_own.shape[2] // width - 1):

            @pl.when(step == FIRST + kind)
            def _(kind=kind):
                part = pl.ds(kind * width, width)
                spread_rows(me, result, b_own.at[:, :, part], b_other.at[:, :, part], short, True)
    else:
        d_up, d_down, d_out = grads
        d_down[...] = dot_tn(hidden, out_grad[...]).astype(BF16)
        d_up[...] = dot_tn(normed[...], pre).astype(BF16)

    @pl.when(step == last)
    def _():
        layer_out[...] = layer[...].astype(BF16)
        value = residual[...]
        scale = lax.rsqrt(jnp.mean(value * value, axis=-1, keepdims=True) + EPS)
        norm = value * scale
        grad = total[...]
        back = scale * (grad - norm * jnp.mean(grad * norm, axis=-1, keepdims=True))
        grad = out_grad[...].astype(F32) + back
        residual_grad[...] = grad
        attn_grad = grad.astype(BF16)
        split_lanes(dot_nt(attn_grad, w_out[...]), scratch)
        to_heads(scratch, parts, positions, sequences, heads)
        if spread:
            result[...] = dot_tn(mixed[...], attn_grad)
            part = pl.ds(b_own.shape[2] - width, width)
            spread_rows(me, result, b_own.at[:, :, part], b_other.at[:, :, part], short, True)
        else:
            d_out[...] = dot_tn(mixed[...], attn_grad).astype(BF16)


def middle(lay, pieces, tokens, out_grad, out_weight, up_weight, down_weight, hidden):
    rows, width = tokens.shape
    steps = hidden // width
    piece = (GROUPS, lay.group, lay.positions, lay.lanes)
    chips, short, tall = lay.devices // 2, width // lay.devices, hidden // lay.devices
    flat = (rows, width)

    def whole(*dims):
        return pl.BlockSpec(dims, lambda i, me: (0,) * len(dims))

    if lay.small:
        weights = [up_weight, up_weight, *down_weight]
        weight_specs = [
            pl.BlockSpec((width, width), lambda i, me: (0, steps)),
            pl.BlockSpec((width, width), lambda i, me: (0, i)),
        ]
        weight_specs += [whole(*array.shape) for array in down_weight]
        grads = [(chips, short, FIRST * width)] * 2 + [(chips, short, (steps + 1 - FIRST) * width)] * 2
        grads += [(chips, tall // 2, width)] * 4
        block = (chips, short, width)
        specs = [pl.BlockSpec(block, lambda i, me: (0, 0, jnp.minimum(i, FIRST - 1)))] * 2
        specs += [whole(*dims) for dims in grads[2:]]
    else:
        weights = [out_weight, up_weight, down_weight]
        weight_specs = [
            whole(width, width),
            pl.BlockSpec((width, width), lambda i, me: (0, i)),
            pl.BlockSpec((width, width), lambda i, me: (i, 0)),
        ]
        grads = [(width, hidden), (hidden, width), (width, width)]
        specs = [
            pl.BlockSpec((width, width), lambda i, me: (0, i)),
            pl.BlockSpec((width, width), lambda i, me: (i, 0)),
            whole(width, width),
        ]
    out = pl.pallas_call(
        functools.partial(
            middle_kernel,
            positions=lay.positions,
            sequences=lay.sequences,
            heads=lay.heads,
            spread=lay.small,
        ),
        grid_spec=pltpu.PrefetchScalarGridSpec(
            num_scalar_prefetch=1,
            grid=(steps,),
            in_specs=[whole(*piece), whole(*flat), whole(*flat)]
            + weight_specs,
            out_specs=[whole(*flat), whole(*flat), whole(*piece)] + specs,
            scratch_shapes=[
                pltpu.VMEM(flat, F32),
                pltpu.VMEM(flat, BF16),
                pltpu.VMEM(flat, BF16),
                pltpu.VMEM(flat, F32),
                pltpu.VMEM(flat, F32),
                pltpu.VMEM((width // 128, rows, 128), F32),
                pltpu.VMEM((width, width), F32),
            ]
            + [pltpu.VMEM((width, width), BF16)] * (1 if lay.small else 0),
        ),
        out_shape=[shape(flat), shape(flat, F32), shape(piece)] + [shape(dims) for dims in grads],
        compiler_params=params(60),
        cost_estimate=share("middle"),
        name="middle",
    )(lay.me, pieces, tokens, out_grad, *weights)
    return out[0], out[1], out[2], list(out[3:])


def slot_of(me, chip, x_first, z_plain=False):
    yr, zr, xr = (chip // 8) ^ me[0], (chip // 2) % 4, (chip % 2) ^ me[2]
    zr = zr if z_plain else zr ^ me[1]
    return ((xr * 2 + yr) if x_first else (yr * 2 + xr)) * GROUPS + zr


def spread_rows(me, result, own, other, short, x_first):
    for chip in range(result.shape[0] // (2 * short)):
        slot = slot_of(me, chip, x_first)
        for ref, core in ((own, me[3]), (other, 1 - me[3])):
            start = pl.multiple_of(2 * short * chip + short * core, short)
            ref[slot] = result[pl.ds(start, short), :].astype(BF16)


def back_kernel(me, *refs, xs, dps, positions, by_distance):
    pieces, rows, values = refs[:3]
    outs = refs[3:]
    logit_out, term_outs = outs[0], outs[1:3]
    grads, term, logit = outs[3:]
    dp, z, x, c = me[0], me[1], me[2], me[3]
    part = logit_out.shape[-1]
    for k in range(GROUPS):
        grads[:, k * positions : (k + 1) * positions, :] = pieces[k]
    for head in range(rows.shape[0]):
        term[head] = dot_tn(rows[head], grads[head]).astype(BF16)
        soft = rows[head].astype(F32)
        product = soft * dot_nt(grads[head], values[head])
        logit[...] = (product - soft * jnp.sum(product, axis=-1, keepdims=True)).astype(BF16)
        for r in range(dps):
            for k in range(GROUPS):
                start = pl.multiple_of((dp ^ r if by_distance else r) * part, part)
                logit_out[r, k, head] = logit[
                    k * positions : (k + 1) * positions, pl.ds(start, part)
                ]
    for m in range(2):
        for k in range(GROUPS):
            for j in range(xs):
                block = ((z ^ k) * xs + (x ^ j)) * 2 + (c ^ m)
                start = pl.multiple_of(block * positions, positions)
                term_outs[m][j, k] = term[:, pl.ds(start, positions), :]


def mix_back(lay, pieces, rows, values):
    group, positions, length, lanes = lay.group, lay.positions, lay.length, lay.lanes
    part = length // lay.dp
    result = pl.pallas_call(
        functools.partial(
            back_kernel, xs=lay.xs, dps=lay.dp, positions=positions, by_distance=lay.small
        ),
        in_specs=[smem()] + [vmem()] * 3,
        out_specs=[vmem()] * 3,
        out_shape=[shape((lay.dp, GROUPS, group, positions, part))]
        + [shape((lay.xs, GROUPS, group, positions, lanes))] * 2,
        scratch_shapes=[
            pltpu.VMEM((group, GROUPS * positions, lanes), BF16),
            pltpu.VMEM((group, length, lanes), BF16),
            pltpu.VMEM((GROUPS * positions, length), BF16),
        ],
        compiler_params=params(48),
        cost_estimate=share("mix_back"),
        name="mix_back",
    )(lay.me, pieces, rows, values)
    return result[0], list(result[1:])


def value_grad_kernel(me, *refs, positions, sequences, heads, spread):
    pieces, normed = refs[:GROUPS], refs[GROUPS]
    if spread:
        total, own, other, parts, scratch, result = refs[GROUPS + 1 :]
    else:
        total, parts, scratch, result = refs[GROUPS + 1 :]
    for k, piece in enumerate(pieces):
        parts[me[1] ^ k] = piece[...]
    from_heads(parts, scratch, positions, sequences, heads)
    join_lanes(scratch, total)
    if spread:
        result[...] = dot_tn(normed[...], total[...])
        spread_rows(me, result, own, other, own.shape[1], True)


def value_grads(lay, pieces, normed):
    rows, width = normed.shape
    piece = (lay.group, lay.positions, lay.lanes)
    chips, short = lay.devices // 2, width // lay.devices
    outs = [shape((rows, width))] + ([shape((chips, short, width))] * 2 if lay.small else [])
    return pl.pallas_call(
        functools.partial(
            value_grad_kernel,
            positions=lay.positions,
            sequences=lay.sequences,
            heads=lay.heads,
            spread=lay.small,
        ),
        in_specs=[smem()] + [vmem()] * (GROUPS + 1),
        out_specs=[vmem()] * len(outs),
        out_shape=outs,
        scratch_shapes=[
            pltpu.VMEM((GROUPS,) + piece, BF16),
            pltpu.VMEM((width // 128, rows, 128), F32),
            pltpu.VMEM((width, width), F32),
        ],
        compiler_params=params(32),
        cost_estimate=share("value_grads"),
        name="value_grads",
    )(lay.me, *pieces, normed)


def tokens_grad_kernel(total, weight, tokens, residual_grad, out):
    grad = dot_nt(total[...], weight[...])
    inputs = tokens[...].astype(F32)
    scale = lax.rsqrt(jnp.mean(inputs * inputs, axis=-1, keepdims=True) + EPS)
    norm = inputs * scale
    back = scale * (grad - norm * jnp.mean(grad * norm, axis=-1, keepdims=True))
    out[...] = residual_grad[...] + back


def make_tokens_grad(total, weight, tokens, residual_grad):
    rows, width = tokens.shape
    return pl.pallas_call(
        tokens_grad_kernel,
        out_shape=shape((rows, width), F32),
        in_specs=[vmem()] * 4,
        out_specs=vmem(),
        compiler_params=params(24),
        cost_estimate=share("make_tokens_grad"),
        name="make_tokens_grad",
    )(total, weight, tokens, residual_grad)


def add_kernel(*refs):
    left, right, *outs = refs
    half = outs[0].shape[0]
    for i, out in enumerate(outs):
        part = pl.ds(i * half, half)
        out[...] = (left[part].astype(F32) + right[part].astype(F32)).astype(BF16)


def add_split(left, right, parts=2):
    dims = (left.shape[0] // parts,) + left.shape[1:]
    return pl.pallas_call(
        add_kernel,
        out_shape=[shape(dims)] * parts,
        in_specs=[vmem()] * 2,
        out_specs=[vmem()] * parts,
        compiler_params=params(24),
        cost_estimate=share("add_split"),
        name="add_split",
    )(left, right)


def stack_kernel(*refs):
    *parts, out = refs
    for i, part in enumerate(parts):
        out[i] = part[...]


def stack_all(parts):
    return pl.pallas_call(
        stack_kernel,
        out_shape=shape((len(parts),) + parts[0].shape),
        in_specs=[vmem()] * len(parts),
        out_specs=vmem(),
        compiler_params=params(24),
        cost_estimate=share("stack_all"),
        name="stack_all",
    )(*parts)


def pass_kernel(source, target):
    del source, target


def pass_on(array):
    return pl.pallas_call(
        pass_kernel,
        out_shape=shape(array.shape, array.dtype),
        in_specs=[pl.BlockSpec(memory_space=pl.ANY)],
        out_specs=pl.BlockSpec(memory_space=pl.ANY),
        input_output_aliases={0: 0},
        cost_estimate=share("pass_on"),
        name="pass_on",
    )(array)


def total_kernel(*refs):
    *parts, out = refs
    total = parts[0][...].astype(F32)
    for part in parts[1:]:
        total = total + part[...].astype(F32)
    out[...] = total.astype(BF16)


def add_all(parts):
    return pl.pallas_call(
        total_kernel,
        out_shape=shape(parts[0].shape),
        in_specs=[vmem()] * len(parts),
        out_specs=vmem(),
        compiler_params=params(24),
        cost_estimate=share("add_all"),
        name="add_all",
    )(*parts)


def after(value, *done):
    return lax.optimization_barrier((value, done))[0]


def along_z(lay, pieces):
    return [pieces[0]] + [lay.swap(pieces[k], z=k) for k in range(1, GROUPS)]


def along_z_gather(lay, array):
    return jnp.stack([array] + [lay.swap(array, z=k) for k in range(1, GROUPS)])


def double(lay, array, **way):
    return jnp.concatenate([array, lay.swap(array, **way)])


def halves(own, other):
    half = own.shape[0] // 2
    return add_low(own[:half], other[:half]), add_low(own[half:], other[half:])


def sum_z(lay, array):
    total = array[0].astype(F32)
    for k in range(1, GROUPS):
        total = total + lay.swap(array[k], z=k).astype(F32)
    return total


def on_device(
    tokens,
    norm_gain1,
    value_weight,
    mixer_logits,
    out_weight,
    norm_gain2,
    up_weight,
    down_weight,
    out_grad,
):
    lay = Layout(tokens, mixer_logits)
    out_shape = tokens.shape
    width = lay.width
    tokens = tokens.reshape(lay.rows, width)
    out_grad = out_grad.reshape(lay.rows, width)
    gain_one = norm_gain1.astype(F32)[:, None]
    gain_two = norm_gain2.astype(F32)[:, None]
    value_rows = (gain_one * value_weight.astype(F32)).astype(BF16)
    up_rows = (gain_two * up_weight.astype(F32)).astype(BF16)
    small = lay.small

    tie = lax.optimization_barrier
    rows = softmax_rows(lay, mixer_logits)
    if small:
        with jax.named_scope("round_one"):
            kinds = up_rows.reshape(up_rows.shape[0], -1, width).swapaxes(0, 1)
            wide = jnp.concatenate([kinds, out_weight[None], value_rows[None]])
            wide = [wide] + [lay.swap(wide, z=k) for k in range(1, GROUPS)]
            *wide, rows = tie((*wide, rows))
        with jax.named_scope("round_two"):
            rows = lay.across_z(rows)
            own = jnp.stack([part[-1] for part in wide])
            wide = jnp.stack([part[:-1] for part in wide])
            one, two = wide[:, :SPLIT], wide[:, SPLIT:]
            four = [own, lay.swap(own, dp=1), lay.swap(own, x=1), lay.swap(own, dp=1, x=1)]
            one_other, two_other = lay.swap(one, dp=1), lay.swap(two, x=1)
            four, one_other, two_other = tie((four, one_other, two_other))
            own = jnp.concatenate(four)
            w_value = [own, lay.swap(own, c=1)]
            one, two = jnp.concatenate([one, one_other]), jnp.concatenate([two, two_other])
            one_other, two_other = lay.swap(one, x=1), lay.swap(two, dp=1)
            w_value, rows = tie((w_value, rows))
        with jax.named_scope("round_three"):
            normed_one, w_value, value_parts = make_values(lay, tokens, w_value)
            first = along_z(lay, value_parts)
            first, one_other, two_other = tie((first, one_other, two_other))
        with jax.named_scope("round_four"):
            values = stack_all(first)
            values_other = lay.swap(values, x=1)
            rows_other = lay.swap(rows, dp=1)
            tall = [down_weight] + [lay.swap(down_weight, z=k) for k in range(1, GROUPS)]
            values_other, rows_other, tall = tie((values_other, rows_other, tall))
            rows = [rows, rows_other]
        with jax.named_scope("round_five"):
            tall = stack_all(tall)
            cut = tall.shape[1] // 2
            three, four = tall[:, :cut], tall[:, cut:]
            three_other, four_other = lay.swap(three, dp=1), lay.swap(four, x=1)
            values = [values, values_other, lay.swap(values, c=1), lay.swap(values_other, c=1)]
            mix_low, values, pieces = mix_values(lay, values, rows)
            pieces = lay.across_z(pieces)
            values = pass_on(values)
            three_other, four_other, values = tie((three_other, four_other, values))
            three, four = jnp.concatenate([three, three_other]), jnp.concatenate([four, four_other])
            three_other, four_other = lay.swap(three, x=1), lay.swap(four, dp=1)
            one, two = jnp.concatenate([one, one_other]), jnp.concatenate([two, two_other])
            w_up = [one, lay.swap(one, c=1), two, lay.swap(two, c=1)]
            w_up = prepare_weights(lay, w_up)
            w_down = [three, three_other, four, four_other]
            w_down += [lay.swap(array, c=1) for array in w_down]
            w_down = [w_down[i] for i in (0, 1, 4, 5, 2, 3, 6, 7)]
            w_out = None
    else:
        w_up = lax.all_gather(up_rows, AXES, axis=0, tiled=True)
        w_out = lax.all_gather(out_weight, AXES, axis=0, tiled=True)
        w_down = lax.all_gather(down_weight, AXES, axis=0, tiled=True)
        w_value = [lax.all_gather(value_rows, AXES, axis=0, tiled=True)]
        rows = lay.across_z(rows)
        rows = [rows, lay.swap(rows, dp=1)]
        normed_one, w_value, value_parts = make_values(lay, tokens, w_value)
        values = [jnp.stack(along_z(lay, value_parts))]
        values += [lay.swap(values[0], x=j) for j in range(1, lay.xs)]
        values += [lay.swap(piece, c=1) for piece in values]
        mix_low, values, pieces = mix_values(lay, values, rows)
        pieces = lay.across_z(pieces)
    with jax.named_scope("feed_forward"):
        layer_out, residual_grad, pieces, grads = middle(
            lay, pieces, tokens, out_grad, w_out, w_up, w_down, up_rows.shape[1]
        )
        pieces = lay.across_z(pieces)
    with jax.named_scope("weight_grads"):
        if small:
            a_own, a_other, b_own, b_other, *c_parts = grads
            c_one, one_send = halves(c_parts[0], lay.swap(c_parts[1], c=1))
            c_two, two_send = halves(c_parts[2], lay.swap(c_parts[3], c=1))
            one_other, two_other = lay.swap(one_send, x=1), lay.swap(two_send, dp=1)
            a_own, a_send = halves(a_own, lay.swap(a_other, c=1))
            b_own, b_send = halves(b_own, lay.swap(b_other, c=1))
            pieces, one_other, two_other, a_send, b_send = tie(
                (pieces, one_other, two_other, a_send, b_send)
            )
            c_one, one_send = halves(c_one, one_other)
            c_two, two_send = halves(c_two, two_other)
            one_other, two_other = lay.swap(one_send, dp=1), lay.swap(two_send, x=1)
    with jax.named_scope("mixing_back"):
        logit_parts, terms = mix_back(lay, pieces, mix_low, values)
    if small:
        with jax.named_scope("mixing_back"):
            terms, one_other, two_other = tie((terms, one_other, two_other))
            term, term_send = add_split(terms[0], lay.swap(terms[1], c=1))
            term_other = lay.swap(term_send, x=1)
            logit_other = lay.swap(logit_parts[1], dp=1)
        with jax.named_scope("weight_grads"):
            c_sum = jnp.concatenate([add_low(c_one, one_other), add_low(c_two, two_other)], axis=1)
            c_rest = [lay.swap(c_sum[k], z=k) for k in range(1, GROUPS)]
        with jax.named_scope("mixing_back"):
            term_other, logit_other, c_rest = tie((term_other, logit_other, c_rest))
            (term,) = add_split(term[0], term_other[0], 1)
            pieces = along_z(lay, [term[k] for k in range(GROUPS)])
        with jax.named_scope("weight_grads"):
            a_other = lay.swap(after(a_send, term), dp=1)
            b_other = lay.swap(after(b_send, term), x=1)
            pieces, a_other, b_other = tie((pieces, a_other, b_other))
        with jax.named_scope("value_grads"):
            total, own, other = value_grads(lay, pieces, normed_one)
            other = lay.swap(other, c=1)
        with jax.named_scope("mixing_back"):
            logit_parts = add_low(logit_parts[0], after(logit_other, total))
            logit_parts = lay.across_z(logit_parts)
        with jax.named_scope("value_grads"):
            own = add_split(own, other, 4)
            parts = [lay.swap(own[1], dp=1), lay.swap(own[2], x=1), lay.swap(own[3], dp=1, x=1)]
        with jax.named_scope("weight_grads"):
            a_own, a_send = halves(a_own, after(a_other, own))
            b_own, b_send = halves(b_own, after(b_other, own))
            a_other, b_other = lay.swap(a_send, x=1), lay.swap(b_send, dp=1)
        with jax.named_scope("value_grads"):
            parts, a_other, b_other, logit_parts = tie((parts, a_other, b_other, logit_parts))
            own = add_all([own[0]] + list(parts))
        with jax.named_scope("weight_grads"):
            last = jnp.concatenate([own, add_low(a_own, a_other), add_low(b_own, b_other)], axis=2)
            last = sum_z(lay, last)
            value_sum, up_sum, out_wgrad = last[:, :width], last[:, width:-width], last[:, -width:]
            down_grad = c_sum[0].astype(F32)
            for part in c_rest:
                down_grad = down_grad + part.astype(F32)
            down_grad, total, logit_parts = after((down_grad, total, logit_parts), own)
        with jax.named_scope("mixing_back"):
            logits_grad = logit_parts.astype(F32).reshape(lay.heads, lay.positions, -1)
    else:
        with jax.named_scope("mixing_back"):
            piece, other = terms[0], lay.swap(terms[1], c=1)
            bit = lay.xs // 2
            while bit:
                piece, send = halves(piece, other)
                other = lay.swap(send, x=bit)
                bit //= 2
            piece = add_low(piece[0], other[0])
            pieces = along_z(lay, [piece[k] for k in range(GROUPS)])
            logit_parts = lax.psum_scatter(logit_parts, "dp", scatter_dimension=0)
            logits_grad = lay.across_z(logit_parts).astype(F32).reshape(lay.heads, lay.positions, -1)
        with jax.named_scope("value_grads"):
            (total,) = value_grads(lay, pieces, normed_one)
            value_sum = scatter_sum(dot_tn(normed_one, total))
        with jax.named_scope("weight_grads"):
            up_sum, down_grad, out_wgrad = (scatter_sum(grad) for grad in grads)
    with jax.named_scope("value_grads"):
        tokens_grad = make_tokens_grad(total, w_value, tokens, residual_grad)
        value_wgrad = gain_one * value_sum
        gain_one_grad = jnp.sum(value_sum * value_weight.astype(F32), axis=1)
    with jax.named_scope("weight_grads"):
        up_grad = gain_two * up_sum
        gain_two_grad = jnp.sum(up_sum * up_weight.astype(F32), axis=1)
    return (
        layer_out.reshape(out_shape),
        tokens_grad.reshape(out_shape),
        gain_one_grad,
        value_wgrad,
        logits_grad,
        out_wgrad,
        gain_two_grad,
        up_grad,
        down_grad,
    )


def scatter_sum(array):
    return lax.psum_scatter(array.astype(BF16), AXES, scatter_dimension=0, tiled=True).astype(F32)


def solution(mesh):
    placed = (
        P("seq", "dp", None),
        P(("dp", "seq")),
        P(("dp", "seq"), None),
        P(None, "seq", None),
        P(("dp", "seq"), None),
        P(("dp", "seq")),
        P(("dp", "seq"), None),
        P(("dp", "seq"), None),
        P("seq", "dp", None),
    )
    return jax.shard_map(
        on_device,
        mesh=mesh,
        in_specs=placed,
        out_specs=(
            P("seq", "dp", None),
            P("seq", "dp", None),
            P(("dp", "seq")),
            P(("dp", "seq"), None),
            P(None, "seq", "dp"),
            P(("dp", "seq"), None),
            P(("dp", "seq")),
            P(("dp", "seq"), None),
            P(("dp", "seq"), None),
        ),
        check_vma=False,
    )
```

```python
import functools

import jax
import jax.numpy as jnp
from jax import lax
from jax.experimental import pallas as pl
from jax.experimental.pallas import tpu as pltpu
from jax.sharding import PartitionSpec as P

F32 = jnp.float32
BF16 = jnp.bfloat16
AXES = ("dp", "seq")
HEAD = 64
GROUPS = 4
EPS = 1e-06
SHARES = {
    "mix_rows": 50000000000,
    "finish": 768,
    "make_values": 20000000000,
    "mix_values": 50000000000,
    "prepare_weights": 120000000000,
    "middle": 50000000000,
    "mix_back": 768,
    "value_grads": 120000000000,
    "make_tokens_grad": 8000000000,
    "add_split": 768,
    "stack_all": 50000000000,
    "pass_on": 50000000000,
    "add_all": 50000000000,
}
FIRST = 2
SPLIT = 3
MIB = 1 << 20


def smem():
    return pl.BlockSpec(memory_space=pltpu.SMEM)


def vmem():
    return pl.BlockSpec(memory_space=pltpu.VMEM)


def params(mib):
    return pltpu.CompilerParams(vmem_limit_bytes=mib * MIB)


def share(name):
    return pl.CostEstimate(flops=SHARES[name], bytes_accessed=1, transcendentals=0)


def shape(dims, kind=BF16):
    return jax.ShapeDtypeStruct(tuple(dims), kind)


def dot_nn(left, right):
    return lax.dot_general(left, right, (((1,), (0,)), ((), ())), preferred_element_type=F32)


def dot_nt(left, right):
    return lax.dot_general(left, right, (((1,), (1,)), ((), ())), preferred_element_type=F32)


def dot_tn(left, right):
    return lax.dot_general(left, right, (((0,), (0,)), ((), ())), preferred_element_type=F32)


class Layout:
    def __init__(self, tokens, logits):
        self.positions, self.sequences, self.width = tokens.shape
        self.heads, _, self.length = logits.shape
        self.dp, self.seq = lax.axis_size("dp"), lax.axis_size("seq")
        self.xs = self.seq // (2 * GROUPS)
        self.rows = self.positions * self.sequences
        self.group = self.heads // GROUPS
        self.lanes = self.sequences * HEAD
        self.devices = self.dp * self.seq
        dp, seq = lax.axis_index("dp"), lax.axis_index("seq")
        self.z, self.x, self.c = seq // (2 * self.xs), (seq // 2) % self.xs, seq % 2
        self.me = jnp.stack([dp, self.z, self.x, self.c, seq, seq, seq, seq]).astype(jnp.int32)
        self.small = self.dp == 2 and self.xs == 2

    def swap(self, array, dp=0, z=0, x=0, c=0):
        mask = ((dp * GROUPS + z) * self.xs + x) * 2 + c
        return lax.ppermute(array, AXES, [(i, i ^ mask) for i in range(self.devices)])


    def across_z(self, array):
        step = 2 * self.xs
        lines = [[z * step + i for z in range(GROUPS)] for i in range(step)]
        return lax.all_to_all(array, "seq", 0, 0, axis_index_groups=lines)


def add_low(left, right):
    return (left.astype(F32) + right.astype(F32)).astype(BF16)


def to_heads(source, target, positions, sequences, heads):
    group = heads // GROUPS
    low = lax.broadcasted_iota(jnp.int32, (positions, 2 * HEAD), 1) < HEAD
    for pair in range(sequences // 2):
        for two in range(heads // 2):
            a = source[two, pl.ds(2 * pair, positions, stride=sequences), :]
            b = source[two, pl.ds(2 * pair + 1, positions, stride=sequences), :]
            even = jnp.where(low, a, pltpu.roll(b, HEAD, 1))
            odd = jnp.where(low, pltpu.roll(a, HEAD, 1), b)
            for head, tile in ((2 * two, even), (2 * two + 1, odd)):
                target[head // group, head % group, :, 128 * pair : 128 * pair + 128] = tile.astype(BF16)


def from_heads(source, target, positions, sequences, heads):
    group = heads // GROUPS
    low = lax.broadcasted_iota(jnp.int32, (positions, 2 * HEAD), 1) < HEAD
    for pair in range(sequences // 2):
        for two in range(heads // 2):
            even, odd = (
                source[head // group, head % group, :, 128 * pair : 128 * pair + 128].astype(F32)
                for head in (2 * two, 2 * two + 1)
            )
            first = jnp.where(low, even, pltpu.roll(odd, HEAD, 1))
            second = jnp.where(low, pltpu.roll(even, HEAD, 1), odd)
            target[two, pl.ds(2 * pair, positions, stride=sequences), :] = first
            target[two, pl.ds(2 * pair + 1, positions, stride=sequences), :] = second


def split_lanes(value, target):
    for two in range(target.shape[0]):
        target[two] = value[:, 128 * two : 128 * two + 128]


def join_lanes(source, target):
    for two in range(source.shape[0]):
        target[:, 128 * two : 128 * two + 128] = source[two].astype(target.dtype)


def softmax_kernel(me, logits, out):
    positions, length = logits.shape[2], logits.shape[3]
    half = positions // 2
    start = pl.multiple_of((me[0] % 2) * half, half)
    column = lax.broadcasted_iota(jnp.int32, (half, length), 1)
    row = lax.broadcasted_iota(jnp.int32, (half, length), 0) + (me[4] * positions + start)
    allowed = column <= row
    for group in range(GROUPS):
        for head in range(logits.shape[1]):
            values = logits[group, head, pl.ds(start, half), :].astype(F32)
            masked = jnp.where(allowed, values, -jnp.inf)
            expo = jnp.exp(masked - jnp.max(masked, axis=-1, keepdims=True))
            out[group, head] = (expo * (1.0 / jnp.sum(expo, axis=-1, keepdims=True))).astype(BF16)


def softmax_rows(lay, logits):
    group, positions, length = lay.group, lay.positions, lay.length
    return pl.pallas_call(
        softmax_kernel,
        in_specs=[smem(), vmem()],
        out_specs=vmem(),
        out_shape=shape((GROUPS, group, positions // 2, length)),
        compiler_params=params(24),
        cost_estimate=share("mix_rows"),
        name="mix_rows",
    )(lay.me, logits.reshape(GROUPS, group, positions, length))


def chip_at(me, slot, x_first):
    high, mid, zr = slot // 8, (slot // GROUPS) % 2, slot % GROUPS
    xr, yr = (high, mid) if x_first else (mid, high)
    return ((me[0] ^ yr) * GROUPS + (me[1] ^ zr)) * 2 + (me[2] ^ xr)


def gather_rows(me, own, other, store, x_first):
    first = me[3] == 0
    for r in range(own.shape[0]):
        mine, theirs = own[r].astype(F32), other[r].astype(F32)
        block = jnp.concatenate([jnp.where(first, mine, theirs), jnp.where(first, theirs, mine)], 0)
        store(chip_at(me, r, x_first), block.astype(BF16))


def value_body(me, tokens, weight, scratch, parts, outs, normed, positions, sequences, heads):
    inputs = tokens[...].astype(F32)
    scale = lax.rsqrt(jnp.mean(inputs * inputs, axis=-1, keepdims=True) + EPS)
    low = (inputs * scale).astype(BF16)
    normed[...] = low
    split_lanes(dot_nn(low, weight[...]), scratch)
    to_heads(scratch, parts, positions, sequences, heads)
    for k, out in enumerate(outs):
        out[...] = parts[me[1] ^ k]


def value_kernel(me, tokens, *rest, positions, sequences, heads, blocks):
    if blocks:
        own, other, normed, whole, *outs = rest[:8]
        rows = whole.shape[0] // blocks

        def store(chip, block):
            whole[pl.ds(pl.multiple_of(chip * rows, rows), rows), :] = block

        gather_rows(me, own, other, store, True)
    else:
        whole, normed, *outs = rest[:6]
    parts, scratch = rest[-2:]
    value_body(me, tokens, whole, scratch, parts, outs, normed, positions, sequences, heads)


def make_values(lay, tokens, weight):
    rows, width = tokens.shape
    piece = (lay.group, lay.positions, lay.lanes)
    blocks = 0 if len(weight) == 1 else lay.devices // 2
    outs = [shape((rows, width))] + ([shape((width, width))] if blocks else []) + [shape(piece)] * GROUPS
    result = pl.pallas_call(
        functools.partial(
            value_kernel,
            positions=lay.positions,
            sequences=lay.sequences,
            heads=lay.heads,
            blocks=blocks,
        ),
        in_specs=[smem()] + [vmem()] * (1 + len(weight)),
        out_specs=[vmem()] * len(outs),
        out_shape=outs,
        scratch_shapes=[pltpu.VMEM((GROUPS,) + piece, BF16), pltpu.VMEM((width // 128, rows, 128), F32)],
        compiler_params=params(24),
        cost_estimate=share("make_values"),
        name="make_values",
    )(lay.me, tokens, *weight)
    normed = result[0]
    whole = result[1] if blocks else weight[0]
    return normed, whole, list(result[-GROUPS:])


def mix_kernel(me, *refs, xs, positions):
    values = refs[: 2 * xs]
    refs = refs[2 * xs :]
    near, far, rows_out, values_out, mixed = refs
    z, x, c, side = me[1], me[2], me[3], me[0] % 2
    half = positions // 2
    for k in range(GROUPS):
        base = k * positions
        rows_out[:, pl.ds(pl.multiple_of(base + side * half, half), half), :] = near[k]
        rows_out[:, pl.ds(pl.multiple_of(base + (1 - side) * half, half), half), :] = far[k]
    index = 0
    for m in range(2):
        for j in range(xs):
            for k in range(GROUPS):
                block = ((z ^ k) * xs + (x ^ j)) * 2 + (c ^ m)
                start = pl.multiple_of(block * positions, positions)
                values_out[:, pl.ds(start, positions), :] = values[index][k]
            index += 1
    for head in range(rows_out.shape[0]):
        result = dot_nn(rows_out[head], values_out[head]).astype(BF16)
        for k in range(GROUPS):
            mixed[k, head] = result[k * positions : (k + 1) * positions]


def mix_values(lay, values, rows):
    group, positions, length, lanes = lay.group, lay.positions, lay.length, lay.lanes
    inputs = list(values) + list(rows)
    result = pl.pallas_call(
        functools.partial(mix_kernel, xs=lay.xs, positions=positions),
        in_specs=[smem()] + [vmem()] * len(inputs),
        out_specs=[vmem()] * 3,
        out_shape=[
            shape((group, GROUPS * positions, length)),
            shape((group, length, lanes)),
            shape((GROUPS, group, positions, lanes)),
        ],
        compiler_params=params(40),
        cost_estimate=share("mix_values"),
        name="mix_values",
    )(lay.me, *inputs)
    return result


ROOT = 0.7978845608028654
CUBE = 0.044715


def prepare_kernel(me, *refs):
    ups, out = refs[:4], refs[4]
    step, rows = pl.program_id(0), out.shape[0] // refs[0].shape[0]

    def store(chip, block):
        out[pl.ds(pl.multiple_of(chip * rows, rows), rows), :] = block

    pl.when(step < SPLIT)(lambda: gather_rows(me, ups[0].at[:, 0], ups[1].at[:, 0], store, True))
    pl.when(step >= SPLIT)(lambda: gather_rows(me, ups[2].at[:, 0], ups[3].at[:, 0], store, False))


def prepare_weights(lay, ups):
    chips, _, short, width = ups[0].shape
    kinds = ups[0].shape[1] + ups[2].shape[1]
    block = (chips, 1, short, width)
    specs = [pl.BlockSpec(block, lambda i, me: (0, jnp.minimum(i, SPLIT - 1), 0, 0))] * 2
    specs += [pl.BlockSpec(block, lambda i, me: (0, jnp.maximum(i - SPLIT, 0), 0, 0))] * 2
    return pl.pallas_call(
        prepare_kernel,
        grid_spec=pltpu.PrefetchScalarGridSpec(
            num_scalar_prefetch=1,
            grid=(kinds,),
            in_specs=specs,
            out_specs=pl.BlockSpec((width, width), lambda i, me: (0, i)),
        ),
        out_shape=shape((width, kinds * width)),
        compiler_params=params(24),
        cost_estimate=share("prepare_weights"),
        name="prepare_weights",
    )(lay.me, *ups)


def middle_kernel(me, *refs, positions, sequences, heads, spread):
    step, last = pl.program_id(0), pl.num_programs(0) - 1
    if spread:
        *refs, w_down = refs
        pieces, tokens, out_grad, w_out, up = refs[:5]
        downs = refs[5:13]
        layer_out, residual_grad, parts = refs[13:16]
        grads = refs[16:-7]
        first, half_tall = me[3] == 0, downs[0].shape[1]
        count = w_down.shape[0] // (4 * half_tall)
        for i in range(count):
            for part in range(2):
                slot = slot_of(me, step * count + i, part == 0)
                far, slot = slot >= 8, slot % 8
                near_own, far_own, near_other, far_other = downs[4 * part : 4 * part + 4]
                mine = jnp.where(far, far_own[slot], near_own[slot])
                theirs = jnp.where(far, far_other[slot], near_other[slot])
                start = (4 * i + part) * half_tall
                w_down[start : start + half_tall, :] = jnp.where(first, mine, theirs)
                start += 2 * half_tall
                w_down[start : start + half_tall, :] = jnp.where(first, theirs, mine)
    else:
        pieces, tokens, out_grad, w_out, up, w_down, layer_out, residual_grad, parts = refs[:9]
        grads = refs[9:-7]
    residual, normed, mixed, total, layer, scratch, result = refs[-7:]

    @pl.when(step == 0)
    def _():
        from_heads(pieces, scratch, positions, sequences, heads)
        join_lanes(scratch, mixed)
        value = tokens[...].astype(F32) + dot_nn(mixed[...], w_out[...])
        residual[...] = value
        scale = lax.rsqrt(jnp.mean(value * value, axis=-1, keepdims=True) + EPS)
        normed[...] = (value * scale).astype(BF16)
        layer[...] = value
        total[...] = jnp.zeros_like(total)

    down = w_down[...]
    u = dot_nn(normed[...], up[...])
    back = dot_nt(out_grad[...], down)
    square = u * u
    tanh = jnp.tanh(u * (ROOT + ROOT * CUBE * square))
    half = 0.5 + 0.5 * tanh
    active = u * half
    hidden = active.astype(BF16)
    slope = half + active * (1.0 - tanh) * (ROOT + 3.0 * ROOT * CUBE * square)
    pre = (slope * back).astype(BF16)
    total[...] += dot_nt(pre, up[...])
    layer[...] += dot_nn(hidden, down)
    if spread:
        a_own, a_other, b_own, b_other, *c_parts = grads
        short, half_tall = a_own.shape[1], c_parts[0].shape[1]
        width = result.shape[0]
        result[...] = dot_tn(hidden, out_grad[...])
        for i in range(width // (4 * half_tall)):
            chip = step * (width // (4 * half_tall)) + i
            for part in range(2):
                slot = slot_of(me, chip, part == 0)
                for ref, core in ((c_parts[2 * part], me[3]), (c_parts[2 * part + 1], 1 - me[3])):
                    start = pl.multiple_of(((2 * i + core) * 2 + part) * half_tall, half_tall)
                    ref[slot] = result[pl.ds(start, half_tall), :].astype(BF16)
        result[...] = dot_tn(normed[...], pre)

        @pl.when(step < FIRST)
        def _():
            spread_rows(me, result, a_own, a_other, short, False)

        for kind in range(b_own.shape[2] // width - 1):

            @pl.when(step == FIRST + kind)
            def _(kind=kind):
                part = pl.ds(kind * width, width)
                spread_rows(me, result, b_own.at[:, :, part], b_other.at[:, :, part], short, True)
    else:
        d_up, d_down, d_out = grads
        d_down[...] = dot_tn(hidden, out_grad[...]).astype(BF16)
        d_up[...] = dot_tn(normed[...], pre).astype(BF16)

    @pl.when(step == last)
    def _():
        layer_out[...] = layer[...].astype(BF16)
        value = residual[...]
        scale = lax.rsqrt(jnp.mean(value * value, axis=-1, keepdims=True) + EPS)
        norm = value * scale
        grad = total[...]
        back = scale * (grad - norm * jnp.mean(grad * norm, axis=-1, keepdims=True))
        grad = out_grad[...].astype(F32) + back
        residual_grad[...] = grad
        attn_grad = grad.astype(BF16)
        split_lanes(dot_nt(attn_grad, w_out[...]), scratch)
        to_heads(scratch, parts, positions, sequences, heads)
        if spread:
            result[...] = dot_tn(mixed[...], attn_grad)
            part = pl.ds(b_own.shape[2] - width, width)
            spread_rows(me, result, b_own.at[:, :, part], b_other.at[:, :, part], short, True)
        else:
            d_out[...] = dot_tn(mixed[...], attn_grad).astype(BF16)


def middle(lay, pieces, tokens, out_grad, out_weight, up_weight, down_weight, hidden):
    rows, width = tokens.shape
    steps = hidden // width
    piece = (GROUPS, lay.group, lay.positions, lay.lanes)
    chips, short, tall = lay.devices // 2, width // lay.devices, hidden // lay.devices
    flat = (rows, width)

    def whole(*dims):
        return pl.BlockSpec(dims, lambda i, me: (0,) * len(dims))

    if lay.small:
        weights = [up_weight, up_weight, *down_weight]
        weight_specs = [
            pl.BlockSpec((width, width), lambda i, me: (0, steps)),
            pl.BlockSpec((width, width), lambda i, me: (0, i)),
        ]
        weight_specs += [whole(*array.shape) for array in down_weight]
        grads = [(chips, short, FIRST * width)] * 2 + [(chips, short, (steps + 1 - FIRST) * width)] * 2
        grads += [(chips, tall // 2, width)] * 4
        block = (chips, short, width)
        specs = [pl.BlockSpec(block, lambda i, me: (0, 0, jnp.minimum(i, FIRST - 1)))] * 2
        specs += [whole(*dims) for dims in grads[2:]]
    else:
        weights = [out_weight, up_weight, down_weight]
        weight_specs = [
            whole(width, width),
            pl.BlockSpec((width, width), lambda i, me: (0, i)),
            pl.BlockSpec((width, width), lambda i, me: (i, 0)),
        ]
        grads = [(width, hidden), (hidden, width), (width, width)]
        specs = [
            pl.BlockSpec((width, width), lambda i, me: (0, i)),
            pl.BlockSpec((width, width), lambda i, me: (i, 0)),
            whole(width, width),
        ]
    out = pl.pallas_call(
        functools.partial(
            middle_kernel,
            positions=lay.positions,
            sequences=lay.sequences,
            heads=lay.heads,
            spread=lay.small,
        ),
        grid_spec=pltpu.PrefetchScalarGridSpec(
            num_scalar_prefetch=1,
            grid=(steps,),
            in_specs=[whole(*piece), whole(*flat), whole(*flat)]
            + weight_specs,
            out_specs=[whole(*flat), whole(*flat), whole(*piece)] + specs,
            scratch_shapes=[
                pltpu.VMEM(flat, F32),
                pltpu.VMEM(flat, BF16),
                pltpu.VMEM(flat, BF16),
                pltpu.VMEM(flat, F32),
                pltpu.VMEM(flat, F32),
                pltpu.VMEM((width // 128, rows, 128), F32),
                pltpu.VMEM((width, width), F32),
            ]
            + [pltpu.VMEM((width, width), BF16)] * (1 if lay.small else 0),
        ),
        out_shape=[shape(flat), shape(flat, F32), shape(piece)] + [shape(dims) for dims in grads],
        compiler_params=params(60),
        cost_estimate=share("middle"),
        name="middle",
    )(lay.me, pieces, tokens, out_grad, *weights)
    return out[0], out[1], out[2], list(out[3:])


def slot_of(me, chip, x_first, z_plain=False):
    yr, zr, xr = (chip // 8) ^ me[0], (chip // 2) % 4, (chip % 2) ^ me[2]
    zr = zr if z_plain else zr ^ me[1]
    return ((xr * 2 + yr) if x_first else (yr * 2 + xr)) * GROUPS + zr


def spread_rows(me, result, own, other, short, x_first):
    for chip in range(result.shape[0] // (2 * short)):
        slot = slot_of(me, chip, x_first)
        for ref, core in ((own, me[3]), (other, 1 - me[3])):
            start = pl.multiple_of(2 * short * chip + short * core, short)
            ref[slot] = result[pl.ds(start, short), :].astype(BF16)


def back_kernel(me, *refs, xs, dps, positions, by_distance):
    pieces, rows, values = refs[:3]
    outs = refs[3:]
    logit_out, term_outs = outs[0], outs[1:3]
    grads, term, logit = outs[3:]
    dp, z, x, c = me[0], me[1], me[2], me[3]
    part = logit_out.shape[-1]
    for k in range(GROUPS):
        grads[:, k * positions : (k + 1) * positions, :] = pieces[k]
    for head in range(rows.shape[0]):
        term[head] = dot_tn(rows[head], grads[head]).astype(BF16)
        soft = rows[head].astype(F32)
        product = soft * dot_nt(grads[head], values[head])
        logit[...] = (product - soft * jnp.sum(product, axis=-1, keepdims=True)).astype(BF16)
        for r in range(dps):
            for k in range(GROUPS):
                start = pl.multiple_of((dp ^ r if by_distance else r) * part, part)
                logit_out[r, k, head] = logit[
                    k * positions : (k + 1) * positions, pl.ds(start, part)
                ]
    for m in range(2):
        for k in range(GROUPS):
            for j in range(xs):
                block = ((z ^ k) * xs + (x ^ j)) * 2 + (c ^ m)
                start = pl.multiple_of(block * positions, positions)
                term_outs[m][j, k] = term[:, pl.ds(start, positions), :]


def mix_back(lay, pieces, rows, values):
    group, positions, length, lanes = lay.group, lay.positions, lay.length, lay.lanes
    part = length // lay.dp
    result = pl.pallas_call(
        functools.partial(
            back_kernel, xs=lay.xs, dps=lay.dp, positions=positions, by_distance=lay.small
        ),
        in_specs=[smem()] + [vmem()] * 3,
        out_specs=[vmem()] * 3,
        out_shape=[shape((lay.dp, GROUPS, group, positions, part))]
        + [shape((lay.xs, GROUPS, group, positions, lanes))] * 2,
        scratch_shapes=[
            pltpu.VMEM((group, GROUPS * positions, lanes), BF16),
            pltpu.VMEM((group, length, lanes), BF16),
            pltpu.VMEM((GROUPS * positions, length), BF16),
        ],
        compiler_params=params(48),
        cost_estimate=share("mix_back"),
        name="mix_back",
    )(lay.me, pieces, rows, values)
    return result[0], list(result[1:])


def value_grad_kernel(me, *refs, positions, sequences, heads, spread):
    pieces, normed = refs[:GROUPS], refs[GROUPS]
    if spread:
        total, own, other, parts, scratch, result = refs[GROUPS + 1 :]
    else:
        total, parts, scratch, result = refs[GROUPS + 1 :]
    for k, piece in enumerate(pieces):
        parts[me[1] ^ k] = piece[...]
    from_heads(parts, scratch, positions, sequences, heads)
    join_lanes(scratch, total)
    if spread:
        result[...] = dot_tn(normed[...], total[...])
        spread_rows(me, result, own, other, own.shape[1], True)


def value_grads(lay, pieces, normed):
    rows, width = normed.shape
    piece = (lay.group, lay.positions, lay.lanes)
    chips, short = lay.devices // 2, width // lay.devices
    outs = [shape((rows, width))] + ([shape((chips, short, width))] * 2 if lay.small else [])
    return pl.pallas_call(
        functools.partial(
            value_grad_kernel,
            positions=lay.positions,
            sequences=lay.sequences,
            heads=lay.heads,
            spread=lay.small,
        ),
        in_specs=[smem()] + [vmem()] * (GROUPS + 1),
        out_specs=[vmem()] * len(outs),
        out_shape=outs,
        scratch_shapes=[
            pltpu.VMEM((GROUPS,) + piece, BF16),
            pltpu.VMEM((width // 128, rows, 128), F32),
            pltpu.VMEM((width, width), F32),
        ],
        compiler_params=params(32),
        cost_estimate=share("value_grads"),
        name="value_grads",
    )(lay.me, *pieces, normed)


def tokens_grad_kernel(total, weight, tokens, residual_grad, out):
    grad = dot_nt(total[...], weight[...])
    inputs = tokens[...].astype(F32)
    scale = lax.rsqrt(jnp.mean(inputs * inputs, axis=-1, keepdims=True) + EPS)
    norm = inputs * scale
    back = scale * (grad - norm * jnp.mean(grad * norm, axis=-1, keepdims=True))
    out[...] = residual_grad[...] + back


def make_tokens_grad(total, weight, tokens, residual_grad):
    rows, width = tokens.shape
    return pl.pallas_call(
        tokens_grad_kernel,
        out_shape=shape((rows, width), F32),
        in_specs=[vmem()] * 4,
        out_specs=vmem(),
        compiler_params=params(24),
        cost_estimate=share("make_tokens_grad"),
        name="make_tokens_grad",
    )(total, weight, tokens, residual_grad)


def finish_kernel(*refs):
    parts, (gain_one, gain_two, value_weight, up_weight) = refs[:GROUPS], refs[GROUPS : GROUPS + 4]
    value_out, up_out, out_out, one_out, two_out = refs[GROUPS + 4 :]
    total = parts[0][...].astype(F32)
    for part in parts[1:]:
        total = total + part[...].astype(F32)
    width = value_out.shape[1]
    value_sum, up_sum = total[:, :width], total[:, width:-width]
    value_out[...] = gain_one[...] * value_sum
    up_out[...] = gain_two[...] * up_sum
    out_out[...] = total[:, -width:]
    one_out[...] = jnp.sum(value_sum * value_weight[...].astype(F32), axis=1, keepdims=True)
    two_out[...] = jnp.sum(up_sum * up_weight[...].astype(F32), axis=1, keepdims=True)


def finish(parts, gain_one, gain_two, value_weight, up_weight):
    rows, width = value_weight.shape
    return pl.pallas_call(
        finish_kernel,
        out_shape=[
            shape((rows, width), F32),
            shape(up_weight.shape, F32),
            shape((rows, width), F32),
            shape((rows, 1), F32),
            shape((rows, 1), F32),
        ],
        in_specs=[vmem()] * (GROUPS + 4),
        out_specs=[vmem()] * 5,
        compiler_params=params(16),
        cost_estimate=share("finish"),
        name="finish",
    )(*parts, gain_one, gain_two, value_weight, up_weight)


def add_kernel(*refs):
    left, right, *outs = refs
    half = outs[0].shape[0]
    for i, out in enumerate(outs):
        part = pl.ds(i * half, half)
        out[...] = (left[part].astype(F32) + right[part].astype(F32)).astype(BF16)


def add_split(left, right, parts=2):
    dims = (left.shape[0] // parts,) + left.shape[1:]
    return pl.pallas_call(
        add_kernel,
        out_shape=[shape(dims)] * parts,
        in_specs=[vmem()] * 2,
        out_specs=[vmem()] * parts,
        compiler_params=params(24),
        cost_estimate=share("add_split"),
        name="add_split",
    )(left, right)


def stack_kernel(*refs):
    *parts, out = refs
    for i, part in enumerate(parts):
        out[i] = part[...]


def stack_all(parts):
    return pl.pallas_call(
        stack_kernel,
        out_shape=shape((len(parts),) + parts[0].shape),
        in_specs=[vmem()] * len(parts),
        out_specs=vmem(),
        compiler_params=params(24),
        cost_estimate=share("stack_all"),
        name="stack_all",
    )(*parts)


def pass_kernel(source, target):
    del source, target


def pass_on(array):
    return pl.pallas_call(
        pass_kernel,
        out_shape=shape(array.shape, array.dtype),
        in_specs=[pl.BlockSpec(memory_space=pl.ANY)],
        out_specs=pl.BlockSpec(memory_space=pl.ANY),
        input_output_aliases={0: 0},
        cost_estimate=share("pass_on"),
        name="pass_on",
    )(array)


def total_kernel(*refs):
    *parts, out = refs
    total = parts[0][...].astype(F32)
    for part in parts[1:]:
        total = total + part[...].astype(F32)
    out[...] = total.astype(BF16)


def add_all(parts):
    return pl.pallas_call(
        total_kernel,
        out_shape=shape(parts[0].shape),
        in_specs=[vmem()] * len(parts),
        out_specs=vmem(),
        compiler_params=params(24),
        cost_estimate=share("add_all"),
        name="add_all",
    )(*parts)


def after(value, *done):
    return lax.optimization_barrier((value, done))[0]


def along_z(lay, pieces):
    return [pieces[0]] + [lay.swap(pieces[k], z=k) for k in range(1, GROUPS)]


def along_z_gather(lay, array):
    return jnp.stack([array] + [lay.swap(array, z=k) for k in range(1, GROUPS)])


def double(lay, array, **way):
    return jnp.concatenate([array, lay.swap(array, **way)])


def halves(own, other):
    half = own.shape[0] // 2
    return add_low(own[:half], other[:half]), add_low(own[half:], other[half:])


def sum_z(lay, array):
    total = array[0].astype(F32)
    for k in range(1, GROUPS):
        total = total + lay.swap(array[k], z=k).astype(F32)
    return total


def on_device(
    tokens,
    norm_gain1,
    value_weight,
    mixer_logits,
    out_weight,
    norm_gain2,
    up_weight,
    down_weight,
    out_grad,
):
    lay = Layout(tokens, mixer_logits)
    out_shape = tokens.shape
    width = lay.width
    tokens = tokens.reshape(lay.rows, width)
    out_grad = out_grad.reshape(lay.rows, width)
    gain_one = norm_gain1.astype(F32)[:, None]
    gain_two = norm_gain2.astype(F32)[:, None]
    value_rows = (gain_one * value_weight.astype(F32)).astype(BF16)
    up_rows = (gain_two * up_weight.astype(F32)).astype(BF16)
    small = lay.small

    tie = lax.optimization_barrier
    rows = softmax_rows(lay, mixer_logits)
    if small:
        with jax.named_scope("round_one"):
            kinds = up_rows.reshape(up_rows.shape[0], -1, width).swapaxes(0, 1)
            wide = jnp.concatenate([kinds, out_weight[None], value_rows[None]])
            wide = [wide] + [lay.swap(wide, z=k) for k in range(1, GROUPS)]
            *wide, rows = tie((*wide, rows))
        with jax.named_scope("round_two"):
            rows = lay.across_z(rows)
            own = jnp.stack([part[-1] for part in wide])
            wide = jnp.stack([part[:-1] for part in wide])
            one, two = wide[:, :SPLIT], wide[:, SPLIT:]
            four = [own, lay.swap(own, dp=1), lay.swap(own, x=1), lay.swap(own, dp=1, x=1)]
            one_other, two_other = lay.swap(one, dp=1), lay.swap(two, x=1)
            four, one_other, two_other = tie((four, one_other, two_other))
            own = jnp.concatenate(four)
            w_value = [own, lay.swap(own, c=1)]
            one, two = jnp.concatenate([one, one_other]), jnp.concatenate([two, two_other])
            one_other, two_other = lay.swap(one, x=1), lay.swap(two, dp=1)
            w_value, rows = tie((w_value, rows))
        with jax.named_scope("round_three"):
            normed_one, w_value, value_parts = make_values(lay, tokens, w_value)
            first = along_z(lay, value_parts)
            first, one_other, two_other = tie((first, one_other, two_other))
        with jax.named_scope("round_four"):
            values = stack_all(first)
            values_other = lay.swap(values, x=1)
            rows_other = lay.swap(rows, dp=1)
            tall = [down_weight] + [lay.swap(down_weight, z=k) for k in range(1, GROUPS)]
            values_other, rows_other, tall = tie((values_other, rows_other, tall))
            rows = [rows, rows_other]
        with jax.named_scope("round_five"):
            tall = stack_all(tall)
            cut = tall.shape[1] // 2
            three, four = tall[:, :cut], tall[:, cut:]
            three_other, four_other = lay.swap(three, dp=1), lay.swap(four, x=1)
            values = [values, values_other, lay.swap(values, c=1), lay.swap(values_other, c=1)]
            mix_low, values, pieces = mix_values(lay, values, rows)
            pieces = lay.across_z(pieces)
            values = pass_on(values)
            three_other, four_other, values = tie((three_other, four_other, values))
            three, four = jnp.concatenate([three, three_other]), jnp.concatenate([four, four_other])
            three_other, four_other = lay.swap(three, x=1), lay.swap(four, dp=1)
            one, two = jnp.concatenate([one, one_other]), jnp.concatenate([two, two_other])
            w_up = [one, lay.swap(one, c=1), two, lay.swap(two, c=1)]
            w_up = prepare_weights(lay, w_up)
            w_down = [three, three_other, four, four_other]
            w_down += [lay.swap(array, c=1) for array in w_down]
            w_down = [w_down[i] for i in (0, 1, 4, 5, 2, 3, 6, 7)]
            w_out = None
    else:
        w_up = lax.all_gather(up_rows, AXES, axis=0, tiled=True)
        w_out = lax.all_gather(out_weight, AXES, axis=0, tiled=True)
        w_down = lax.all_gather(down_weight, AXES, axis=0, tiled=True)
        w_value = [lax.all_gather(value_rows, AXES, axis=0, tiled=True)]
        rows = lay.across_z(rows)
        rows = [rows, lay.swap(rows, dp=1)]
        normed_one, w_value, value_parts = make_values(lay, tokens, w_value)
        values = [jnp.stack(along_z(lay, value_parts))]
        values += [lay.swap(values[0], x=j) for j in range(1, lay.xs)]
        values += [lay.swap(piece, c=1) for piece in values]
        mix_low, values, pieces = mix_values(lay, values, rows)
        pieces = lay.across_z(pieces)
    with jax.named_scope("feed_forward"):
        layer_out, residual_grad, pieces, grads = middle(
            lay, pieces, tokens, out_grad, w_out, w_up, w_down, up_rows.shape[1]
        )
        pieces = lay.across_z(pieces)
    with jax.named_scope("weight_grads"):
        if small:
            a_own, a_other, b_own, b_other, *c_parts = grads
            c_one, one_send = halves(c_parts[0], lay.swap(c_parts[1], c=1))
            c_two, two_send = halves(c_parts[2], lay.swap(c_parts[3], c=1))
            one_other, two_other = lay.swap(one_send, x=1), lay.swap(two_send, dp=1)
            a_own, a_send = halves(a_own, lay.swap(a_other, c=1))
            b_own, b_send = halves(b_own, lay.swap(b_other, c=1))
            pieces, one_other, two_other, a_send, b_send = tie(
                (pieces, one_other, two_other, a_send, b_send)
            )
            c_one, one_send = halves(c_one, one_other)
            c_two, two_send = halves(c_two, two_other)
            one_other, two_other = lay.swap(one_send, dp=1), lay.swap(two_send, x=1)
    with jax.named_scope("mixing_back"):
        logit_parts, terms = mix_back(lay, pieces, mix_low, values)
    if small:
        with jax.named_scope("mixing_back"):
            terms, one_other, two_other = tie((terms, one_other, two_other))
            term, term_send = add_split(terms[0], lay.swap(terms[1], c=1))
            term_other = lay.swap(term_send, x=1)
            logit_other = lay.swap(logit_parts[1], dp=1)
        with jax.named_scope("weight_grads"):
            c_sum = jnp.concatenate([add_low(c_one, one_other), add_low(c_two, two_other)], axis=1)
            c_rest = [lay.swap(c_sum[k], z=k) for k in range(1, GROUPS)]
        with jax.named_scope("mixing_back"):
            term_other, logit_other, c_rest = tie((term_other, logit_other, c_rest))
            (term,) = add_split(term[0], term_other[0], 1)
            pieces = along_z(lay, [term[k] for k in range(GROUPS)])
        with jax.named_scope("weight_grads"):
            a_other = lay.swap(after(a_send, term), dp=1)
            b_other = lay.swap(after(b_send, term), x=1)
            pieces, a_other, b_other = tie((pieces, a_other, b_other))
        with jax.named_scope("value_grads"):
            total, own, other = value_grads(lay, pieces, normed_one)
            other = lay.swap(other, c=1)
        with jax.named_scope("mixing_back"):
            logit_parts = add_low(logit_parts[0], after(logit_other, total))
            logit_parts = lay.across_z(logit_parts)
        with jax.named_scope("value_grads"):
            own = add_split(own, other, 4)
            parts = [lay.swap(own[1], dp=1), lay.swap(own[2], x=1), lay.swap(own[3], dp=1, x=1)]
        with jax.named_scope("weight_grads"):
            a_own, a_send = halves(a_own, after(a_other, own))
            b_own, b_send = halves(b_own, after(b_other, own))
            a_other, b_other = lay.swap(a_send, x=1), lay.swap(b_send, dp=1)
        with jax.named_scope("value_grads"):
            parts, a_other, b_other, logit_parts = tie((parts, a_other, b_other, logit_parts))
            own = add_all([own[0]] + list(parts))
        with jax.named_scope("weight_grads"):
            last = jnp.concatenate([own, add_low(a_own, a_other), add_low(b_own, b_other)], axis=2)
            last = [last[0]] + [lay.swap(last[k], z=k) for k in range(1, GROUPS)]
            value_wgrad, up_grad, out_wgrad, gain_one_grad, gain_two_grad = finish(
                last, gain_one, gain_two, value_weight, up_weight
            )
            gain_one_grad, gain_two_grad = gain_one_grad[:, 0], gain_two_grad[:, 0]
            down_grad = c_sum[0].astype(F32)
            for part in c_rest:
                down_grad = down_grad + part.astype(F32)
            down_grad, total, logit_parts = after((down_grad, total, logit_parts), own)
        with jax.named_scope("mixing_back"):
            logits_grad = logit_parts.astype(F32).reshape(lay.heads, lay.positions, -1)
    else:
        with jax.named_scope("mixing_back"):
            piece, other = terms[0], lay.swap(terms[1], c=1)
            bit = lay.xs // 2
            while bit:
                piece, send = halves(piece, other)
                other = lay.swap(send, x=bit)
                bit //= 2
            piece = add_low(piece[0], other[0])
            pieces = along_z(lay, [piece[k] for k in range(GROUPS)])
            logit_parts = lax.psum_scatter(logit_parts, "dp", scatter_dimension=0)
            logits_grad = lay.across_z(logit_parts).astype(F32).reshape(lay.heads, lay.positions, -1)
        with jax.named_scope("value_grads"):
            (total,) = value_grads(lay, pieces, normed_one)
            value_sum = scatter_sum(dot_tn(normed_one, total))
        with jax.named_scope("weight_grads"):
            up_sum, down_grad, out_wgrad = (scatter_sum(grad) for grad in grads)
    with jax.named_scope("value_grads"):
        tokens_grad = make_tokens_grad(total, w_value, tokens, residual_grad)
    if not small:
        value_wgrad = gain_one * value_sum
        gain_one_grad = jnp.sum(value_sum * value_weight.astype(F32), axis=1)
        up_grad = gain_two * up_sum
        gain_two_grad = jnp.sum(up_sum * up_weight.astype(F32), axis=1)
    return (
        layer_out.reshape(out_shape),
        tokens_grad.reshape(out_shape),
        gain_one_grad,
        value_wgrad,
        logits_grad,
        out_wgrad,
        gain_two_grad,
        up_grad,
        down_grad,
    )


def scatter_sum(array):
    return lax.psum_scatter(array.astype(BF16), AXES, scatter_dimension=0, tiled=True).astype(F32)


def solution(mesh):
    placed = (
        P("seq", "dp", None),
        P(("dp", "seq")),
        P(("dp", "seq"), None),
        P(None, "seq", None),
        P(("dp", "seq"), None),
        P(("dp", "seq")),
        P(("dp", "seq"), None),
        P(("dp", "seq"), None),
        P("seq", "dp", None),
    )
    return jax.shard_map(
        on_device,
        mesh=mesh,
        in_specs=placed,
        out_specs=(
            P("seq", "dp", None),
            P("seq", "dp", None),
            P(("dp", "seq")),
            P(("dp", "seq"), None),
            P(None, "seq", "dp"),
            P(("dp", "seq"), None),
            P(("dp", "seq")),
            P(("dp", "seq"), None),
            P(("dp", "seq"), None),
        ),
        check_vma=False,
    )
```

```python
import functools

import jax
import jax.numpy as jnp
from jax import lax
from jax.experimental import pallas as pl
from jax.experimental.pallas import tpu as pltpu
from jax.sharding import PartitionSpec as P

F32 = jnp.float32
BF16 = jnp.bfloat16
AXES = ("dp", "seq")
HEAD = 64
GROUPS = 4
EPS = 1e-06
SHARES = {
    "mix_rows": 50000000000,
    "finish": 768,
    "make_values": 20000000000,
    "mix_values": 50000000000,
    "prepare_weights": 120000000000,
    "middle": 50000000000,
    "mix_back": 768,
    "value_grads": 120000000000,
    "make_tokens_grad": 8000000000,
    "add_split": 768,
    "stack_all": 50000000000,
    "pass_on": 50000000000,
    "add_all": 50000000000,
}
FIRST = 2
SPLIT = 2
MIB = 1 << 20


def smem():
    return pl.BlockSpec(memory_space=pltpu.SMEM)


def vmem():
    return pl.BlockSpec(memory_space=pltpu.VMEM)


def params(mib):
    return pltpu.CompilerParams(vmem_limit_bytes=mib * MIB)


def share(name):
    return pl.CostEstimate(flops=SHARES[name], bytes_accessed=1, transcendentals=0)


def shape(dims, kind=BF16):
    return jax.ShapeDtypeStruct(tuple(dims), kind)


def dot_nn(left, right):
    return lax.dot_general(left, right, (((1,), (0,)), ((), ())), preferred_element_type=F32)


def dot_nt(left, right):
    return lax.dot_general(left, right, (((1,), (1,)), ((), ())), preferred_element_type=F32)


def dot_tn(left, right):
    return lax.dot_general(left, right, (((0,), (0,)), ((), ())), preferred_element_type=F32)


class Layout:
    def __init__(self, tokens, logits):
        self.positions, self.sequences, self.width = tokens.shape
        self.heads, _, self.length = logits.shape
        self.dp, self.seq = lax.axis_size("dp"), lax.axis_size("seq")
        self.xs = self.seq // (2 * GROUPS)
        self.rows = self.positions * self.sequences
        self.group = self.heads // GROUPS
        self.lanes = self.sequences * HEAD
        self.devices = self.dp * self.seq
        dp, seq = lax.axis_index("dp"), lax.axis_index("seq")
        self.z, self.x, self.c = seq // (2 * self.xs), (seq // 2) % self.xs, seq % 2
        self.me = jnp.stack([dp, self.z, self.x, self.c, seq, seq, seq, seq]).astype(jnp.int32)
        self.small = self.dp == 2 and self.xs == 2

    def swap(self, array, dp=0, z=0, x=0, c=0):
        mask = ((dp * GROUPS + z) * self.xs + x) * 2 + c
        return lax.ppermute(array, AXES, [(i, i ^ mask) for i in range(self.devices)])


    def across_z(self, array):
        step = 2 * self.xs
        lines = [[z * step + i for z in range(GROUPS)] for i in range(step)]
        return lax.all_to_all(array, "seq", 0, 0, axis_index_groups=lines)


def add_low(left, right):
    return (left.astype(F32) + right.astype(F32)).astype(BF16)


def to_heads(source, target, positions, sequences, heads):
    group = heads // GROUPS
    low = lax.broadcasted_iota(jnp.int32, (positions, 2 * HEAD), 1) < HEAD
    for pair in range(sequences // 2):
        for two in range(heads // 2):
            a = source[two, pl.ds(2 * pair, positions, stride=sequences), :]
            b = source[two, pl.ds(2 * pair + 1, positions, stride=sequences), :]
            even = jnp.where(low, a, pltpu.roll(b, HEAD, 1))
            odd = jnp.where(low, pltpu.roll(a, HEAD, 1), b)
            for head, tile in ((2 * two, even), (2 * two + 1, odd)):
                target[head // group, head % group, :, 128 * pair : 128 * pair + 128] = tile.astype(BF16)


def from_heads(source, target, positions, sequences, heads):
    group = heads // GROUPS
    low = lax.broadcasted_iota(jnp.int32, (positions, 2 * HEAD), 1) < HEAD
    for pair in range(sequences // 2):
        for two in range(heads // 2):
            even, odd = (
                source[head // group, head % group, :, 128 * pair : 128 * pair + 128].astype(F32)
                for head in (2 * two, 2 * two + 1)
            )
            first = jnp.where(low, even, pltpu.roll(odd, HEAD, 1))
            second = jnp.where(low, pltpu.roll(even, HEAD, 1), odd)
            target[two, pl.ds(2 * pair, positions, stride=sequences), :] = first
            target[two, pl.ds(2 * pair + 1, positions, stride=sequences), :] = second


def split_lanes(value, target):
    for two in range(target.shape[0]):
        target[two] = value[:, 128 * two : 128 * two + 128]


def join_lanes(source, target):
    for two in range(source.shape[0]):
        target[:, 128 * two : 128 * two + 128] = source[two].astype(target.dtype)


def softmax_kernel(me, logits, out):
    positions, length = logits.shape[2], logits.shape[3]
    half = positions // 2
    start = pl.multiple_of((me[0] % 2) * half, half)
    column = lax.broadcasted_iota(jnp.int32, (half, length), 1)
    row = lax.broadcasted_iota(jnp.int32, (half, length), 0) + (me[4] * positions + start)
    allowed = column <= row
    for group in range(GROUPS):
        for head in range(logits.shape[1]):
            values = logits[group, head, pl.ds(start, half), :].astype(F32)
            masked = jnp.where(allowed, values, -jnp.inf)
            expo = jnp.exp(masked - jnp.max(masked, axis=-1, keepdims=True))
            out[group, head] = (expo * (1.0 / jnp.sum(expo, axis=-1, keepdims=True))).astype(BF16)


def softmax_rows(lay, logits):
    group, positions, length = lay.group, lay.positions, lay.length
    return pl.pallas_call(
        softmax_kernel,
        in_specs=[smem(), vmem()],
        out_specs=vmem(),
        out_shape=shape((GROUPS, group, positions // 2, length)),
        compiler_params=params(24),
        cost_estimate=share("mix_rows"),
        name="mix_rows",
    )(lay.me, logits.reshape(GROUPS, group, positions, length))


def chip_at(me, slot, x_first):
    high, mid, zr = slot // 8, (slot // GROUPS) % 2, slot % GROUPS
    xr, yr = (high, mid) if x_first else (mid, high)
    return ((me[0] ^ yr) * GROUPS + (me[1] ^ zr)) * 2 + (me[2] ^ xr)


def gather_rows(me, own, other, store, x_first):
    first = me[3] == 0
    for r in range(own.shape[0]):
        mine, theirs = own[r].astype(F32), other[r].astype(F32)
        block = jnp.concatenate([jnp.where(first, mine, theirs), jnp.where(first, theirs, mine)], 0)
        store(chip_at(me, r, x_first), block.astype(BF16))


def value_body(me, tokens, weight, scratch, parts, outs, normed, positions, sequences, heads):
    inputs = tokens[...].astype(F32)
    scale = lax.rsqrt(jnp.mean(inputs * inputs, axis=-1, keepdims=True) + EPS)
    low = (inputs * scale).astype(BF16)
    normed[...] = low
    split_lanes(dot_nn(low, weight[...]), scratch)
    to_heads(scratch, parts, positions, sequences, heads)
    for k, out in enumerate(outs):
        out[...] = parts[me[1] ^ k]


def value_kernel(me, tokens, *rest, positions, sequences, heads, blocks):
    if blocks:
        own, other, normed, whole, *outs = rest[:8]
        rows = whole.shape[0] // blocks

        def store(chip, block):
            whole[pl.ds(pl.multiple_of(chip * rows, rows), rows), :] = block

        gather_rows(me, own, other, store, True)
    else:
        whole, normed, *outs = rest[:6]
    parts, scratch = rest[-2:]
    value_body(me, tokens, whole, scratch, parts, outs, normed, positions, sequences, heads)


def make_values(lay, tokens, weight):
    rows, width = tokens.shape
    piece = (lay.group, lay.positions, lay.lanes)
    blocks = 0 if len(weight) == 1 else lay.devices // 2
    outs = [shape((rows, width))] + ([shape((width, width))] if blocks else []) + [shape(piece)] * GROUPS
    result = pl.pallas_call(
        functools.partial(
            value_kernel,
            positions=lay.positions,
            sequences=lay.sequences,
            heads=lay.heads,
            blocks=blocks,
        ),
        in_specs=[smem()] + [vmem()] * (1 + len(weight)),
        out_specs=[vmem()] * len(outs),
        out_shape=outs,
        scratch_shapes=[pltpu.VMEM((GROUPS,) + piece, BF16), pltpu.VMEM((width // 128, rows, 128), F32)],
        compiler_params=params(24),
        cost_estimate=share("make_values"),
        name="make_values",
    )(lay.me, tokens, *weight)
    normed = result[0]
    whole = result[1] if blocks else weight[0]
    return normed, whole, list(result[-GROUPS:])


def mix_kernel(me, *refs, xs, positions):
    values = refs[: 2 * xs]
    refs = refs[2 * xs :]
    near, far, rows_out, values_out, mixed = refs
    z, x, c, side = me[1], me[2], me[3], me[0] % 2
    half = positions // 2
    for k in range(GROUPS):
        base = k * positions
        rows_out[:, pl.ds(pl.multiple_of(base + side * half, half), half), :] = near[k]
        rows_out[:, pl.ds(pl.multiple_of(base + (1 - side) * half, half), half), :] = far[k]
    index = 0
    for m in range(2):
        for j in range(xs):
            for k in range(GROUPS):
                block = ((z ^ k) * xs + (x ^ j)) * 2 + (c ^ m)
                start = pl.multiple_of(block * positions, positions)
                values_out[:, pl.ds(start, positions), :] = values[index][k]
            index += 1
    for head in range(rows_out.shape[0]):
        result = dot_nn(rows_out[head], values_out[head]).astype(BF16)
        for k in range(GROUPS):
            mixed[k, head] = result[k * positions : (k + 1) * positions]


def mix_values(lay, values, rows):
    group, positions, length, lanes = lay.group, lay.positions, lay.length, lay.lanes
    inputs = list(values) + list(rows)
    result = pl.pallas_call(
        functools.partial(mix_kernel, xs=lay.xs, positions=positions),
        in_specs=[smem()] + [vmem()] * len(inputs),
        out_specs=[vmem()] * 3,
        out_shape=[
            shape((group, GROUPS * positions, length)),
            shape((group, length, lanes)),
            shape((GROUPS, group, positions, lanes)),
        ],
        compiler_params=params(40),
        cost_estimate=share("mix_values"),
        name="mix_values",
    )(lay.me, *inputs)
    return result


ROOT = 0.7978845608028654
CUBE = 0.044715


def prepare_kernel(me, *refs):
    ups, out = refs[:4], refs[4]
    step, rows = pl.program_id(0), out.shape[0] // refs[0].shape[0]

    def store(chip, block):
        out[pl.ds(pl.multiple_of(chip * rows, rows), rows), :] = block

    pl.when(step < SPLIT)(lambda: gather_rows(me, ups[0].at[:, 0], ups[1].at[:, 0], store, True))
    pl.when(step >= SPLIT)(lambda: gather_rows(me, ups[2].at[:, 0], ups[3].at[:, 0], store, False))


def prepare_weights(lay, ups):
    chips, _, short, width = ups[0].shape
    kinds = ups[0].shape[1] + ups[2].shape[1]
    block = (chips, 1, short, width)
    specs = [pl.BlockSpec(block, lambda i, me: (0, jnp.minimum(i, SPLIT - 1), 0, 0))] * 2
    specs += [pl.BlockSpec(block, lambda i, me: (0, jnp.maximum(i - SPLIT, 0), 0, 0))] * 2
    return pl.pallas_call(
        prepare_kernel,
        grid_spec=pltpu.PrefetchScalarGridSpec(
            num_scalar_prefetch=1,
            grid=(kinds,),
            in_specs=specs,
            out_specs=pl.BlockSpec((width, width), lambda i, me: (0, i)),
        ),
        out_shape=shape((width, kinds * width)),
        compiler_params=params(24),
        cost_estimate=share("prepare_weights"),
        name="prepare_weights",
    )(lay.me, *ups)


def middle_kernel(me, *refs, positions, sequences, heads, spread):
    step, last = pl.program_id(0), pl.num_programs(0) - 1
    if spread:
        *refs, w_down = refs
        pieces, tokens, out_grad, w_out, up = refs[:5]
        downs = refs[5:13]
        layer_out, residual_grad, parts = refs[13:16]
        grads = refs[16:-7]
        first, half_tall = me[3] == 0, downs[0].shape[1]
        count = w_down.shape[0] // (4 * half_tall)
        for i in range(count):
            for part in range(2):
                slot = slot_of(me, step * count + i, part == 0)
                far, slot = slot >= 8, slot % 8
                near_own, far_own, near_other, far_other = downs[4 * part : 4 * part + 4]
                mine = jnp.where(far, far_own[slot], near_own[slot])
                theirs = jnp.where(far, far_other[slot], near_other[slot])
                start = (4 * i + part) * half_tall
                w_down[start : start + half_tall, :] = jnp.where(first, mine, theirs)
                start += 2 * half_tall
                w_down[start : start + half_tall, :] = jnp.where(first, theirs, mine)
    else:
        pieces, tokens, out_grad, w_out, up, w_down, layer_out, residual_grad, parts = refs[:9]
        grads = refs[9:-7]
    residual, normed, mixed, total, layer, scratch, result = refs[-7:]

    @pl.when(step == 0)
    def _():
        from_heads(pieces, scratch, positions, sequences, heads)
        join_lanes(scratch, mixed)
        value = tokens[...].astype(F32) + dot_nn(mixed[...], w_out[...])
        residual[...] = value
        scale = lax.rsqrt(jnp.mean(value * value, axis=-1, keepdims=True) + EPS)
        normed[...] = (value * scale).astype(BF16)
        layer[...] = value
        total[...] = jnp.zeros_like(total)

    down = w_down[...]
    u = dot_nn(normed[...], up[...])
    back = dot_nt(out_grad[...], down)
    square = u * u
    tanh = jnp.tanh(u * (ROOT + ROOT * CUBE * square))
    half = 0.5 + 0.5 * tanh
    active = u * half
    hidden = active.astype(BF16)
    slope = half + active * (1.0 - tanh) * (ROOT + 3.0 * ROOT * CUBE * square)
    pre = (slope * back).astype(BF16)
    total[...] += dot_nt(pre, up[...])
    layer[...] += dot_nn(hidden, down)
    if spread:
        a_own, a_other, b_own, b_other, *c_parts = grads
        short, half_tall = a_own.shape[1], c_parts[0].shape[1]
        width = result.shape[0]
        result[...] = dot_tn(hidden, out_grad[...])
        for i in range(width // (4 * half_tall)):
            chip = step * (width // (4 * half_tall)) + i
            for part in range(2):
                slot = slot_of(me, chip, part == 0)
                for ref, core in ((c_parts[2 * part], me[3]), (c_parts[2 * part + 1], 1 - me[3])):
                    start = pl.multiple_of(((2 * i + core) * 2 + part) * half_tall, half_tall)
                    ref[slot] = result[pl.ds(start, half_tall), :].astype(BF16)
        result[...] = dot_tn(normed[...], pre)

        @pl.when(step < FIRST)
        def _():
            spread_rows(me, result, a_own, a_other, short, False)

        for kind in range(b_own.shape[2] // width - 1):

            @pl.when(step == FIRST + kind)
            def _(kind=kind):
                part = pl.ds(kind * width, width)
                spread_rows(me, result, b_own.at[:, :, part], b_other.at[:, :, part], short, True)
    else:
        d_up, d_down, d_out = grads
        d_down[...] = dot_tn(hidden, out_grad[...]).astype(BF16)
        d_up[...] = dot_tn(normed[...], pre).astype(BF16)

    @pl.when(step == last)
    def _():
        layer_out[...] = layer[...].astype(BF16)
        value = residual[...]
        scale = lax.rsqrt(jnp.mean(value * value, axis=-1, keepdims=True) + EPS)
        norm = value * scale
        grad = total[...]
        back = scale * (grad - norm * jnp.mean(grad * norm, axis=-1, keepdims=True))
        grad = out_grad[...].astype(F32) + back
        residual_grad[...] = grad
        attn_grad = grad.astype(BF16)
        split_lanes(dot_nt(attn_grad, w_out[...]), scratch)
        to_heads(scratch, parts, positions, sequences, heads)
        if spread:
            result[...] = dot_tn(mixed[...], attn_grad)
            part = pl.ds(b_own.shape[2] - width, width)
            spread_rows(me, result, b_own.at[:, :, part], b_other.at[:, :, part], short, True)
        else:
            d_out[...] = dot_tn(mixed[...], attn_grad).astype(BF16)


def middle(lay, pieces, tokens, out_grad, out_weight, up_weight, down_weight, hidden):
    rows, width = tokens.shape
    steps = hidden // width
    piece = (GROUPS, lay.group, lay.positions, lay.lanes)
    chips, short, tall = lay.devices // 2, width // lay.devices, hidden // lay.devices
    flat = (rows, width)

    def whole(*dims):
        return pl.BlockSpec(dims, lambda i, me: (0,) * len(dims))

    if lay.small:
        weights = [up_weight, up_weight, *down_weight]
        weight_specs = [
            pl.BlockSpec((width, width), lambda i, me: (0, steps)),
            pl.BlockSpec((width, width), lambda i, me: (0, i)),
        ]
        weight_specs += [whole(*array.shape) for array in down_weight]
        grads = [(chips, short, FIRST * width)] * 2 + [(chips, short, (steps + 1 - FIRST) * width)] * 2
        grads += [(chips, tall // 2, width)] * 4
        block = (chips, short, width)
        specs = [pl.BlockSpec(block, lambda i, me: (0, 0, jnp.minimum(i, FIRST - 1)))] * 2
        specs += [whole(*dims) for dims in grads[2:]]
    else:
        weights = [out_weight, up_weight, down_weight]
        weight_specs = [
            whole(width, width),
            pl.BlockSpec((width, width), lambda i, me: (0, i)),
            pl.BlockSpec((width, width), lambda i, me: (i, 0)),
        ]
        grads = [(width, hidden), (hidden, width), (width, width)]
        specs = [
            pl.BlockSpec((width, width), lambda i, me: (0, i)),
            pl.BlockSpec((width, width), lambda i, me: (i, 0)),
            whole(width, width),
        ]
    out = pl.pallas_call(
        functools.partial(
            middle_kernel,
            positions=lay.positions,
            sequences=lay.sequences,
            heads=lay.heads,
            spread=lay.small,
        ),
        grid_spec=pltpu.PrefetchScalarGridSpec(
            num_scalar_prefetch=1,
            grid=(steps,),
            in_specs=[whole(*piece), whole(*flat), whole(*flat)]
            + weight_specs,
            out_specs=[whole(*flat), whole(*flat), whole(*piece)] + specs,
            scratch_shapes=[
                pltpu.VMEM(flat, F32),
                pltpu.VMEM(flat, BF16),
                pltpu.VMEM(flat, BF16),
                pltpu.VMEM(flat, F32),
                pltpu.VMEM(flat, F32),
                pltpu.VMEM((width // 128, rows, 128), F32),
                pltpu.VMEM((width, width), F32),
            ]
            + [pltpu.VMEM((width, width), BF16)] * (1 if lay.small else 0),
        ),
        out_shape=[shape(flat), shape(flat, F32), shape(piece)] + [shape(dims) for dims in grads],
        compiler_params=params(60),
        cost_estimate=share("middle"),
        name="middle",
    )(lay.me, pieces, tokens, out_grad, *weights)
    return out[0], out[1], out[2], list(out[3:])


def slot_of(me, chip, x_first, z_plain=False):
    yr, zr, xr = (chip // 8) ^ me[0], (chip // 2) % 4, (chip % 2) ^ me[2]
    zr = zr if z_plain else zr ^ me[1]
    return ((xr * 2 + yr) if x_first else (yr * 2 + xr)) * GROUPS + zr


def spread_rows(me, result, own, other, short, x_first):
    for chip in range(result.shape[0] // (2 * short)):
        slot = slot_of(me, chip, x_first)
        for ref, core in ((own, me[3]), (other, 1 - me[3])):
            start = pl.multiple_of(2 * short * chip + short * core, short)
            ref[slot] = result[pl.ds(start, short), :].astype(BF16)


def back_kernel(me, *refs, xs, dps, positions, by_distance):
    pieces, rows, values = refs[:3]
    outs = refs[3:]
    logit_out, term_outs = outs[0], outs[1:3]
    grads, term, logit = outs[3:]
    dp, z, x, c = me[0], me[1], me[2], me[3]
    part = logit_out.shape[-1]
    for k in range(GROUPS):
        grads[:, k * positions : (k + 1) * positions, :] = pieces[k]
    for head in range(rows.shape[0]):
        term[head] = dot_tn(rows[head], grads[head]).astype(BF16)
        soft = rows[head].astype(F32)
        product = soft * dot_nt(grads[head], values[head])
        logit[...] = (product - soft * jnp.sum(product, axis=-1, keepdims=True)).astype(BF16)
        for r in range(dps):
            for k in range(GROUPS):
                start = pl.multiple_of((dp ^ r if by_distance else r) * part, part)
                logit_out[r, k, head] = logit[
                    k * positions : (k + 1) * positions, pl.ds(start, part)
                ]
    for m in range(2):
        for k in range(GROUPS):
            for j in range(xs):
                block = ((z ^ k) * xs + (x ^ j)) * 2 + (c ^ m)
                start = pl.multiple_of(block * positions, positions)
                term_outs[m][j, k] = term[:, pl.ds(start, positions), :]


def mix_back(lay, pieces, rows, values):
    group, positions, length, lanes = lay.group, lay.positions, lay.length, lay.lanes
    part = length // lay.dp
    result = pl.pallas_call(
        functools.partial(
            back_kernel, xs=lay.xs, dps=lay.dp, positions=positions, by_distance=lay.small
        ),
        in_specs=[smem()] + [vmem()] * 3,
        out_specs=[vmem()] * 3,
        out_shape=[shape((lay.dp, GROUPS, group, positions, part))]
        + [shape((lay.xs, GROUPS, group, positions, lanes))] * 2,
        scratch_shapes=[
            pltpu.VMEM((group, GROUPS * positions, lanes), BF16),
            pltpu.VMEM((group, length, lanes), BF16),
            pltpu.VMEM((GROUPS * positions, length), BF16),
        ],
        compiler_params=params(48),
        cost_estimate=share("mix_back"),
        name="mix_back",
    )(lay.me, pieces, rows, values)
    return result[0], list(result[1:])


def value_grad_kernel(me, *refs, positions, sequences, heads, spread):
    pieces, normed = refs[:GROUPS], refs[GROUPS]
    if spread:
        total, own, other, parts, scratch, result = refs[GROUPS + 1 :]
    else:
        total, parts, scratch, result = refs[GROUPS + 1 :]
    for k, piece in enumerate(pieces):
        parts[me[1] ^ k] = piece[...]
    from_heads(parts, scratch, positions, sequences, heads)
    join_lanes(scratch, total)
    if spread:
        result[...] = dot_tn(normed[...], total[...])
        spread_rows(me, result, own, other, own.shape[1], True)


def value_grads(lay, pieces, normed):
    rows, width = normed.shape
    piece = (lay.group, lay.positions, lay.lanes)
    chips, short = lay.devices // 2, width // lay.devices
    outs = [shape((rows, width))] + ([shape((chips, short, width))] * 2 if lay.small else [])
    return pl.pallas_call(
        functools.partial(
            value_grad_kernel,
            positions=lay.positions,
            sequences=lay.sequences,
            heads=lay.heads,
            spread=lay.small,
        ),
        in_specs=[smem()] + [vmem()] * (GROUPS + 1),
        out_specs=[vmem()] * len(outs),
        out_shape=outs,
        scratch_shapes=[
            pltpu.VMEM((GROUPS,) + piece, BF16),
            pltpu.VMEM((width // 128, rows, 128), F32),
            pltpu.VMEM((width, width), F32),
        ],
        compiler_params=params(32),
        cost_estimate=share("value_grads"),
        name="value_grads",
    )(lay.me, *pieces, normed)


def tokens_grad_kernel(total, weight, tokens, residual_grad, out):
    grad = dot_nt(total[...], weight[...])
    inputs = tokens[...].astype(F32)
    scale = lax.rsqrt(jnp.mean(inputs * inputs, axis=-1, keepdims=True) + EPS)
    norm = inputs * scale
    back = scale * (grad - norm * jnp.mean(grad * norm, axis=-1, keepdims=True))
    out[...] = residual_grad[...] + back


def make_tokens_grad(total, weight, tokens, residual_grad):
    rows, width = tokens.shape
    return pl.pallas_call(
        tokens_grad_kernel,
        out_shape=shape((rows, width), F32),
        in_specs=[vmem()] * 4,
        out_specs=vmem(),
        compiler_params=params(24),
        cost_estimate=share("make_tokens_grad"),
        name="make_tokens_grad",
    )(total, weight, tokens, residual_grad)


def finish_kernel(*refs):
    parts, (gain_one, gain_two, value_weight, up_weight) = refs[:GROUPS], refs[GROUPS : GROUPS + 4]
    value_out, up_out, out_out, one_out, two_out = refs[GROUPS + 4 :]
    total = parts[0][...].astype(F32)
    for part in parts[1:]:
        total = total + part[...].astype(F32)
    width = value_out.shape[1]
    value_sum, up_sum = total[:, :width], total[:, width:-width]
    value_out[...] = gain_one[...] * value_sum
    up_out[...] = gain_two[...] * up_sum
    out_out[...] = total[:, -width:]
    one_out[...] = jnp.sum(value_sum * value_weight[...].astype(F32), axis=1, keepdims=True)
    two_out[...] = jnp.sum(up_sum * up_weight[...].astype(F32), axis=1, keepdims=True)


def finish(parts, gain_one, gain_two, value_weight, up_weight):
    rows, width = value_weight.shape
    return pl.pallas_call(
        finish_kernel,
        out_shape=[
            shape((rows, width), F32),
            shape(up_weight.shape, F32),
            shape((rows, width), F32),
            shape((rows, 1), F32),
            shape((rows, 1), F32),
        ],
        in_specs=[vmem()] * (GROUPS + 4),
        out_specs=[vmem()] * 5,
        compiler_params=params(16),
        cost_estimate=share("finish"),
        name="finish",
    )(*parts, gain_one, gain_two, value_weight, up_weight)


def add_kernel(*refs):
    left, right, *outs = refs
    half = outs[0].shape[0]
    for i, out in enumerate(outs):
        part = pl.ds(i * half, half)
        out[...] = (left[part].astype(F32) + right[part].astype(F32)).astype(BF16)


def add_split(left, right, parts=2):
    dims = (left.shape[0] // parts,) + left.shape[1:]
    return pl.pallas_call(
        add_kernel,
        out_shape=[shape(dims)] * parts,
        in_specs=[vmem()] * 2,
        out_specs=[vmem()] * parts,
        compiler_params=params(24),
        cost_estimate=share("add_split"),
        name="add_split",
    )(left, right)


def stack_kernel(*refs):
    *parts, out = refs
    for i, part in enumerate(parts):
        out[i] = part[...]


def stack_all(parts):
    return pl.pallas_call(
        stack_kernel,
        out_shape=shape((len(parts),) + parts[0].shape),
        in_specs=[vmem()] * len(parts),
        out_specs=vmem(),
        compiler_params=params(24),
        cost_estimate=share("stack_all"),
        name="stack_all",
    )(*parts)


def pass_kernel(source, target):
    del source, target


def pass_on(array):
    return pl.pallas_call(
        pass_kernel,
        out_shape=shape(array.shape, array.dtype),
        in_specs=[pl.BlockSpec(memory_space=pl.ANY)],
        out_specs=pl.BlockSpec(memory_space=pl.ANY),
        input_output_aliases={0: 0},
        cost_estimate=share("pass_on"),
        name="pass_on",
    )(array)


def total_kernel(*refs):
    *parts, out = refs
    total = parts[0][...].astype(F32)
    for part in parts[1:]:
        total = total + part[...].astype(F32)
    out[...] = total.astype(BF16)


def add_all(parts):
    return pl.pallas_call(
        total_kernel,
        out_shape=shape(parts[0].shape),
        in_specs=[vmem()] * len(parts),
        out_specs=vmem(),
        compiler_params=params(24),
        cost_estimate=share("add_all"),
        name="add_all",
    )(*parts)


def after(value, *done):
    return lax.optimization_barrier((value, done))[0]


def along_z(lay, pieces):
    return [pieces[0]] + [lay.swap(pieces[k], z=k) for k in range(1, GROUPS)]


def along_z_gather(lay, array):
    return jnp.stack([array] + [lay.swap(array, z=k) for k in range(1, GROUPS)])


def double(lay, array, **way):
    return jnp.concatenate([array, lay.swap(array, **way)])


def halves(own, other):
    half = own.shape[0] // 2
    return add_low(own[:half], other[:half]), add_low(own[half:], other[half:])


def sum_z(lay, array):
    total = array[0].astype(F32)
    for k in range(1, GROUPS):
        total = total + lay.swap(array[k], z=k).astype(F32)
    return total


def on_device(
    tokens,
    norm_gain1,
    value_weight,
    mixer_logits,
    out_weight,
    norm_gain2,
    up_weight,
    down_weight,
    out_grad,
):
    lay = Layout(tokens, mixer_logits)
    out_shape = tokens.shape
    width = lay.width
    tokens = tokens.reshape(lay.rows, width)
    out_grad = out_grad.reshape(lay.rows, width)
    gain_one = norm_gain1.astype(F32)[:, None]
    gain_two = norm_gain2.astype(F32)[:, None]
    value_rows = (gain_one * value_weight.astype(F32)).astype(BF16)
    up_rows = (gain_two * up_weight.astype(F32)).astype(BF16)
    small = lay.small

    tie = lax.optimization_barrier
    rows = softmax_rows(lay, mixer_logits)
    if small:
        with jax.named_scope("round_one"):
            kinds = up_rows.reshape(up_rows.shape[0], -1, width).swapaxes(0, 1)
            wide = jnp.concatenate([kinds, out_weight[None], value_rows[None]])
            wide = [wide] + [lay.swap(wide, z=k) for k in range(1, GROUPS)]
            *wide, rows = tie((*wide, rows))
        with jax.named_scope("round_two"):
            rows = lay.across_z(rows)
            own = jnp.stack([part[-1] for part in wide])
            wide = jnp.stack([part[:-1] for part in wide])
            one, two = wide[:, :SPLIT], wide[:, SPLIT:]
            four = [own, lay.swap(own, dp=1), lay.swap(own, x=1), lay.swap(own, dp=1, x=1)]
            one_other, two_other = lay.swap(one, dp=1), lay.swap(two, x=1)
            four, one_other, two_other = tie((four, one_other, two_other))
            own = jnp.concatenate(four)
            w_value = [own, lay.swap(own, c=1)]
            one, two = jnp.concatenate([one, one_other]), jnp.concatenate([two, two_other])
            one_other, two_other = lay.swap(one, x=1), lay.swap(two, dp=1)
            w_value, rows = tie((w_value, rows))
        with jax.named_scope("round_three"):
            normed_one, w_value, value_parts = make_values(lay, tokens, w_value)
            first = along_z(lay, value_parts)
            first, one_other, two_other = tie((first, one_other, two_other))
        with jax.named_scope("round_four"):
            values = stack_all(first)
            values_other = lay.swap(values, x=1)
            rows_other = lay.swap(rows, dp=1)
            tall = [down_weight] + [lay.swap(down_weight, z=k) for k in range(1, GROUPS)]
            values_other, rows_other, tall = tie((values_other, rows_other, tall))
            rows = [rows, rows_other]
        with jax.named_scope("round_five"):
            tall = stack_all(tall)
            cut = tall.shape[1] // 2
            three, four = tall[:, :cut], tall[:, cut:]
            three_other, four_other = lay.swap(three, dp=1), lay.swap(four, x=1)
            values = [values, values_other, lay.swap(values, c=1), lay.swap(values_other, c=1)]
            mix_low, values, pieces = mix_values(lay, values, rows)
            pieces = lay.across_z(pieces)
            values = pass_on(values)
            three_other, four_other, values = tie((three_other, four_other, values))
            three, four = jnp.concatenate([three, three_other]), jnp.concatenate([four, four_other])
            three_other, four_other = lay.swap(three, x=1), lay.swap(four, dp=1)
            one, two = jnp.concatenate([one, one_other]), jnp.concatenate([two, two_other])
            w_up = [one, lay.swap(one, c=1), two, lay.swap(two, c=1)]
            w_up = prepare_weights(lay, w_up)
            w_down = [three, three_other, four, four_other]
            w_down += [lay.swap(array, c=1) for array in w_down]
            w_down = [w_down[i] for i in (0, 1, 4, 5, 2, 3, 6, 7)]
            w_out = None
    else:
        w_up = lax.all_gather(up_rows, AXES, axis=0, tiled=True)
        w_out = lax.all_gather(out_weight, AXES, axis=0, tiled=True)
        w_down = lax.all_gather(down_weight, AXES, axis=0, tiled=True)
        w_value = [lax.all_gather(value_rows, AXES, axis=0, tiled=True)]
        rows = lay.across_z(rows)
        rows = [rows, lay.swap(rows, dp=1)]
        normed_one, w_value, value_parts = make_values(lay, tokens, w_value)
        values = [jnp.stack(along_z(lay, value_parts))]
        values += [lay.swap(values[0], x=j) for j in range(1, lay.xs)]
        values += [lay.swap(piece, c=1) for piece in values]
        mix_low, values, pieces = mix_values(lay, values, rows)
        pieces = lay.across_z(pieces)
    with jax.named_scope("feed_forward"):
        layer_out, residual_grad, pieces, grads = middle(
            lay, pieces, tokens, out_grad, w_out, w_up, w_down, up_rows.shape[1]
        )
        pieces = lay.across_z(pieces)
    with jax.named_scope("weight_grads"):
        if small:
            a_own, a_other, b_own, b_other, *c_parts = grads
            c_one, one_send = halves(c_parts[0], lay.swap(c_parts[1], c=1))
            c_two, two_send = halves(c_parts[2], lay.swap(c_parts[3], c=1))
            one_other, two_other = lay.swap(one_send, x=1), lay.swap(two_send, dp=1)
            a_own, a_send = halves(a_own, lay.swap(a_other, c=1))
            b_own, b_send = halves(b_own, lay.swap(b_other, c=1))
            pieces, one_other, two_other, a_send, b_send = tie(
                (pieces, one_other, two_other, a_send, b_send)
            )
            c_one, one_send = halves(c_one, one_other)
            c_two, two_send = halves(c_two, two_other)
            one_other, two_other = lay.swap(one_send, dp=1), lay.swap(two_send, x=1)
    with jax.named_scope("mixing_back"):
        logit_parts, terms = mix_back(lay, pieces, mix_low, values)
    if small:
        with jax.named_scope("mixing_back"):
            terms, one_other, two_other = tie((terms, one_other, two_other))
            term, term_send = add_split(terms[0], lay.swap(terms[1], c=1))
            term_other = lay.swap(term_send, x=1)
            logit_other = lay.swap(logit_parts[1], dp=1)
        with jax.named_scope("weight_grads"):
            c_sum = jnp.concatenate([add_low(c_one, one_other), add_low(c_two, two_other)], axis=1)
            c_rest = [lay.swap(c_sum[k], z=k) for k in range(1, GROUPS)]
        with jax.named_scope("mixing_back"):
            term_other, logit_other, c_rest = tie((term_other, logit_other, c_rest))
            (term,) = add_split(term[0], term_other[0], 1)
            pieces = along_z(lay, [term[k] for k in range(GROUPS)])
        with jax.named_scope("weight_grads"):
            a_other = lay.swap(after(a_send, term), dp=1)
            b_other = lay.swap(after(b_send, term), x=1)
            pieces, a_other, b_other = tie((pieces, a_other, b_other))
        with jax.named_scope("value_grads"):
            total, own, other = value_grads(lay, pieces, normed_one)
            other = lay.swap(other, c=1)
        with jax.named_scope("mixing_back"):
            logit_parts = add_low(logit_parts[0], after(logit_other, total))
            logit_parts = lay.across_z(logit_parts)
        with jax.named_scope("value_grads"):
            own = add_split(own, other, 4)
            parts = [lay.swap(own[1], dp=1), lay.swap(own[2], x=1), lay.swap(own[3], dp=1, x=1)]
        with jax.named_scope("weight_grads"):
            a_own, a_send = halves(a_own, after(a_other, own))
            b_own, b_send = halves(b_own, after(b_other, own))
            a_other, b_other = lay.swap(a_send, x=1), lay.swap(b_send, dp=1)
        with jax.named_scope("value_grads"):
            parts, a_other, b_other, logit_parts = tie((parts, a_other, b_other, logit_parts))
            own = add_all([own[0]] + list(parts))
        with jax.named_scope("weight_grads"):
            last = jnp.concatenate([own, add_low(a_own, a_other), add_low(b_own, b_other)], axis=2)
            last = [last[0]] + [lay.swap(last[k], z=k) for k in range(1, GROUPS)]
            value_wgrad, up_grad, out_wgrad, gain_one_grad, gain_two_grad = finish(
                last, gain_one, gain_two, value_weight, up_weight
            )
            gain_one_grad, gain_two_grad = gain_one_grad[:, 0], gain_two_grad[:, 0]
            down_grad = c_sum[0].astype(F32)
            for part in c_rest:
                down_grad = down_grad + part.astype(F32)
            down_grad, total, logit_parts = after((down_grad, total, logit_parts), own)
        with jax.named_scope("mixing_back"):
            logits_grad = logit_parts.astype(F32).reshape(lay.heads, lay.positions, -1)
    else:
        with jax.named_scope("mixing_back"):
            piece, other = terms[0], lay.swap(terms[1], c=1)
            bit = lay.xs // 2
            while bit:
                piece, send = halves(piece, other)
                other = lay.swap(send, x=bit)
                bit //= 2
            piece = add_low(piece[0], other[0])
            pieces = along_z(lay, [piece[k] for k in range(GROUPS)])
            logit_parts = lax.psum_scatter(logit_parts, "dp", scatter_dimension=0)
            logits_grad = lay.across_z(logit_parts).astype(F32).reshape(lay.heads, lay.positions, -1)
        with jax.named_scope("value_grads"):
            (total,) = value_grads(lay, pieces, normed_one)
            value_sum = scatter_sum(dot_tn(normed_one, total))
        with jax.named_scope("weight_grads"):
            up_sum, down_grad, out_wgrad = (scatter_sum(grad) for grad in grads)
    with jax.named_scope("value_grads"):
        tokens_grad = make_tokens_grad(total, w_value, tokens, residual_grad)
    if not small:
        value_wgrad = gain_one * value_sum
        gain_one_grad = jnp.sum(value_sum * value_weight.astype(F32), axis=1)
        up_grad = gain_two * up_sum
        gain_two_grad = jnp.sum(up_sum * up_weight.astype(F32), axis=1)
    return (
        layer_out.reshape(out_shape),
        tokens_grad.reshape(out_shape),
        gain_one_grad,
        value_wgrad,
        logits_grad,
        out_wgrad,
        gain_two_grad,
        up_grad,
        down_grad,
    )


def scatter_sum(array):
    return lax.psum_scatter(array.astype(BF16), AXES, scatter_dimension=0, tiled=True).astype(F32)


def solution(mesh):
    placed = (
        P("seq", "dp", None),
        P(("dp", "seq")),
        P(("dp", "seq"), None),
        P(None, "seq", None),
        P(("dp", "seq"), None),
        P(("dp", "seq")),
        P(("dp", "seq"), None),
        P(("dp", "seq"), None),
        P("seq", "dp", None),
    )
    return jax.shard_map(
        on_device,
        mesh=mesh,
        in_specs=placed,
        out_specs=(
            P("seq", "dp", None),
            P("seq", "dp", None),
            P(("dp", "seq")),
            P(("dp", "seq"), None),
            P(None, "seq", "dp"),
            P(("dp", "seq"), None),
            P(("dp", "seq")),
            P(("dp", "seq"), None),
            P(("dp", "seq"), None),
        ),
        check_vma=False,
    )
```
